32 devices in a mesh: groups: 2 (over y), leaf: 16 (over z, x, core).
Axes of the slice: x: 2, y: 2, z: 4, core: 2. Of those that a mesh axis runs over, the one named last changes fastest.
Arguments:
- right_side: float32 [64, 262144], P(None, ('groups', 'leaf')), parts along dimension 1
- scaling: float32 [262144], P(('groups', 'leaf')), parts along dimension 0, may hold values from 0.5 to 2
- embeddings: float32 [32, 262144], P(None, ('groups', 'leaf')), parts along dimension 1
- near_leaves: int32 [512, 3], P(('groups', 'leaf')), parts along dimension 0, may hold values from 0 to 255, as said below
- far_leaves: int32 [512, 8], P(('groups', 'leaf')), parts along dimension 0, may hold values from 0 to 255, as said below
- leaf_basis: bfloat16 [512, 64, 512], P(('groups', 'leaf')), parts along dimension 0, may hold values from -0.25 to 0.25
- leaf_coupling: bfloat16 [512, 8, 4096], P(('groups', 'leaf')), parts along dimension 0, may hold values from -0.25 to 0.25
- transfer: bfloat16 [512, 4096], P(('groups', 'leaf')), parts along dimension 0, may hold values from -0.25 to 0.25
- coarse_coupling: bfloat16 [4, 2, 4096], P('groups'), parts along dimension 0, may hold values from -0.5 to 0.5
Outputs:
- solution: float32 [64, 262144], P(None, ('groups', 'leaf')), parts along dimension 1
- residual: float32 [64, 262144], P(None, ('groups', 'leaf')), parts along dimension 1
The draws below stay inside these ranges and needn't reach their ends.
There are 2 independent parts, one for each index of `groups`. The reference program is written for one: setup_inputs(seed, part) draws one part's arguments, and reference() takes and returns one part's arrays. A program takes and returns all parts, laid end to end along the dimension named above; each array names one. Nothing has to cross between parts.
Inputs may be any that keep to these rules, and one draw needn't show every extreme that they name: `near_leaves`: the first entry of a row is the leaf itself; the entries of a row are distinct and lie among the leaves of the owner's device and the 8 leaves on either side of them. `far_leaves`: the entries of a row are distinct leaves that lie on devices 2 to 4 places below or above the owner's device.
All inputs are finite; a program needn't handle non-finite values.
Results may differ from the reference program's by a relative error of at most 0.006.
Values may be sent and summed in bfloat16 or wider, within the bound.
No kernel may reach another device: no remote copies, remote signals or barrier semaphores. Data moves between devices by JAX's collectives and lax.ppermute only.
A program may use at most 128 MiB of HBM per device.

```python
import math
import jax
import jax.numpy as jnp
from jax import lax

DIM = 32
NRHS = 64
RANK = 64
LEAF = 512
LPD = 16
NNEAR = 3
NFAR = 8
FARDEV = 4
CDEV = 8
ITERS = 2
LEAVES = 256
POINTS = 131072
COARSE = 2


def draw_embeddings(key, part):
    key = jax.random.fold_in(key, 11)
    center_key, spread_key = jax.random.split(key)
    centers = 0.5 * jax.random.normal(center_key, (DIM, LEAVES), jnp.float32)
    spread = 0.7 * jax.random.normal(spread_key, (DIM, LEAVES, LEAF), jnp.float32)
    return (centers[:, :, None] + spread).reshape(DIM, LEAVES * LEAF)


def draw_right_side(key, part):
    key = jax.random.fold_in(key, 12)
    value_key, column_key = jax.random.split(key, 2)
    ramp_place = jnp.arange(POINTS, dtype=jnp.float32) / (POINTS - 1)
    row_scale = jnp.exp(jnp.log(3.0) * ramp_place)
    values = jax.random.normal(value_key, (NRHS, POINTS), jnp.float32)
    column_scale = jnp.exp(jax.random.uniform(column_key, (NRHS, 1), jnp.float32, 0.0, 2.3)) / 3.0
    return values * row_scale[None, :] * column_scale


def ordered_picks(key, usable, width, picks):
    row_keys = jax.random.split(key, LEAVES)
    shuffled = jax.vmap(lambda row_key: jax.random.permutation(row_key, width))(row_keys)
    places = jnp.arange(width, dtype=jnp.int32)[None, :]
    priority = jnp.where(usable, shuffled.astype(jnp.int32), width + places)
    return (priority, picks)


def draw_near_leaves(key, part):
    key = jax.random.fold_in(key, 13)
    margin = LPD // 2
    width = LPD + 2 * margin
    leaf_ids = jnp.arange(LEAVES, dtype=jnp.int32)
    owner = leaf_ids // LPD
    start = owner * LPD - margin
    candidates = start[:, None] + jnp.arange(width, dtype=jnp.int32)[None, :]
    usable = (candidates >= 0) & (candidates < LEAVES)
    priority, picks = ordered_picks(key, usable, width, NNEAR)
    priority = jnp.where(candidates == leaf_ids[:, None], -1, priority)
    order = jnp.argsort(priority, axis=1)
    return jnp.take_along_axis(candidates, order[:, :picks], axis=1).astype(jnp.int32)


def draw_far_leaves(key, part):
    key = jax.random.fold_in(key, 14)
    width = (2 * FARDEV + 1) * LPD
    leaf_ids = jnp.arange(LEAVES, dtype=jnp.int32)
    owner = leaf_ids // LPD
    start = (owner - FARDEV) * LPD
    candidates = start[:, None] + jnp.arange(width, dtype=jnp.int32)[None, :]
    spacing = jnp.abs(jnp.floor_divide(candidates, LPD) - owner[:, None])
    usable = (candidates >= 0) & (candidates < LEAVES) & (spacing >= 2)
    priority, picks = ordered_picks(key, usable, width, NFAR)
    order = jnp.argsort(priority, axis=1)
    return jnp.take_along_axis(candidates, order[:, :picks], axis=1).astype(jnp.int32)


def shard_levels(rng, extent, pieces, smallest, top_value):
    factor_of, own = 1.0, jax.random.fold_in(rng, 6)
    for axis_at, blocks in pieces:
        heights = jnp.exp(jax.random.uniform(jax.random.fold_in(own, axis_at), (blocks,), jnp.float32, smallest / len(pieces), top_value / len(pieces)))
        factor_of = factor_of * jnp.repeat(heights, extent[axis_at] // blocks).reshape([-1 if axis == axis_at else 1 for axis in range(len(extent))])
    return factor_of


def scatter_about(own_key, extent, scale, bound, cuts=(), held_as=jnp.bfloat16):
    drawn = jax.random.normal(own_key, extent, jnp.float32) * scale
    if len(cuts) > 0:
        drawn = shard_levels(own_key, extent, cuts, -0.22, 0.18) * drawn
    return jnp.clip(drawn, min=-bound, max=bound).astype(held_as)


def setup_inputs(seed: int = 0, part: int = 0) -> dict:
    seeds = jax.random.split(jax.random.key(seed), 10)
    own_keys = jax.random.split(jax.random.fold_in(seeds[9], part), 10)
    return {
        "right_side": draw_right_side(jax.random.fold_in(jax.random.fold_in(seeds[9], part), 71), part),
        "scaling": jnp.clip(jnp.exp(math.log(2.0) - 1.3862944 * jax.random.uniform(own_keys[1], (POINTS,), jnp.float32) ** shard_levels(own_keys[1], (POINTS,), ((0, 16),), -0.2, 0.2)), 0.5, 2.0),
        "embeddings": draw_embeddings(jax.random.fold_in(jax.random.fold_in(seeds[9], part), 71), part),
        "near_leaves": draw_near_leaves(jax.random.fold_in(jax.random.fold_in(seeds[9], part), 71), part),
        "far_leaves": draw_far_leaves(jax.random.fold_in(jax.random.fold_in(seeds[9], part), 71), part),
        "leaf_basis": scatter_about(own_keys[5], (LEAVES, RANK, LEAF), LEAF ** -0.5, 0.25, ((0, 16),)),
        "leaf_coupling": scatter_about(own_keys[6], (LEAVES, NFAR, RANK * RANK), (RANK * NFAR) ** -0.5, 0.25, ((0, 16),)),
        "transfer": scatter_about(own_keys[7], (LEAVES, RANK * RANK), (RANK * CDEV) ** -0.5, 0.25, ((0, 16),)),
        "coarse_coupling": scatter_about(own_keys[8], (COARSE, COARSE, RANK * RANK), (RANK * COARSE) ** -0.5, 0.5),
    }


KERNEL_SCALE = 0.0625
RIDGE_TERM = 1.0
EPSILON = 1e-6
HIGHEST = lax.Precision.HIGHEST


def kernel_block(own_points, other_points):
    own_square = jnp.sum(own_points * own_points, axis=0)
    other_square = jnp.sum(other_points * other_points, axis=0)
    crossed = jnp.dot(own_points.T, other_points, precision=HIGHEST, preferred_element_type=jnp.float32)
    distance = (own_square[:, None] + other_square[None, :]) - 2.0 * crossed
    return jnp.exp(-distance * KERNEL_SCALE).astype(jnp.bfloat16)


def apply_kernel(values, embeddings, near_leaves, far_leaves, leaf_basis, leaf_coupling, transfer, coarse_coupling):
    rounded = values.astype(jnp.bfloat16)

    def one_leaf(leaf_number):
        own_points = lax.dynamic_slice_in_dim(embeddings, leaf_number * LEAF, LEAF, 1)
        accumulated = jnp.zeros((NRHS, LEAF), jnp.float32)
        for near_slot in range(NNEAR):
            neighbour = near_leaves[leaf_number, near_slot].astype(jnp.int32)
            kernel_tile = kernel_block(own_points, lax.dynamic_slice_in_dim(embeddings, neighbour * LEAF, LEAF, 1))
            neighbour_values = lax.dynamic_slice_in_dim(rounded, neighbour * LEAF, LEAF, 1)
            accumulated = accumulated + jnp.dot(neighbour_values, kernel_tile.T, preferred_element_type=jnp.float32)
        return accumulated

    near_rows = lax.map(one_leaf, jnp.arange(LEAVES, dtype=jnp.int32))
    near_part = near_rows.transpose(1, 0, 2).reshape(NRHS, LEAVES * LEAF)

    basis_wide = leaf_basis.astype(jnp.float32)
    leaf_values = rounded.astype(jnp.float32).reshape(NRHS, LEAVES, LEAF)
    coefficients = jnp.einsum("iap,nip->ian", basis_wide, leaf_values).astype(jnp.bfloat16)
    picked = coefficients[far_leaves].astype(jnp.float32)
    couplings = leaf_coupling.astype(jnp.float32).reshape(LEAVES, NFAR, RANK, RANK)
    coupled = jnp.einsum("isab,isbn->ian", couplings, picked)
    basis_transfer = transfer.astype(jnp.float32).reshape(LEAVES, RANK, RANK)
    leaf_shares = jnp.einsum("iab,ian->ibn", basis_transfer, coefficients.astype(jnp.float32))
    cluster_sums = jnp.sum(leaf_shares.reshape(COARSE, LEAVES // COARSE, RANK, NRHS), axis=1)
    others = (jnp.arange(COARSE)[:, None] != jnp.arange(COARSE)[None, :]).astype(jnp.float32)
    coarse_rows = coarse_coupling.astype(jnp.float32).reshape(COARSE, COARSE, RANK, RANK) * others[:, :, None, None]
    from_coarse = jnp.einsum("abxy,byn->axn", coarse_rows, cluster_sums, precision=HIGHEST)
    leaf_coarse = jnp.repeat(from_coarse, LEAVES // COARSE, axis=0)
    combined = coupled + jnp.einsum("iab,ibn->ian", basis_transfer, leaf_coarse, precision=HIGHEST)
    combined_rounded = combined.astype(jnp.bfloat16).astype(jnp.float32)
    far_part = jnp.einsum("iap,ian->nip", basis_wide, combined_rounded).reshape(NRHS, LEAVES * LEAF)
    return RIDGE_TERM * values + near_part + far_part


def reference(right_side, scaling, embeddings, near_leaves, far_leaves, leaf_basis, leaf_coupling, transfer, coarse_coupling):
    solution = jnp.zeros_like(right_side)
    residual = right_side
    direction = right_side
    direction_image = right_side
    curvature = jnp.zeros((NRHS,), jnp.float32)
    for iteration in range(ITERS):
        scaled = scaling[None, :] * residual
        product_now = apply_kernel(scaled, embeddings, near_leaves, far_leaves, leaf_basis, leaf_coupling, transfer, coarse_coupling)
        if iteration == 0:
            direction = scaled
            direction_image = product_now
        else:
            beta_factor = -jnp.sum(product_now * direction_image, axis=1) / (curvature + EPSILON)
            direction = scaled + beta_factor[:, None] * direction
            direction_image = product_now + beta_factor[:, None] * direction_image
        curvature = jnp.sum(direction_image * direction_image, axis=1)
        step_size = jnp.sum(residual * direction_image, axis=1) / (curvature + EPSILON)
        solution = solution + step_size[:, None] * direction
        residual = residual - step_size[:, None] * direction_image
    return solution, residual
```

```python
import math

import jax
import jax.numpy as jnp
from jax import lax
from jax.experimental import pallas as pl
from jax.experimental.pallas import tpu as pltpu
from jax.sharding import PartitionSpec as P

FARDEV = 4
NEARDEV = 2
CDEV = 8
KERNEL_SCALE = 0.0625
RIDGE_TERM = 1.0
EPSILON = 1e-06
F32 = jnp.float32
BF16 = jnp.bfloat16
HALF_SCALE = math.sqrt(2.0 * KERNEL_SCALE * math.log2(math.e))
BLOCK = 2
VMEM_LIMIT = 56 * 1024 * 1024
FAR_SHIFTS = (-4, -3, -2, 2, 3, 4)


def shifted(value, steps):
    count = lax.axis_size("leaf")
    pairs = [(i, i + steps) for i in range(count) if 0 <= i + steps < count]
    return lax.ppermute(value, "leaf", pairs)


def swapped(value, mask):
    count = lax.axis_size("leaf")
    return lax.ppermute(value, "leaf", [(i, i ^ mask) for i in range(count)])


def dot(a, b, ca, cb):
    return lax.dot_general(a, b, (((ca,), (cb,)), ((), ())), preferred_element_type=F32)


def split3(value):
    high = value.astype(BF16)
    rest = value - high.astype(F32)
    mid = rest.astype(BF16)
    low = (rest - mid.astype(F32)).astype(BF16)
    return high, mid, low


def point_pieces(points):
    scaled = points * HALF_SCALE
    high, mid, low = split3(scaled)
    square = 0.5 * jnp.sum(scaled * scaled, axis=0, keepdims=True)
    s_high, s_mid, s_low = split3(square)
    return high, mid, low, s_high.astype(F32), s_mid.astype(F32), s_low.astype(F32)


def norm_rows(first, second, third, width, swap, sign):
    row = lax.broadcasted_iota(jnp.int32, (16, width), 0)
    base = 3 if swap else 0
    ones = 0 if swap else 3
    out = jnp.where((row >= ones) & (row < ones + 3), sign, 0.0)
    for at, piece in enumerate((first, second, third)):
        out = jnp.where(row == base + at, sign * piece, out)
    return out.astype(BF16)


def own_rows(points):
    high, mid, low, a, b, c = point_pieces(points)
    norms = norm_rows(a, b, c, points.shape[1], False, 1.0)
    return jnp.concatenate([high, mid, high, mid, low, high, norms], axis=0)


def other_rows(points):
    high, mid, low, a, b, c = point_pieces(points)
    norms = norm_rows(a, b, c, points.shape[1], True, -1.0)
    return jnp.concatenate([high, high, mid, mid, high, low, norms], axis=0)


def tile_of(other, own):
    return jnp.exp2(dot(other, own, 0, 0)).astype(BF16)


def pack_pair(block):
    half = block.shape[0] // 2
    return jnp.concatenate([block[:half], block[half:]], axis=1)


def leaf_coefficients(basis, rounded, trans):
    coef = dot(basis, rounded, 1, 1).astype(BF16)
    return pack_pair(coef), dot(trans, coef, 0, 0)


def prep_kernel(rs_ref, sc_ref, basis_ref, trans_ref, lo_ref, hi_ref, coef_ref, part_ref):
    step = pl.program_id(0)
    block, rank, leaf = basis_ref.shape
    half = lo_ref.shape[1] // leaf
    total = jnp.zeros(part_ref.shape, F32)
    for j in range(block):
        cols = slice(j * leaf, (j + 1) * leaf)
        rounded = (rs_ref[:, cols] * sc_ref[:, cols]).astype(BF16)
        packed, share = leaf_coefficients(basis_ref[j], rounded, trans_ref[j])
        coef_ref[j] = packed
        total += share
        at = step * block + j

        @pl.when(at < half)
        def _():
            lo_ref[:, pl.ds(pl.multiple_of(at * leaf, leaf), leaf)] = rounded

        @pl.when(at >= half)
        def _():
            hi_ref[:, pl.ds(pl.multiple_of((at - half) * leaf, leaf), leaf)] = rounded

    @pl.when(step == 0)
    def _():
        part_ref[...] = total

    @pl.when(step > 0)
    def _():
        part_ref[...] += total


def self_kernel(e_ref, tile_ref):
    leaf = tile_ref.shape[1]
    for j in range(tile_ref.shape[0]):
        points = e_ref[:, j * leaf : (j + 1) * leaf]
        tile_ref[j] = tile_of(other_rows(points), own_rows(points))


def load_windows(refs, vw, cw):
    vl, vo_lo, vo_hi, vh = refs[:4]
    leaf = vw.shape[2]
    for at in range(vw.shape[0]):
        src = (vl, vo_lo, vo_hi, vh)[at // (vw.shape[0] // 4)]
        place = at % (vw.shape[0] // 4)
        vw[at] = src[:, place * leaf : (place + 1) * leaf]
    for slot, ref in enumerate(refs[4:]):
        per = ref.shape[0]
        cw[slot * per : (slot + 1) * per] = ref[...]


def coarse_rows(coarse_ref, sums_ref, fc):
    acc = jnp.zeros(sums_ref.shape[1:], F32)
    for at in range(sums_ref.shape[0]):
        for piece in split3(sums_ref[at]):
            acc += dot(coarse_ref[at], piece, 1, 0)
    fc[...] = jnp.concatenate(split3(acc), axis=1)


def far_columns(j, l, pos, far_ref, cw, coup_ref, trans_ref, fc, basis_ref):
    per = cw.shape[0] // len(FAR_SHIFTS)
    rank = basis_ref.shape[1]
    picks = []
    for s in range(far_ref.shape[1]):
        leaf_id = far_ref[l, s]
        gap = leaf_id // per - pos
        slot = jnp.where(gap < 0, gap + 4, gap + 1)
        picks.append(cw[slot * per + leaf_id % per])
    wide = dot(coup_ref[j], jnp.concatenate(picks, axis=0), 1, 0)
    coupled = wide[:rank, :rank] + wide[rank:, rank:]
    moved = dot(trans_ref[j], fc[...], 1, 0)
    combined = coupled + moved[:, :rank] + moved[:, rank : 2 * rank] + moved[:, 2 * rank :]
    return dot(combined.astype(BF16), basis_ref[j], 0, 0)


def first_kernel(
    near_ref, far_ref, pos_ref,
    tself_ref, rs_ref, sc_ref, basis_ref, coup_ref, trans_ref, coarse_ref, sums_ref,
    el_ref, eo_ref, eh_ref, *rest,
):
    window_refs, rest = rest[:10], rest[10:]
    tile_ref, u_ref, lo_ref, hi_ref, coef_ref, part_ref, msg_ref = rest[:7]
    ew, vw, cw, fc, acc_uu, acc_ru = rest[7:]
    step = pl.program_id(0)
    steps = pl.num_programs(0)
    block, rank, leaf = basis_ref.shape
    half = lo_ref.shape[1] // leaf
    pos = pos_ref[0]

    @pl.when(step == 0)
    def _():
        load_windows(window_refs, vw, cw)
        for at in range(ew.shape[0]):
            quarter = ew.shape[0] // 4
            if at < quarter:
                ew[at] = el_ref[:, at * leaf : (at + 1) * leaf]
            elif at < 3 * quarter:
                ew[at] = eo_ref[:, (at - quarter) * leaf : (at - quarter + 1) * leaf]
            else:
                ew[at] = eh_ref[:, (at - 3 * quarter) * leaf : (at - 3 * quarter + 1) * leaf]
        coarse_rows(coarse_ref, sums_ref, fc)
        acc_uu[...] = jnp.zeros_like(acc_uu)
        acc_ru[...] = jnp.zeros_like(acc_ru)
        part_ref[...] = jnp.zeros_like(part_ref)

    base = pos * 2 * half - half
    for j in range(block):
        l = step * block + j
        cols = slice(j * leaf, (j + 1) * leaf)
        own = own_rows(ew[l + half])
        near = dot(vw[l + half], tself_ref[j], 1, 0)
        for s in range(1, near_ref.shape[1]):
            m = near_ref[l, s] - base
            tile = tile_of(other_rows(ew[m]), own)
            tile_ref[j, s - 1] = tile
            near += dot(vw[m], tile, 1, 0)
        far = far_columns(j, l, pos, far_ref, cw, coup_ref, trans_ref, fc, basis_ref)
        right = rs_ref[:, cols]
        scale = sc_ref[:, cols]
        image = RIDGE_TERM * (right * scale) + (near + far)
        u_ref[:, cols] = image
        acc_uu[...] += image * image
        acc_ru[...] += right * image
        rounded = (image * scale).astype(BF16)
        packed, share = leaf_coefficients(basis_ref[j], rounded, trans_ref[j])
        coef_ref[j] = packed
        part_ref[...] += share

        @pl.when(l < half)
        def _():
            lo_ref[:, pl.ds(pl.multiple_of(l * leaf, leaf), leaf)] = rounded

        @pl.when(l >= half)
        def _():
            hi_ref[:, pl.ds(pl.multiple_of((l - half) * leaf, leaf), leaf)] = rounded

    @pl.when(step == steps - 1)
    def _():
        lane = lax.broadcasted_iota(jnp.int32, msg_ref.shape, 1)
        out = jnp.where(lane == 0, jnp.sum(acc_uu[...], axis=1, keepdims=True), 0.0)
        out = jnp.where(lane == 1, jnp.sum(acc_ru[...], axis=1, keepdims=True), out)
        msg_ref[...] = out


def second_kernel(
    near_ref, far_ref, pos_ref,
    tself_ref, tile_ref, rs_ref, sc_ref, u_ref, basis_ref, coup_ref, trans_ref, coarse_ref,
    sums_ref, prev_ref, *rest,
):
    window_refs, rest = rest[:10], rest[10:]
    w_ref, msg_ref = rest[:2]
    vw, cw, fc, acc_uw, acc_ww, acc_rw = rest[2:]
    step = pl.program_id(0)
    steps = pl.num_programs(0)
    block, rank, leaf = basis_ref.shape
    half = vw.shape[0] // 4
    pos = pos_ref[0]

    @pl.when(step == 0)
    def _():
        load_windows(window_refs, vw, cw)
        coarse_rows(coarse_ref, sums_ref, fc)
        for acc in (acc_uw, acc_ww, acc_rw):
            acc[...] = jnp.zeros_like(acc)

    base = pos * 2 * half - half
    for j in range(block):
        l = step * block + j
        cols = slice(j * leaf, (j + 1) * leaf)
        near = dot(vw[l + half], tself_ref[j], 1, 0)
        for s in range(1, near_ref.shape[1]):
            near += dot(vw[near_ref[l, s] - base], tile_ref[j, s - 1], 1, 0)
        far = far_columns(j, l, pos, far_ref, cw, coup_ref, trans_ref, fc, basis_ref)
        image = u_ref[:, cols]
        second = RIDGE_TERM * (image * sc_ref[:, cols]) + (near + far)
        w_ref[:, cols] = second
        acc_uw[...] += image * second
        acc_ww[...] += second * second
        acc_rw[...] += rs_ref[:, cols] * second

    @pl.when(step == steps - 1)
    def _():
        lane = lax.broadcasted_iota(jnp.int32, msg_ref.shape, 1)
        out = prev_ref[...]
        for at, acc in enumerate((acc_uw, acc_ww, acc_rw)):
            out = jnp.where(lane == 2 + at, jnp.sum(acc[...], axis=1, keepdims=True), out)
        msg_ref[...] = out


def whole(shape):
    return pl.BlockSpec(shape, lambda i, *_: (0,) * len(shape))


def column_block(rows, width):
    return pl.BlockSpec((rows, width), lambda i, *_: (0, i))


def lead_block(shape):
    return pl.BlockSpec(shape, lambda i, *_: (i,) + (0,) * (len(shape) - 1))


def cluster_exchange(part):
    count = lax.axis_size("leaf")
    mask = 1
    while mask < CDEV:
        part = part + swapped(part, mask)
        mask *= 2
    sums = part[None]
    while mask < count:
        sums = jnp.concatenate([sums, swapped(sums, mask)], axis=0)
        mask *= 2
    return sums[1:]


def exchange(lo, hi, coef, part):
    coefs = [shifted(coef, -gap) for gap in FAR_SHIFTS]
    sums = cluster_exchange(part)
    below = shifted(hi, 1)
    above = shifted(lo, -1)
    return [below, lo, hi, above] + coefs, sums


def body(
    right_side, scaling, embeddings, near_leaves, far_leaves, leaf_basis, leaf_coupling,
    transfer, coarse_coupling,
):
    columns, local_points = right_side.shape
    per, rank, leaf = leaf_basis.shape
    features = embeddings.shape[0]
    near_count = near_leaves.shape[1]
    far_count = far_leaves.shape[1]
    half = per // 2
    margin = half * leaf
    steps = per // BLOCK
    width = BLOCK * leaf
    count = lax.axis_size("leaf")
    pos = lax.axis_index("leaf")
    position = pos.reshape(1).astype(jnp.int32)
    cluster = pos // CDEV
    coarse_count = count // CDEV
    scale_row = scaling.reshape(1, local_points)
    trans = transfer.reshape(per, rank, rank)
    coup = leaf_coupling.reshape(per, far_count, rank, 2, rank // 2)
    coup = coup.transpose(0, 3, 2, 1, 4).reshape(per, 2 * rank, far_count * rank // 2)
    row = lax.dynamic_index_in_dim(coarse_coupling, cluster, 0, keepdims=False)
    order = jnp.arange(1, coarse_count, dtype=jnp.int32) ^ cluster
    coarse = jnp.take(row, order, axis=0).reshape(coarse_count - 1, rank, rank)
    params = pltpu.CompilerParams(vmem_limit_bytes=VMEM_LIMIT)

    e_below = shifted(embeddings[:, local_points - margin :], 1)
    e_above = shifted(embeddings[:, :margin], -1)

    half_shape = jax.ShapeDtypeStruct((columns, margin), BF16)
    coef_shape = jax.ShapeDtypeStruct((per, rank // 2, 2 * columns), BF16)
    part_shape = jax.ShapeDtypeStruct((rank, columns), F32)
    msg_shape = jax.ShapeDtypeStruct((columns, 128), F32)
    block_specs = dict(
        rs=column_block(columns, width), sc=column_block(1, width),
        basis=lead_block((BLOCK, rank, leaf)),
        coup=lead_block((BLOCK,) + coup.shape[1:]),
        trans=lead_block((BLOCK, rank, rank)),
        coef=lead_block((BLOCK, rank // 2, 2 * columns)),
        tself=lead_block((BLOCK, leaf, leaf)),
        tile=lead_block((BLOCK, near_count - 1, leaf, leaf)),
    )
    lo, hi, coef, part = pl.pallas_call(
        prep_kernel,
        grid=(per // 4,),
        in_specs=[
            column_block(columns, 4 * leaf), column_block(1, 4 * leaf),
            lead_block((4, rank, leaf)), lead_block((4, rank, rank)),
        ],
        out_specs=[
            whole((columns, margin)), whole((columns, margin)),
            lead_block((4, rank // 2, 2 * columns)), whole((rank, columns)),
        ],
        out_shape=[half_shape, half_shape, coef_shape, part_shape],
        compiler_params=params,
        name="prep",
    )(right_side, scale_row, leaf_basis, trans)

    windows, sums = exchange(lo, hi, coef, part)

    tself = pl.pallas_call(
        self_kernel,
        grid=(steps,),
        in_specs=[column_block(features, width)],
        out_specs=block_specs["tself"],
        out_shape=jax.ShapeDtypeStruct((per, leaf, leaf), BF16),
        compiler_params=params,
        cost_estimate=pl.CostEstimate(
            flops=2 * per * leaf * leaf * 256, bytes_accessed=per * leaf * leaf * 2,
            transcendentals=per * leaf * leaf,
        ),
        name="self_tiles",
    )(embeddings)

    vw_shape = pltpu.VMEM((4 * half, columns, leaf), BF16)
    cw_shape = pltpu.VMEM((len(FAR_SHIFTS) * per, rank // 2, 2 * columns), BF16)
    fc_shape = pltpu.VMEM((rank, 3 * columns), BF16)
    acc_shape = pltpu.VMEM((columns, leaf), F32)
    window_specs = [whole((columns, margin))] * 4
    window_specs += [whole(coef_shape.shape)] * len(FAR_SHIFTS)
    tiles, image, lo, hi, coef, part, msg = pl.pallas_call(
        first_kernel,
        grid_spec=pltpu.PrefetchScalarGridSpec(
            num_scalar_prefetch=3,
            grid=(steps,),
            in_specs=[
                block_specs["tself"], block_specs["rs"], block_specs["sc"], block_specs["basis"],
                block_specs["coup"], block_specs["trans"], whole(coarse.shape), whole(sums.shape),
                whole((features, margin)), whole(embeddings.shape), whole((features, margin)),
            ] + window_specs,
            out_specs=[
                block_specs["tile"], block_specs["rs"], whole((columns, margin)),
                whole((columns, margin)), block_specs["coef"], whole((rank, columns)),
                whole((columns, 128)),
            ],
            scratch_shapes=[
                pltpu.VMEM((4 * half, features, leaf), F32), vw_shape, cw_shape, fc_shape,
                acc_shape, acc_shape,
            ],
        ),
        out_shape=[
            jax.ShapeDtypeStruct((per, near_count - 1, leaf, leaf), BF16),
            jax.ShapeDtypeStruct(right_side.shape, F32),
            half_shape, half_shape, coef_shape, part_shape, msg_shape,
        ],
        compiler_params=params,
        name="first_product",
    )(
        near_leaves, far_leaves, position, tself, right_side, scale_row, leaf_basis, coup, trans,
        coarse, sums, e_below, embeddings, e_above, *windows,
    )

    windows, sums = exchange(lo, hi, coef, part)

    second, msg = pl.pallas_call(
        second_kernel,
        grid_spec=pltpu.PrefetchScalarGridSpec(
            num_scalar_prefetch=3,
            grid=(steps,),
            in_specs=[
                block_specs["tself"], block_specs["tile"], block_specs["rs"], block_specs["sc"],
                block_specs["rs"], block_specs["basis"], block_specs["coup"], block_specs["trans"],
                whole(coarse.shape), whole(sums.shape), whole((columns, 128)),
            ] + window_specs,
            out_specs=[block_specs["rs"], whole((columns, 128))],
            scratch_shapes=[vw_shape, cw_shape, fc_shape, acc_shape, acc_shape, acc_shape],
        ),
        out_shape=[jax.ShapeDtypeStruct(right_side.shape, F32), msg_shape],
        compiler_params=params,
        name="second_product",
    )(
        near_leaves, far_leaves, position, tself, tiles, right_side, scale_row, image, leaf_basis,
        coup, trans, coarse, sums, msg, *windows,
    )

    mask = 1
    while mask < count:
        msg = msg + swapped(msg, mask)
        mask *= 2
    uu, ru, uw, ww, rw = [msg[:, k : k + 1] for k in range(5)]
    step_one = ru / (uu + EPSILON)
    beta = -(uu - step_one * uw) / (uu + EPSILON)
    lead = 1.0 + beta
    curvature = lead * lead * uu - 2.0 * lead * step_one * uw + step_one * step_one * ww
    aligned = lead * (ru - step_one * uu) - step_one * (rw - step_one * uw)
    step_two = aligned / (curvature + EPSILON)
    first_weight = step_one + step_two * lead
    second_weight = step_two * step_one
    solution = scale_row * (first_weight * right_side - second_weight * image)
    residual = right_side - first_weight * image + second_weight * second
    return (solution, residual)


def solution(mesh):
    return jax.shard_map(
        body,
        mesh=mesh,
        in_specs=(
            P(None, ("groups", "leaf")),
            P(("groups", "leaf")),
            P(None, ("groups", "leaf")),
            P(("groups", "leaf"), None),
            P(("groups", "leaf"), None),
            P(("groups", "leaf"), None, None),
            P(("groups", "leaf"), None, None),
            P(("groups", "leaf"), None),
            P("groups", None, None),
        ),
        out_specs=(P(None, ("groups", "leaf")), P(None, ("groups", "leaf"))),
        check_vma=False,
    )
```

```python
import math

import jax
import jax.numpy as jnp
from jax import lax
from jax.experimental import pallas as pl
from jax.experimental.pallas import tpu as pltpu
from jax.sharding import PartitionSpec as P

FARDEV = 4
CDEV = 8
KERNEL_SCALE = 0.0625
RIDGE_TERM = 1.0
EPSILON = 1e-06
F32 = jnp.float32
BF16 = jnp.bfloat16
HALF_SCALE = math.sqrt(2.0 * KERNEL_SCALE * math.log2(math.e))
UNROLL = 2
VMEM_LIMIT = 12 * 1024 * 1024
WHOLE = pl.BlockSpec(memory_space=pltpu.VMEM)
SCALAR = pl.BlockSpec(memory_space=pltpu.SMEM)


def involution(value, partner):
    count = lax.axis_size("leaf")
    pairs = [(i, partner(i)) for i in range(count) if 0 <= partner(i) < count]
    return lax.ppermute(value, "leaf", pairs)


def sibling(value):
    return involution(value, lambda i: i ^ 1)


def beside(value):
    return involution(value, lambda i: i + 1 if i % 2 else i - 1)


def two_chips(value):
    return involution(value, lambda i: i + 3 if i % 2 else i - 3)


def dot(a, b, ca, cb):
    return lax.dot_general(a, b, (((ca,), (cb,)), ((), ())), preferred_element_type=F32)


def split3(value):
    high = value.astype(BF16)
    rest = value - high.astype(F32)
    mid = rest.astype(BF16)
    low = (rest - mid.astype(F32)).astype(BF16)
    return high, mid, low


def point_pieces(points):
    scaled = points * HALF_SCALE
    high, mid, low = split3(scaled)
    square = 0.5 * jnp.sum(scaled * scaled, axis=0, keepdims=True)
    s_high, s_mid, s_low = split3(square)
    return high, mid, low, s_high.astype(F32), s_mid.astype(F32), s_low.astype(F32)


def norm_rows(first, second, third, width, swap, sign):
    row = lax.broadcasted_iota(jnp.int32, (16, width), 0)
    base = 3 if swap else 0
    ones = 0 if swap else 3
    out = jnp.where((row >= ones) & (row < ones + 3), sign, 0.0)
    for at, piece in enumerate((first, second, third)):
        out = jnp.where(row == base + at, sign * piece, out)
    return out.astype(BF16)


def own_rows(points):
    high, mid, low, a, b, c = point_pieces(points)
    norms = norm_rows(a, b, c, points.shape[1], False, 1.0)
    return jnp.concatenate([high, mid, high, mid, low, high, norms], axis=0)


def other_rows(points):
    high, mid, low, a, b, c = point_pieces(points)
    norms = norm_rows(a, b, c, points.shape[1], True, -1.0)
    return jnp.concatenate([high, high, mid, mid, high, low, norms], axis=0)


def tile_of(other, own):
    return jnp.exp2(dot(other, own, 0, 0)).astype(BF16)


def pack_pair(block):
    half = block.shape[0] // 2
    return jnp.concatenate([block[:half], block[half:]], axis=1)


def leaf_coefficients(basis, rounded, trans):
    coef = dot(basis, rounded, 1, 1).astype(BF16)
    return pack_pair(coef), dot(trans, coef, 0, 0)


def columns_of(ref, at, width):
    return ref[:, pl.ds(pl.multiple_of(at * width, width), width)]


def leaf_loop(count, unroll, fn):
    def trip(i, carry):
        for u in range(unroll):
            fn(i * unroll + u)
        return carry

    lax.fori_loop(0, count // unroll, trip, 0)


def send_margins(v_ref, mx_ref, mo_ref, odd):
    half = mx_ref.shape[0]
    mx_ref[...] = v_ref[pl.ds(half * (1 - odd), half)]
    mo_ref[...] = v_ref[pl.ds(half * odd, half)]


def store_share(total, part_ref, cp_ref, rows):
    packed = pack_pair(total)
    part_ref[...] = packed
    size = packed.shape[0]
    for at, piece in enumerate(split3(packed)):
        cp_ref[rows + at * size : rows + (at + 1) * size] = piece


def prep_kernel(pos_ref, rs_ref, sc_ref, basis_ref, trans_ref, v_ref, mx_ref, mo_ref, cp_ref, part_ref, acc):
    per, rank, leaf = basis_ref.shape
    size = rank // 2
    acc[...] = jnp.zeros_like(acc)

    def one(at):
        rounded = (columns_of(rs_ref, at, leaf) * columns_of(sc_ref, at, leaf)).astype(BF16)
        packed, share = leaf_coefficients(basis_ref[at], rounded, trans_ref[at])
        v_ref[at] = rounded
        cp_ref[pl.ds(pl.multiple_of(at * size, size), size)] = packed
        acc[...] += share

    leaf_loop(per, UNROLL, one)
    store_share(acc[...], part_ref, cp_ref, per * size)
    send_margins(v_ref, mx_ref, mo_ref, pos_ref[0] % 2)


def pair_kernel(pos_ref, own_ref, got_ref, part_ref, pair_ref, sum_ref):
    odd = pos_ref[0] % 2
    rows = pair_ref.shape[1]
    size = part_ref.shape[0]
    pair_ref[odd] = own_ref[:rows]
    pair_ref[1 - odd] = got_ref[:rows]
    total = part_ref[...]
    for at in range(3):
        total += got_ref[rows + at * size : rows + (at + 1) * size].astype(F32)
    sum_ref[...] = total


def list_entries(near_ref, list_ref, pos, half, want_own):
    slots = near_ref.shape[1] - 1
    total = near_ref.shape[0] * slots
    base = pos * 2 * half - half

    def put(at, n):
        m = near_ref[at // slots, 1 + at % slots] - base
        own = (m >= half) & (m < 3 * half)
        list_ref[n] = at
        return n + jnp.where(own == want_own, 1, 0)

    n = lax.fori_loop(0, total, put, 0)
    list_ref[n] = total
    return n


def near_entry(near_ref, list_ref, at, pos, half, own):
    slots = near_ref.shape[1] - 1
    per = near_ref.shape[0]
    entry = list_ref[at]
    spare = entry == per * slots
    leaf_at = entry // slots
    row = jnp.minimum(leaf_at, per - 1)
    m = near_ref[row, 1 + entry % slots] - (pos * 2 * half - half)
    if own:
        place = jnp.clip(m - half, 0, per - 1)
    else:
        place = jnp.clip(jnp.where(m < half, m, m - 2 * half), 0, 2 * half - 1)
    return entry, leaf_at, row, place


def load_halves(target, from_sibling, from_beside, odd):
    half = from_sibling.shape[0]
    target[pl.ds(half * (1 - odd), half)] = from_sibling[...]
    target[pl.ds(half * odd, half)] = from_beside[...]


def own_kernel(pos_ref, near_ref, e_ref, v_ref, tile_ref, near_out, list_ref):
    per, _, leaf = v_ref.shape
    half = per // 2
    pos = pos_ref[0]

    def one(at):
        points = columns_of(e_ref, at, leaf)
        tile = tile_of(other_rows(points), own_rows(points))
        tile_ref[at] = tile
        near_out[at] = dot(v_ref[at], tile, 1, 0)

    leaf_loop(per, UNROLL, one)
    n = list_entries(near_ref, list_ref, pos, half, True)

    def trip(i, carry):
        for u in range(UNROLL):
            entry, leaf_at, row, place = near_entry(near_ref, list_ref, i * UNROLL + u, pos, half, True)
            tile = tile_of(other_rows(columns_of(e_ref, place, leaf)), own_rows(columns_of(e_ref, row, leaf)))
            tile_ref[per + entry] = tile
            near_out[leaf_at] += dot(v_ref[place], tile, 1, 0)
        return carry

    lax.fori_loop(0, (n + UNROLL - 1) // UNROLL, trip, 0)


def own_again_kernel(pos_ref, near_ref, v_ref, tile_ref, near_out, list_ref):
    per, _, leaf = v_ref.shape
    half = per // 2
    pos = pos_ref[0]

    def one(at):
        near_out[at] = dot(v_ref[at], tile_ref[at], 1, 0)

    leaf_loop(per, UNROLL, one)
    n = list_entries(near_ref, list_ref, pos, half, True)

    def trip(i, carry):
        for u in range(UNROLL):
            entry, leaf_at, _, place = near_entry(near_ref, list_ref, i * UNROLL + u, pos, half, True)
            near_out[leaf_at] += dot(v_ref[place], tile_ref[per + entry], 1, 0)
        return carry

    lax.fori_loop(0, (n + UNROLL - 1) // UNROLL, trip, 0)


def load_coefficients(cw, sources):
    rows = sources[0].shape[1]
    per = rows // cw.shape[1]
    for slot, source in enumerate(sources):
        for core in range(2):
            for at in range(per):
                cw[(slot * 2 + core) * per + at] = source[core, at * cw.shape[1] : (at + 1) * cw.shape[1]]


def coarse_rows(coarse_ref, sum_refs, fc):
    rank = coarse_ref.shape[1]
    acc = jnp.zeros((rank, rank), F32)
    for at in range(coarse_ref.shape[0]):
        packed = sum_refs[0][at]
        for ref in sum_refs[1:]:
            packed += ref[at]
        total = jnp.concatenate([packed[:, :rank], packed[:, rank:]], axis=0)
        for piece in split3(total):
            acc += dot(coarse_ref[at], piece, 1, 0)
    fc[...] = jnp.concatenate(split3(acc), axis=1)


def far_columns(l, pos, far_ref, cw, coup_ref, trans_ref, fc, basis_ref):
    per, rank, _ = basis_ref.shape
    odd = pos % 2
    picks = []
    for s in range(far_ref.shape[1]):
        leaf_id = far_ref[l, s]
        device = leaf_id // per
        gap = device // 2 - pos // 2
        direct = (gap < 0) == (odd == 0)
        slot = jnp.where(direct, 0, 2) + jnp.where(jnp.abs(gap) == 2, 1, 0)
        picks.append(cw[(slot * 2 + device % 2) * per + leaf_id % per])
    wide = dot(coup_ref[l], jnp.concatenate(picks, axis=0), 1, 0)
    coupled = wide[:rank, :rank] + wide[rank:, rank:]
    moved = dot(trans_ref[l], fc[...], 1, 0)
    combined = coupled + moved[:, :rank] + moved[:, rank : 2 * rank] + moved[:, 2 * rank :]
    return dot(combined.astype(BF16), basis_ref[l], 0, 0)


def rest_kernel(
    pos_ref, near_ref, far_ref, e_ref, ex_ref, eo_ref, rs_ref, sc_ref, basis_ref, coup_ref, trans_ref,
    coarse_ref, sum_a, sum_b, vx_ref, vo_ref, c0, c1, c2, c3, tile_in, near_in,
    tile_ref, near_ref_out, u_ref, q_ref, mx_ref, mo_ref, cp_ref, part_ref, msg_ref,
    list_ref, vw, cw, fc, acc, acc_uu, acc_ru,
):
    per, rank, leaf = basis_ref.shape
    half = per // 2
    size = rank // 2
    pos = pos_ref[0]
    odd = pos % 2
    load_halves(vw, vx_ref, vo_ref, odd)
    load_coefficients(cw, (c0, c1, c2, c3))
    coarse_rows(coarse_ref, (sum_a, sum_b), fc)
    n = list_entries(near_ref, list_ref, pos, half, False)

    def trip(i, carry):
        for u in range(UNROLL):
            entry, leaf_at, row, place = near_entry(near_ref, list_ref, i * UNROLL + u, pos, half, False)
            beneath = place < half
            from_x = beneath == (odd == 1)
            within = jnp.where(beneath, place, place - half)
            far_x = columns_of(ex_ref, within, leaf)
            far_o = columns_of(eo_ref, within, leaf)
            points = jnp.where(from_x, far_x, far_o)
            tile = tile_of(other_rows(points), own_rows(columns_of(e_ref, row, leaf)))
            tile_ref[per + entry] = tile
            near_ref_out[leaf_at] += dot(vw[place], tile, 1, 0)
        return carry

    lax.fori_loop(0, (n + UNROLL - 1) // UNROLL, trip, 0)
    acc[...] = jnp.zeros_like(acc)
    acc_uu[...] = jnp.zeros_like(acc_uu)
    acc_ru[...] = jnp.zeros_like(acc_ru)

    def one(l):
        far = far_columns(l, pos, far_ref, cw, coup_ref, trans_ref, fc, basis_ref)
        right = columns_of(rs_ref, l, leaf)
        scale = columns_of(sc_ref, l, leaf)
        image = RIDGE_TERM * (right * scale) + (near_ref_out[l] + far)
        u_ref[:, pl.ds(pl.multiple_of(l * leaf, leaf), leaf)] = image
        acc_uu[...] += image * image
        acc_ru[...] += right * image
        rounded = (image * scale).astype(BF16)
        packed, share = leaf_coefficients(basis_ref[l], rounded, trans_ref[l])
        q_ref[l] = rounded
        cp_ref[pl.ds(pl.multiple_of(l * size, size), size)] = packed
        acc[...] += share

    leaf_loop(per, UNROLL, one)
    store_share(acc[...], part_ref, cp_ref, per * size)
    send_margins(q_ref, mx_ref, mo_ref, odd)
    lane = lax.broadcasted_iota(jnp.int32, msg_ref.shape, 1)
    out = jnp.where(lane == 0, jnp.sum(acc_uu[...], axis=1, keepdims=True), 0.0)
    out = jnp.where(lane == 1, jnp.sum(acc_ru[...], axis=1, keepdims=True), out)
    msg_ref[...] = out


def rest_again_kernel(
    pos_ref, near_ref, far_ref, rs_ref, sc_ref, u_ref, basis_ref, coup_ref, trans_ref,
    coarse_ref, sum_a, sum_b, vx_ref, vo_ref, c0, c1, c2, c3, tile_ref, near_in, prev_ref,
    near_out, w_ref, msg_ref,
    list_ref, vw, cw, fc, acc_uw, acc_ww, acc_rw,
):
    per, rank, leaf = basis_ref.shape
    half = per // 2
    pos = pos_ref[0]
    load_halves(vw, vx_ref, vo_ref, pos % 2)
    load_coefficients(cw, (c0, c1, c2, c3))
    coarse_rows(coarse_ref, (sum_a, sum_b), fc)
    n = list_entries(near_ref, list_ref, pos, half, False)

    def trip(i, carry):
        for u in range(UNROLL):
            entry, leaf_at, _, place = near_entry(near_ref, list_ref, i * UNROLL + u, pos, half, False)
            near_out[leaf_at] += dot(vw[place], tile_ref[per + entry], 1, 0)
        return carry

    lax.fori_loop(0, (n + UNROLL - 1) // UNROLL, trip, 0)
    for acc in (acc_uw, acc_ww, acc_rw):
        acc[...] = jnp.zeros_like(acc)

    def one(l):
        far = far_columns(l, pos, far_ref, cw, coup_ref, trans_ref, fc, basis_ref)
        image = columns_of(u_ref, l, leaf)
        second = RIDGE_TERM * (image * columns_of(sc_ref, l, leaf)) + (near_out[l] + far)
        w_ref[:, pl.ds(pl.multiple_of(l * leaf, leaf), leaf)] = second
        acc_uw[...] += image * second
        acc_ww[...] += second * second
        acc_rw[...] += columns_of(rs_ref, l, leaf) * second

    leaf_loop(per, UNROLL, one)
    lane = lax.broadcasted_iota(jnp.int32, msg_ref.shape, 1)
    out = prev_ref[...]
    for at, acc in enumerate((acc_uw, acc_ww, acc_rw)):
        out = jnp.where(lane == 2 + at, jnp.sum(acc[...], axis=1, keepdims=True), out)
    msg_ref[...] = out


def call(kernel, name, in_specs, out_shape, scratch, args, aliases=None, flops=0):
    return pl.pallas_call(
        kernel,
        in_specs=in_specs,
        out_specs=[WHOLE] * len(out_shape),
        out_shape=out_shape,
        scratch_shapes=scratch,
        input_output_aliases=aliases or {},
        compiler_params=pltpu.CompilerParams(vmem_limit_bytes=VMEM_LIMIT),
        cost_estimate=pl.CostEstimate(flops=flops, bytes_accessed=0, transcendentals=0),
        name=name,
    )(*args)


def cluster_sums(pair_sum):
    count = lax.axis_size("leaf")
    if count == 2 * CDEV and CDEV == 8:
        first = involution(pair_sum, lambda i: i ^ (8 + 2 * (i % 2)))
        second = involution(pair_sum, lambda i: i ^ (12 + 2 * (i % 2)))
        mine = (first + second)[None]
        return mine, sibling(mine)
    mask = 2
    while mask < CDEV:
        pair_sum = pair_sum + involution(pair_sum, lambda i: i ^ mask)
        mask *= 2
    sums = pair_sum[None]
    while mask < count:
        sums = jnp.concatenate([sums, involution(sums, lambda i: i ^ mask)], axis=0)
        mask *= 2
    return sums[1:], jnp.zeros_like(sums[1:])


def exchange(position, cp, part, mx, mo):
    rows = cp.shape[0] - 3 * part.shape[0]
    got = sibling(cp)
    pair, pair_sum = call(
        pair_kernel, "pair", [SCALAR] + [WHOLE] * 3,
        [pltpu.VMEM((2, rows, cp.shape[1]), BF16), jax.ShapeDtypeStruct(part.shape, F32)],
        [], (position, cp, got, part),
    )
    near_pair = beside(pair)
    far_pair = two_chips(pair)
    sums = cluster_sums(pair_sum)
    vx = sibling(mx)
    vo = beside(mo)
    return vx, vo, (near_pair, far_pair, sibling(near_pair), sibling(far_pair)), sums


def body(
    right_side, scaling, embeddings, near_leaves, far_leaves, leaf_basis, leaf_coupling,
    transfer, coarse_coupling,
):
    columns, local_points = right_side.shape
    per, rank, leaf = leaf_basis.shape
    features = embeddings.shape[0]
    slots = near_leaves.shape[1] - 1
    far_count = far_leaves.shape[1]
    half = per // 2
    margin = half * leaf
    size = rank // 2
    count = lax.axis_size("leaf")
    pos = lax.axis_index("leaf")
    odd = pos % 2
    position = pos.reshape(1).astype(jnp.int32)
    cluster = pos // CDEV
    coarse_count = count // CDEV

    e_sibling = sibling(lax.dynamic_slice_in_dim(embeddings, (1 - odd) * margin, margin, 1))
    e_beside = beside(lax.dynamic_slice_in_dim(embeddings, odd * margin, margin, 1))

    scale_row = scaling.reshape(1, local_points)
    trans = transfer.reshape(per, rank, rank)
    coup = leaf_coupling.reshape(per, far_count, rank, 2, rank // 2)
    coup = coup.transpose(0, 3, 2, 1, 4).reshape(per, 2 * rank, far_count * rank // 2)
    row = lax.dynamic_index_in_dim(coarse_coupling, cluster, 0, keepdims=False)
    order = jnp.arange(1, coarse_count, dtype=jnp.int32) ^ cluster
    coarse = jnp.take(row, order, axis=0).reshape(coarse_count - 1, rank, rank)

    leaf_shape = pltpu.VMEM((per, columns, leaf), BF16)
    half_shape = pltpu.VMEM((half, columns, leaf), BF16)
    cp_shape = pltpu.VMEM((per * size + 3 * size, 2 * columns), BF16)
    part_shape = pltpu.VMEM((size, 2 * columns), F32)
    tile_shape = pltpu.VMEM((per * (1 + slots) + 1, leaf, leaf), BF16)
    near_shape = pltpu.VMEM((per + 1, columns, leaf), F32)
    wide_shape = pltpu.VMEM((columns, local_points), F32)
    msg_shape = pltpu.VMEM((columns, 128), F32)
    share_acc = pltpu.VMEM((rank, columns), F32)
    acc_shape = pltpu.VMEM((columns, leaf), F32)
    list_shape = pltpu.SMEM((per * slots + UNROLL,), jnp.int32)
    window = [
        pltpu.VMEM((2 * half, columns, leaf), BF16),
        pltpu.VMEM((8 * per, size, 2 * columns), BF16),
        pltpu.VMEM((rank, 3 * columns), BF16),
    ]

    v, mx, mo, cp, part = call(
        prep_kernel, "prep", [SCALAR] + [WHOLE] * 4,
        [leaf_shape, half_shape, half_shape, cp_shape, part_shape], [share_acc],
        (position, right_side, scale_row, leaf_basis, trans),
    )
    vx, vo, coefs, sums = exchange(position, cp, part, mx, mo)
    tiles, near = call(
        own_kernel, "own_tiles", [SCALAR] * 2 + [WHOLE] * 2, [tile_shape, near_shape], [list_shape],
        (position, near_leaves, embeddings, v), flops=2 * 32 * leaf * leaf * 320,
    )
    tiles, _, image, q, mx, mo, cp, part, msg = call(
        rest_kernel, "first_product", [SCALAR] * 3 + [WHOLE] * 19,
        [tile_shape, near_shape, wide_shape, leaf_shape, half_shape, half_shape, cp_shape, part_shape, msg_shape],
        [list_shape] + window + [share_acc, acc_shape, acc_shape],
        (position, near_leaves, far_leaves, embeddings, e_sibling, e_beside, right_side, scale_row,
         leaf_basis, coup, trans, coarse, *sums, vx, vo, *coefs, tiles, near),
        aliases={20: 0, 21: 1}, flops=2 * 16 * leaf * leaf * 320,
    )
    vx, vo, coefs, sums = exchange(position, cp, part, mx, mo)
    (near,) = call(
        own_again_kernel, "own_again", [SCALAR] * 2 + [WHOLE] * 2, [near_shape], [list_shape],
        (position, near_leaves, q, tiles), flops=2 * 32 * leaf * leaf * 64,
    )
    _, second, msg = call(
        rest_again_kernel, "second_product", [SCALAR] * 3 + [WHOLE] * 18,
        [near_shape, wide_shape, msg_shape],
        [list_shape] + window + [acc_shape] * 3,
        (position, near_leaves, far_leaves, right_side, scale_row, image, leaf_basis, coup, trans,
         coarse, *sums, vx, vo, *coefs, tiles, near, msg),
        aliases={19: 0}, flops=2 * 16 * leaf * leaf * 64,
    )

    mask = 1
    while mask < count:
        msg = msg + involution(msg, lambda i: i ^ mask)
        mask *= 2
    uu, ru, uw, ww, rw = [msg[:, k : k + 1] for k in range(5)]
    step_one = ru / (uu + EPSILON)
    beta = -(uu - step_one * uw) / (uu + EPSILON)
    lead = 1.0 + beta
    curvature = lead * lead * uu - 2.0 * lead * step_one * uw + step_one * step_one * ww
    aligned = lead * (ru - step_one * uu) - step_one * (rw - step_one * uw)
    step_two = aligned / (curvature + EPSILON)
    first_weight = step_one + step_two * lead
    second_weight = step_two * step_one
    solution = scale_row * (first_weight * right_side - second_weight * image)
    residual = right_side - first_weight * image + second_weight * second
    return (solution, residual)


def solution(mesh):
    return jax.shard_map(
        body,
        mesh=mesh,
        in_specs=(
            P(None, ("groups", "leaf")),
            P(("groups", "leaf")),
            P(None, ("groups", "leaf")),
            P(("groups", "leaf"), None),
            P(("groups", "leaf"), None),
            P(("groups", "leaf"), None, None),
            P(("groups", "leaf"), None, None),
            P(("groups", "leaf"), None),
            P("groups", None, None),
        ),
        out_specs=(P(None, ("groups", "leaf")), P(None, ("groups", "leaf"))),
        check_vma=False,
    )
```

```python
import math

import jax
import jax.numpy as jnp
from jax import lax
from jax.experimental import pallas as pl
from jax.experimental.pallas import tpu as pltpu
from jax.sharding import PartitionSpec as P

FARDEV = 4
CDEV = 8
KERNEL_SCALE = 0.0625
RIDGE_TERM = 1.0
EPSILON = 1e-06
F32 = jnp.float32
BF16 = jnp.bfloat16
HALF_SCALE = math.sqrt(2.0 * KERNEL_SCALE * math.log2(math.e))
UNROLL = 4
VMEM_LIMIT = 8 * 1024 * 1024
WHOLE = pl.BlockSpec(memory_space=pltpu.VMEM)
ANYWHERE = pl.BlockSpec(memory_space=pl.ANY)
SCALAR = pl.BlockSpec(memory_space=pltpu.SMEM)


def involution(value, partner):
    count = lax.axis_size("leaf")
    pairs = [(i, partner(i)) for i in range(count) if 0 <= partner(i) < count]
    return lax.ppermute(value, "leaf", pairs)


def sibling(value):
    return involution(value, lambda i: i ^ 1)


def beside(value):
    return involution(value, lambda i: i + 1 if i % 2 else i - 1)


def two_chips(value):
    return involution(value, lambda i: i + 3 if i % 2 else i - 3)


def dot(a, b, ca, cb):
    return lax.dot_general(a, b, (((ca,), (cb,)), ((), ())), preferred_element_type=F32)


def split3(value):
    high = value.astype(BF16)
    rest = value - high.astype(F32)
    mid = rest.astype(BF16)
    low = (rest - mid.astype(F32)).astype(BF16)
    return high, mid, low


def point_pieces(points):
    scaled = points * HALF_SCALE
    high, mid, low = split3(scaled)
    square = 0.5 * jnp.sum(scaled * scaled, axis=0, keepdims=True)
    s_high, s_mid, s_low = split3(square)
    return high, mid, low, s_high.astype(F32), s_mid.astype(F32), s_low.astype(F32)


def norm_rows(first, second, third, width, swap, sign):
    row = lax.broadcasted_iota(jnp.int32, (16, width), 0)
    base = 3 if swap else 0
    ones = 0 if swap else 3
    out = jnp.where((row >= ones) & (row < ones + 3), sign, 0.0)
    for at, piece in enumerate((first, second, third)):
        out = jnp.where(row == base + at, sign * piece, out)
    return out.astype(BF16)


def own_rows(points):
    high, mid, low, a, b, c = point_pieces(points)
    norms = norm_rows(a, b, c, points.shape[1], False, 1.0)
    return jnp.concatenate([high, mid, high, mid, low, high, norms], axis=0)


def other_rows(points):
    high, mid, low, a, b, c = point_pieces(points)
    norms = norm_rows(a, b, c, points.shape[1], True, -1.0)
    return jnp.concatenate([high, high, mid, mid, high, low, norms], axis=0)


def tile_of(other, own):
    return jnp.exp2(dot(other, own, 0, 0)).astype(BF16)


def pack_pair(block):
    half = block.shape[0] // 2
    return jnp.concatenate([block[:half], block[half:]], axis=1)


def store_coefficients(basis, rounded, at, cp_ref, coefs):
    coef = dot(basis, rounded, 1, 1).astype(BF16)
    rank = coef.shape[0]
    coefs[pl.ds(pl.multiple_of(at * rank, rank), rank)] = coef
    size = rank // 2
    cp_ref[pl.ds(pl.multiple_of(at * size, size), size)] = pack_pair(coef)


def columns_of(ref, at, width):
    return ref[:, pl.ds(pl.multiple_of(at * width, width), width)]


def leaf_loop(count, unroll, fn):
    def trip(i, carry):
        for u in range(unroll):
            fn(i * unroll + u)
        return carry

    lax.fori_loop(0, count // unroll, trip, 0)


def store_share(trans_ref, coefs, part_ref, cp_ref):
    per, rank, _ = trans_ref.shape
    packed = pack_pair(dot(trans_ref[...].reshape(per * rank, rank), coefs[...], 0, 0))
    part_ref[...] = packed
    size = packed.shape[0]
    rows = per * size
    for at, piece in enumerate(split3(packed)):
        cp_ref[rows + at * size : rows + (at + 1) * size] = piece


def relayout_kernel(coup_ref, out_ref, by_slot, by_row):
    per, slots, flat = coup_ref.shape
    rank = out_ref.shape[1] // 2
    quarter = rank // 2
    pairs = flat // 128
    lane = lax.broadcasted_iota(jnp.int32, (pairs, 128), 1) // quarter

    def one(l, carry):
        wide = coup_ref[l].astype(F32)
        for k in range(pairs):
            by_slot[k * slots : (k + 1) * slots] = wide[:, k * 128 : (k + 1) * 128]
        rows = [by_slot[pl.ds(s, pairs, stride=slots)] for s in range(slots)]
        turned = [[rows[s] if t == 0 else pltpu.roll(rows[s], t * quarter, 1) for t in range(4)] for s in range(slots)]
        for half in range(2):
            for parity in range(2):
                chunk = 2 * parity + half
                for group in range(slots // 4):
                    out = turned[4 * group][(0 - chunk) % 4]
                    for r in range(1, 4):
                        out = jnp.where(lane == r, turned[4 * group + r][(r - chunk) % 4], out)
                    by_row[half, group, pl.ds(parity, pairs, stride=2)] = out
        for half in range(2):
            for group in range(slots // 4):
                out_ref[l, half * rank : (half + 1) * rank, group * 128 : (group + 1) * 128] = by_row[half, group].astype(BF16)
        return carry

    lax.fori_loop(0, per, one, 0)


def margins_kernel(pos_ref, e_ref, ex_ref, eo_ref, sems):
    odd = pos_ref[0] % 2
    width = ex_ref.shape[1]
    first = pltpu.make_async_copy(
        e_ref.at[:, pl.ds(pl.multiple_of((1 - odd) * width, width), width)], ex_ref, sems.at[0]
    )
    second = pltpu.make_async_copy(
        e_ref.at[:, pl.ds(pl.multiple_of(odd * width, width), width)], eo_ref, sems.at[1]
    )
    first.start()
    second.start()
    first.wait()
    second.wait()


def prep_kernel(rs_ref, sc_ref, basis_ref, trans_ref, ex_ref, eo_ref, v_ref, cp_ref, part_ref, coefs):
    per, rank, leaf = basis_ref.shape

    def one(at):
        rounded = (columns_of(rs_ref, at, leaf) * columns_of(sc_ref, at, leaf)).astype(BF16)
        v_ref[at] = rounded
        store_coefficients(basis_ref[at], rounded, at, cp_ref, coefs)

    leaf_loop(per, UNROLL, one)
    store_share(trans_ref, coefs, part_ref, cp_ref)


def send_kernel(pos_ref, v_ref, a_ref, b_ref, *rest):
    mx_ref, mo_ref, sum_ref = rest[-3:]
    odd = pos_ref[0] % 2
    half = mx_ref.shape[0]
    mx_ref[...] = v_ref[pl.ds(half * (1 - odd), half)]
    mo_ref[...] = v_ref[pl.ds(half * odd, half)]
    sum_ref[...] = a_ref[...] + b_ref[...]


def pair_kernel(pos_ref, own_ref, got_ref, part_ref, pair_ref, sum_ref):
    odd = pos_ref[0] % 2
    rows = pair_ref.shape[1]
    size = part_ref.shape[0]
    pair_ref[odd] = own_ref[:rows]
    pair_ref[1 - odd] = got_ref[:rows]
    total = part_ref[...]
    for at in range(3):
        total += got_ref[rows + at * size : rows + (at + 1) * size].astype(F32)
    sum_ref[...] = total


def list_entries(near_ref, list_ref, pos, half, want_own):
    slots = near_ref.shape[1] - 1
    total = near_ref.shape[0] * slots
    base = pos * 2 * half - half

    def put(at, n):
        m = near_ref[at // slots, 1 + at % slots] - base
        own = (m >= half) & (m < 3 * half)
        list_ref[n] = at
        return n + jnp.where(own == want_own, 1, 0)

    n = lax.fori_loop(0, total, put, 0)
    for u in range(UNROLL):
        list_ref[n + u] = total
    return n


def near_entry(near_ref, list_ref, at, pos, half, own):
    slots = near_ref.shape[1] - 1
    per = near_ref.shape[0]
    entry = list_ref[at]
    spare = entry == per * slots
    leaf_at = entry // slots
    row = jnp.minimum(leaf_at, per - 1)
    m = near_ref[row, 1 + entry % slots] - (pos * 2 * half - half)
    if own:
        place = jnp.clip(m - half, 0, per - 1)
    else:
        place = jnp.clip(jnp.where(m < half, m, m - 2 * half), 0, 2 * half - 1)
    return entry, leaf_at, row, place


def load_halves(target, from_sibling, from_beside, odd):
    half = from_sibling.shape[0]
    target[pl.ds(half * (1 - odd), half)] = from_sibling[...]
    target[pl.ds(half * odd, half)] = from_beside[...]


def self_kernel(e_ref, v_ref, self_ref, near_out):
    per, _, leaf = v_ref.shape

    def one(at):
        points = columns_of(e_ref, at, leaf)
        tile = tile_of(other_rows(points), own_rows(points))
        self_ref[at] = tile
        near_out[at] = dot(v_ref[at], tile, 1, 0)

    leaf_loop(per, UNROLL, one)


def own_kernel(pos_ref, near_ref, e_ref, v_ref, near_in, tile_ref, near_out, list_ref):
    per, _, leaf = v_ref.shape
    half = per // 2
    pos = pos_ref[0]
    n = list_entries(near_ref, list_ref, pos, half, True)

    def trip(i, carry):
        for u in range(UNROLL):
            entry, leaf_at, row, place = near_entry(near_ref, list_ref, i * UNROLL + u, pos, half, True)
            tile = tile_of(other_rows(columns_of(e_ref, place, leaf)), own_rows(columns_of(e_ref, row, leaf)))
            tile_ref[entry] = tile
            near_out[leaf_at] += dot(v_ref[place], tile, 1, 0)
        return carry

    lax.fori_loop(0, (n + UNROLL - 1) // UNROLL, trip, 0)


def self_again_kernel(v_ref, self_ref, near_out):
    def one(at):
        near_out[at] = dot(v_ref[at], self_ref[at], 1, 0)

    leaf_loop(v_ref.shape[0], UNROLL, one)


def own_again_kernel(pos_ref, near_ref, v_ref, tile_ref, near_in, near_out, list_ref):
    half = v_ref.shape[0] // 2
    pos = pos_ref[0]
    n = list_entries(near_ref, list_ref, pos, half, True)

    def trip(i, carry):
        for u in range(UNROLL):
            entry, leaf_at, _, place = near_entry(near_ref, list_ref, i * UNROLL + u, pos, half, True)
            near_out[leaf_at] += dot(v_ref[place], tile_ref[entry], 1, 0)
        return carry

    lax.fori_loop(0, (n + UNROLL - 1) // UNROLL, trip, 0)


def load_coefficients(cw, sources):
    rows = sources[0].shape[1]
    per = rows // cw.shape[1]
    for slot, source in enumerate(sources):
        for core in range(2):
            for at in range(per):
                cw[(slot * 2 + core) * per + at] = source[core, at * cw.shape[1] : (at + 1) * cw.shape[1]]


def coarse_rows(coarse_ref, sum_refs, fc):
    rank = coarse_ref.shape[1]
    acc = jnp.zeros((rank, rank), F32)
    for at in range(coarse_ref.shape[0]):
        packed = sum_refs[0][at]
        for ref in sum_refs[1:]:
            packed += ref[at]
        total = jnp.concatenate([packed[:, :rank], packed[:, rank:]], axis=0)
        for piece in split3(total):
            acc += dot(coarse_ref[at], piece, 1, 0)
    fc[...] = jnp.concatenate(split3(acc), axis=1)


def far_columns(l, pos, far_ref, cw, coup_ref, trans_ref, fc, basis_ref):
    per, rank, _ = basis_ref.shape
    odd = pos % 2
    picks = []
    for s in range(far_ref.shape[1]):
        leaf_id = far_ref[l, s]
        device = leaf_id // per
        gap = device // 2 - pos // 2
        direct = (gap < 0) == (odd == 0)
        slot = jnp.where(direct, 0, 2) + jnp.where(jnp.abs(gap) == 2, 1, 0)
        picks.append(cw[(slot * 2 + device % 2) * per + leaf_id % per])
    wide = dot(coup_ref[l], jnp.concatenate(picks, axis=0), 1, 0)
    coupled = wide[:rank, :rank] + wide[rank:, rank:]
    moved = dot(trans_ref[l], fc[...], 1, 0)
    combined = coupled + moved[:, :rank] + moved[:, rank : 2 * rank] + moved[:, 2 * rank :]
    return dot(combined.astype(BF16), basis_ref[l], 0, 0)


def rest_kernel(
    pos_ref, near_ref, far_ref, e_ref, ex_ref, eo_ref, rs_ref, sc_ref, basis_ref, coup_ref, trans_ref,
    coarse_ref, sum_a, sum_b, vx_ref, vo_ref, c0, c1, c2, c3, tile_in, near_in,
    tile_ref, near_ref_out, u_ref, q_ref, cp_ref, part_ref, msg_ref,
    list_ref, vw, cw, fc, coefs, acc_uu, acc_ru,
):
    per, rank, leaf = basis_ref.shape
    half = per // 2
    pos = pos_ref[0]
    odd = pos % 2
    load_halves(vw, vx_ref, vo_ref, odd)
    load_coefficients(cw, (c0, c1, c2, c3))
    coarse_rows(coarse_ref, (sum_a, sum_b), fc)
    n = list_entries(near_ref, list_ref, pos, half, False)

    def trip(i, carry):
        for u in range(UNROLL):
            entry, leaf_at, row, place = near_entry(near_ref, list_ref, i * UNROLL + u, pos, half, False)
            beneath = place < half
            from_x = beneath == (odd == 1)
            within = jnp.where(beneath, place, place - half)
            far_x = columns_of(ex_ref, within, leaf)
            far_o = columns_of(eo_ref, within, leaf)
            points = jnp.where(from_x, far_x, far_o)
            tile = tile_of(other_rows(points), own_rows(columns_of(e_ref, row, leaf)))
            tile_ref[entry] = tile
            near_ref_out[leaf_at] += dot(vw[place], tile, 1, 0)
        return carry

    lax.fori_loop(0, (n + UNROLL - 1) // UNROLL, trip, 0)
    acc_uu[...] = jnp.zeros_like(acc_uu)
    acc_ru[...] = jnp.zeros_like(acc_ru)

    def one(l):
        far = far_columns(l, pos, far_ref, cw, coup_ref, trans_ref, fc, basis_ref)
        right = columns_of(rs_ref, l, leaf)
        scale = columns_of(sc_ref, l, leaf)
        image = RIDGE_TERM * (right * scale) + (near_ref_out[l] + far)
        u_ref[:, pl.ds(pl.multiple_of(l * leaf, leaf), leaf)] = image
        acc_uu[...] += image * image
        acc_ru[...] += right * image
        rounded = (image * scale).astype(BF16)
        q_ref[l] = rounded
        store_coefficients(basis_ref[l], rounded, l, cp_ref, coefs)

    leaf_loop(per, UNROLL, one)
    store_share(trans_ref, coefs, part_ref, cp_ref)
    lane = lax.broadcasted_iota(jnp.int32, msg_ref.shape, 1)
    out = jnp.where(lane == 0, jnp.sum(acc_uu[...], axis=1, keepdims=True), 0.0)
    out = jnp.where(lane == 1, jnp.sum(acc_ru[...], axis=1, keepdims=True), out)
    msg_ref[...] = out


def rest_again_kernel(
    pos_ref, near_ref, far_ref, rs_ref, sc_ref, u_ref, basis_ref, coup_ref, trans_ref,
    coarse_ref, sum_a, sum_b, vx_ref, vo_ref, c0, c1, c2, c3, tile_ref, near_in, prev_ref,
    near_out, w_ref, msg_ref,
    list_ref, vw, cw, fc, acc_uw, acc_ww, acc_rw,
):
    per, rank, leaf = basis_ref.shape
    half = per // 2
    pos = pos_ref[0]
    load_halves(vw, vx_ref, vo_ref, pos % 2)
    load_coefficients(cw, (c0, c1, c2, c3))
    coarse_rows(coarse_ref, (sum_a, sum_b), fc)
    n = list_entries(near_ref, list_ref, pos, half, False)

    def trip(i, carry):
        for u in range(UNROLL):
            entry, leaf_at, _, place = near_entry(near_ref, list_ref, i * UNROLL + u, pos, half, False)
            near_out[leaf_at] += dot(vw[place], tile_ref[entry], 1, 0)
        return carry

    lax.fori_loop(0, (n + UNROLL - 1) // UNROLL, trip, 0)
    for acc in (acc_uw, acc_ww, acc_rw):
        acc[...] = jnp.zeros_like(acc)

    def one(l):
        far = far_columns(l, pos, far_ref, cw, coup_ref, trans_ref, fc, basis_ref)
        image = columns_of(u_ref, l, leaf)
        second = RIDGE_TERM * (image * columns_of(sc_ref, l, leaf)) + (near_out[l] + far)
        w_ref[:, pl.ds(pl.multiple_of(l * leaf, leaf), leaf)] = second
        acc_uw[...] += image * second
        acc_ww[...] += second * second
        acc_rw[...] += columns_of(rs_ref, l, leaf) * second

    leaf_loop(per, UNROLL, one)
    lane = lax.broadcasted_iota(jnp.int32, msg_ref.shape, 1)
    out = prev_ref[...]
    for at, acc in enumerate((acc_uw, acc_ww, acc_rw)):
        out = jnp.where(lane == 2 + at, jnp.sum(acc[...], axis=1, keepdims=True), out)
    msg_ref[...] = out


def call(kernel, name, in_specs, out_shape, scratch, args, aliases=None, flops=0):
    return pl.pallas_call(
        kernel,
        in_specs=in_specs,
        out_specs=[WHOLE] * len(out_shape),
        out_shape=out_shape,
        scratch_shapes=scratch,
        input_output_aliases=aliases or {},
        compiler_params=pltpu.CompilerParams(vmem_limit_bytes=VMEM_LIMIT),
        cost_estimate=pl.CostEstimate(flops=flops, bytes_accessed=0, transcendentals=0),
        name=name,
    )(*args)


def two_clusters():
    return CDEV == 8 and lax.axis_size("leaf") == 2 * CDEV


def cluster_addends(pair_sum):
    count = lax.axis_size("leaf")
    if two_clusters():
        first = involution(pair_sum, lambda i: i ^ (8 + 2 * (i % 2)))
        second = involution(pair_sum, lambda i: i ^ (12 + 2 * (i % 2)))
        return first[None], second[None]
    mask = 2
    while mask < CDEV:
        pair_sum = pair_sum + involution(pair_sum, lambda i: i ^ mask)
        mask *= 2
    sums = pair_sum[None]
    while mask < count:
        sums = jnp.concatenate([sums, involution(sums, lambda i: i ^ mask)], axis=0)
        mask *= 2
    return sums[1:], jnp.zeros_like(sums[1:])


def exchange(position, cp, part, v, meanwhile):
    per, columns, leaf = v.shape
    rows = cp.shape[0] - 3 * part.shape[0]
    got = sibling(cp)
    pair, pair_sum = call(
        pair_kernel, "pair", [SCALAR] + [WHOLE] * 3,
        [pltpu.VMEM((2, rows, cp.shape[1]), BF16), pltpu.VMEM(part.shape, F32)],
        [], (position, cp, got, part),
    )
    near_pair = beside(pair)
    far_pair = two_chips(pair)
    first, second = cluster_addends(pair_sum)
    near = meanwhile()
    half_shape = pltpu.VMEM((per // 2, columns, leaf), BF16)
    mx, mo, mine = call(
        send_kernel, "send", [SCALAR] + [WHOLE] * 3 + [ANYWHERE] * 3,
        [half_shape, half_shape, pltpu.VMEM(first.shape, F32)],
        [], (position, v, first, second, near_pair, far_pair, near),
    )
    other = sibling(mine) if two_clusters() else jnp.zeros_like(mine)
    coefs = (near_pair, far_pair, sibling(near_pair), sibling(far_pair))
    return sibling(mx), beside(mo), coefs, (mine, other), near


def body(
    right_side, scaling, embeddings, near_leaves, far_leaves, leaf_basis, leaf_coupling,
    transfer, coarse_coupling,
):
    columns, local_points = right_side.shape
    per, rank, leaf = leaf_basis.shape
    features = embeddings.shape[0]
    slots = near_leaves.shape[1] - 1
    far_count = far_leaves.shape[1]
    half = per // 2
    margin = half * leaf
    size = rank // 2
    count = lax.axis_size("leaf")
    pos = lax.axis_index("leaf")
    position = pos.reshape(1).astype(jnp.int32)
    cluster = pos // CDEV
    coarse_count = count // CDEV

    margin_shape = pltpu.VMEM((features, margin), F32)
    ex, eo = call(
        margins_kernel, "margins", [SCALAR, ANYWHERE], [margin_shape] * 2,
        [pltpu.SemaphoreType.DMA((2,))], (position, embeddings),
    )
    e_sibling = sibling(ex)
    e_beside = beside(eo)

    scale_row = scaling.reshape(1, local_points)
    trans = transfer.reshape(per, rank, rank)
    (coup,) = call(
        relayout_kernel, "relayout", [WHOLE],
        [pltpu.VMEM((per, 2 * rank, far_count * size), BF16)],
        [pltpu.VMEM((far_count * rank * rank // 128, 128), F32), pltpu.VMEM((2, far_count // 4, rank, 128), F32)],
        (leaf_coupling,),
    )
    row = lax.dynamic_index_in_dim(coarse_coupling, cluster, 0, keepdims=False)
    order = jnp.arange(1, coarse_count, dtype=jnp.int32) ^ cluster
    coarse = jnp.take(row, order, axis=0).reshape(coarse_count - 1, rank, rank)

    leaf_shape = pltpu.VMEM((per, columns, leaf), BF16)
    cp_shape = pltpu.VMEM((per * size + 3 * size, 2 * columns), BF16)
    part_shape = pltpu.VMEM((size, 2 * columns), F32)
    self_shape = pltpu.VMEM((per, leaf, leaf), BF16)
    tile_shape = pltpu.VMEM((per * slots + 1, leaf, leaf), BF16)
    near_shape = pltpu.VMEM((per + 1, columns, leaf), F32)
    wide_shape = pltpu.VMEM((columns, local_points), F32)
    msg_shape = pltpu.VMEM((columns, 128), F32)
    coefs_shape = pltpu.VMEM((per * rank, columns), BF16)
    acc_shape = pltpu.VMEM((columns, leaf), F32)
    list_shape = pltpu.SMEM((per * slots + UNROLL,), jnp.int32)
    window = [
        pltpu.VMEM((2 * half, columns, leaf), BF16),
        pltpu.VMEM((8 * per, size, 2 * columns), BF16),
        pltpu.VMEM((rank, 3 * columns), BF16),
    ]

    v, cp, part = call(
        prep_kernel, "prep", [WHOLE] * 4 + [ANYWHERE] * 2, [leaf_shape, cp_shape, part_shape], [coefs_shape],
        (right_side, scale_row, leaf_basis, trans, ex, eo),
    )
    kept = []

    def self_tiles():
        tself, near = call(
            self_kernel, "self_tiles", [WHOLE] * 2, [self_shape, near_shape], [], (embeddings, v),
            flops=2 * per * leaf * leaf * 320,
        )
        kept.append(tself)
        return near

    vx, vo, coefs, sums, near = exchange(position, cp, part, v, self_tiles)
    (tself,) = kept
    tiles, near = call(
        own_kernel, "own_tiles", [SCALAR] * 2 + [WHOLE] * 3, [tile_shape, near_shape], [list_shape],
        (position, near_leaves, embeddings, v, near), aliases={4: 1}, flops=2 * per * leaf * leaf * 320,
    )
    tiles, _, image, q, cp, part, msg = call(
        rest_kernel, "first_product", [SCALAR] * 3 + [WHOLE] * 19,
        [tile_shape, near_shape, wide_shape, leaf_shape, cp_shape, part_shape, msg_shape],
        [list_shape] + window + [coefs_shape, acc_shape, acc_shape],
        (position, near_leaves, far_leaves, embeddings, e_sibling, e_beside, right_side, scale_row,
         leaf_basis, coup, trans, coarse, *sums, vx, vo, *coefs, tiles, near),
        aliases={20: 0, 21: 1}, flops=2 * per * leaf * leaf * 320,
    )

    def self_products():
        (near,) = call(
            self_again_kernel, "self_again", [WHOLE] * 2, [near_shape], [], (q, tself),
            flops=2 * per * leaf * leaf * 64,
        )
        return near

    vx, vo, coefs, sums, near = exchange(position, cp, part, q, self_products)
    (near,) = call(
        own_again_kernel, "own_again", [SCALAR] * 2 + [WHOLE] * 3, [near_shape], [list_shape],
        (position, near_leaves, q, tiles, near), aliases={4: 0}, flops=2 * per * leaf * leaf * 64,
    )
    _, second, msg = call(
        rest_again_kernel, "second_product", [SCALAR] * 3 + [WHOLE] * 18,
        [near_shape, wide_shape, msg_shape],
        [list_shape] + window + [acc_shape] * 3,
        (position, near_leaves, far_leaves, right_side, scale_row, image, leaf_basis, coup, trans,
         coarse, *sums, vx, vo, *coefs, tiles, near, msg),
        aliases={19: 0}, flops=2 * per * leaf * leaf * 64,
    )

    mask = 1
    while mask < count:
        msg = msg + involution(msg, lambda i: i ^ mask)
        mask *= 2
    uu, ru, uw, ww, rw = [msg[:, k : k + 1] for k in range(5)]
    step_one = ru / (uu + EPSILON)
    beta = -(uu - step_one * uw) / (uu + EPSILON)
    lead = 1.0 + beta
    curvature = lead * lead * uu - 2.0 * lead * step_one * uw + step_one * step_one * ww
    aligned = lead * (ru - step_one * uu) - step_one * (rw - step_one * uw)
    step_two = aligned / (curvature + EPSILON)
    first_weight = step_one + step_two * lead
    second_weight = step_two * step_one
    solution = scale_row * (first_weight * right_side - second_weight * image)
    residual = right_side - first_weight * image + second_weight * second
    return (solution, residual)


def solution(mesh):
    return jax.shard_map(
        body,
        mesh=mesh,
        in_specs=(
            P(None, ("groups", "leaf")),
            P(("groups", "leaf")),
            P(None, ("groups", "leaf")),
            P(("groups", "leaf"), None),
            P(("groups", "leaf"), None),
            P(("groups", "leaf"), None, None),
            P(("groups", "leaf"), None, None),
            P(("groups", "leaf"), None),
            P("groups", None, None),
        ),
        out_specs=(P(None, ("groups", "leaf")), P(None, ("groups", "leaf"))),
        check_vma=False,
    )
```

```python
import functools
import math

import jax
import jax.numpy as jnp
from jax import lax
from jax.experimental import pallas as pl
from jax.experimental.pallas import tpu as pltpu
from jax.sharding import PartitionSpec as P

FARDEV = 4
CDEV = 8
KERNEL_SCALE = 0.0625
RIDGE_TERM = 1.0
EPSILON = 1e-06
F32 = jnp.float32
BF16 = jnp.bfloat16
HALF_SCALE = math.sqrt(2.0 * KERNEL_SCALE * math.log2(math.e))
UNROLL = 4
FAR_UNROLL = 8
VMEM_LIMIT = 12 * 1024 * 1024
WIDE_LIMIT = 54 * 1024 * 1024
SELF_LIMIT = 28 * 1024 * 1024
WHOLE = pl.BlockSpec(memory_space=pltpu.VMEM)
ANYWHERE = pl.BlockSpec(memory_space=pl.ANY)
OUTSIDE = pl.BlockSpec(memory_space=pltpu.HBM)
SCALAR = pl.BlockSpec(memory_space=pltpu.SMEM)


def involution(value, partner):
    count = lax.axis_size("leaf")
    pairs = [(i, partner(i)) for i in range(count) if 0 <= partner(i) < count]
    return lax.ppermute(value, "leaf", pairs)


def sibling(value):
    return involution(value, lambda i: i ^ 1)


def beside(value):
    return involution(value, lambda i: i + 1 if i % 2 else i - 1)


def across(value):
    return involution(value, lambda i: i ^ 2)


def two_chips(value):
    return involution(value, lambda i: i + 3 if i % 2 else i - 3)


def dot(a, b, ca, cb):
    return lax.dot_general(a, b, (((ca,), (cb,)), ((), ())), preferred_element_type=F32)


def split3(value):
    high = value.astype(BF16)
    rest = value - high.astype(F32)
    mid = rest.astype(BF16)
    low = (rest - mid.astype(F32)).astype(BF16)
    return high, mid, low


def point_pieces(points):
    scaled = points * HALF_SCALE
    high, mid, low = split3(scaled)
    square = 0.5 * jnp.sum(scaled * scaled, axis=0, keepdims=True)
    s_high, s_mid, s_low = split3(square)
    return high, mid, low, s_high.astype(F32), s_mid.astype(F32), s_low.astype(F32)


def norm_rows(first, second, third, width, swap, sign):
    row = lax.broadcasted_iota(jnp.int32, (16, width), 0)
    base = 3 if swap else 0
    ones = 0 if swap else 3
    out = jnp.where((row >= ones) & (row < ones + 3), sign, 0.0)
    for at, piece in enumerate((first, second, third)):
        out = jnp.where(row == base + at, sign * piece, out)
    return out.astype(BF16)


def own_rows(points):
    high, mid, low, a, b, c = point_pieces(points)
    norms = norm_rows(a, b, c, points.shape[1], False, 1.0)
    return jnp.concatenate([high, mid, high, mid, low, high, norms], axis=0)


def other_rows(points):
    high, mid, low, a, b, c = point_pieces(points)
    norms = norm_rows(a, b, c, points.shape[1], True, -1.0)
    return jnp.concatenate([high, high, mid, mid, high, low, norms], axis=0)


def tile_of(other, own):
    return jnp.exp2(dot(other, own, 0, 0)).astype(BF16)


def pack_pair(block):
    half = block.shape[0] // 2
    return jnp.concatenate([block[:half], block[half:]], axis=1)


def lane_groups(value):
    total = value[:, :128]
    for at in range(128, value.shape[1], 128):
        total += value[:, at : at + 128]
    return total


def leaf_coefficients(basis, rounded):
    return dot(basis, rounded, 1, 1).astype(BF16)


def share_of(trans, coefs):
    count, rank, _ = trans.shape
    return dot(trans.reshape(count * rank, rank), coefs, 0, 0)


def columns_of(ref, at, width):
    return ref[:, pl.ds(pl.multiple_of(at * width, width), width)]


def leaf_loop(count, unroll, fn):
    def trip(i, carry):
        for u in range(unroll):
            fn(i * unroll + u)
        return carry

    lax.fori_loop(0, count // unroll, trip, 0)


def store_share(total, part_ref, cp_ref):
    packed = pack_pair(total)
    part_ref[...] = packed
    size = packed.shape[0]
    rows = cp_ref.shape[0] - 3 * size
    for at, piece in enumerate(split3(packed)):
        cp_ref[rows + at * size : rows + (at + 1) * size] = piece


def store_square(flat, target):
    pairs = flat.shape[0]
    target[pl.ds(0, pairs, stride=2)] = flat
    target[pl.ds(1, pairs, stride=2)] = pltpu.roll(flat, 64, 1)


def relayout_kernel(pos_ref, coup_ref, coarse_ref, wait_ref, out_ref, coarse_out, by_slot, by_row, flat, square):
    per, slots, entries = coup_ref.shape
    rank = out_ref.shape[1] // 2
    quarter = rank // 2
    pairs = entries // 128
    lane = lax.broadcasted_iota(jnp.int32, (pairs, 128), 1) // quarter

    def one(l, carry):
        wide = coup_ref[l].astype(F32)
        for k in range(pairs):
            by_slot[k * slots : (k + 1) * slots] = wide[:, k * 128 : (k + 1) * 128]
        rows = [by_slot[pl.ds(s, pairs, stride=slots)] for s in range(slots)]
        turned = [[rows[s] if t == 0 else pltpu.roll(rows[s], t * quarter, 1) for t in range(4)] for s in range(slots)]
        for half in range(2):
            for parity in range(2):
                chunk = 2 * parity + half
                for group in range(slots // 4):
                    out = turned[4 * group][(0 - chunk) % 4]
                    for r in range(1, 4):
                        out = jnp.where(lane == r, turned[4 * group + r][(r - chunk) % 4], out)
                    by_row[half, group, pl.ds(parity, pairs, stride=2)] = out
        for half in range(2):
            for group in range(slots // 4):
                out_ref[l, half * rank : (half + 1) * rank, group * 128 : (group + 1) * 128] = by_row[half, group].astype(BF16)
        return carry

    lax.fori_loop(0, per, one, 0)
    cluster = pos_ref[0] // CDEV
    wide = coarse_ref[cluster].astype(F32)
    number = lax.broadcasted_iota(jnp.int32, wide.shape, 0)
    for at in range(coarse_out.shape[0]):
        row = jnp.sum(jnp.where(number == (cluster ^ (at + 1)), wide, 0.0), axis=0, keepdims=True)
        for k in range(pairs):
            flat[k : k + 1] = row[:, k * 128 : (k + 1) * 128]
        store_square(flat[...], square)
        coarse_out[at] = square[:, :rank].astype(BF16)


def margins_kernel(pos_ref, e_ref, ex_ref, eo_ref, sems):
    odd = pos_ref[0] % 2
    width = ex_ref.shape[1]
    first = pltpu.make_async_copy(
        e_ref.at[:, pl.ds(pl.multiple_of((1 - odd) * width, width), width)], ex_ref, sems.at[0]
    )
    second = pltpu.make_async_copy(
        e_ref.at[:, pl.ds(pl.multiple_of(odd * width, width), width)], eo_ref, sems.at[1]
    )
    first.start()
    second.start()
    first.wait()
    second.wait()


def prep_kernel(
    pos_ref, rs_hbm, sc_hbm, basis_hbm, transfer_hbm, v_ref, cp_ref, part_ref, trans_ref, mx_ref, mo_ref,
    rs_ref, sc_ref, basis_ref, transfer_ref, coefs, by_leaf, squares, sems,
):
    per, rank, leaf = basis_ref.shape
    copies = [
        pltpu.make_async_copy(source, target, sems.at[at])
        for at, (source, target) in enumerate(
            ((transfer_hbm, transfer_ref), (sc_hbm, sc_ref), (rs_hbm, rs_ref), (basis_hbm, basis_ref))
        )
    ]
    for copy in copies:
        copy.start()
    copies[0].wait()
    size = rank // 2
    wide = transfer_ref[...].astype(F32)
    for k in range(rank * rank // 128):
        by_leaf[k * per : (k + 1) * per] = wide[:, k * 128 : (k + 1) * 128]
    for at in range(per):
        store_square(by_leaf[pl.ds(at, rank * rank // 128, stride=per)], squares.at[at])
    trans_ref[...] = squares[:, :, :rank].astype(BF16)
    for copy in copies[1:]:
        copy.wait()

    def one(at):
        rounded = (columns_of(rs_ref, at, leaf) * columns_of(sc_ref, at, leaf)).astype(BF16)
        v_ref[at] = rounded
        coef = leaf_coefficients(basis_ref[at], rounded)
        coefs[pl.ds(pl.multiple_of(at * rank, rank), rank)] = coef
        cp_ref[pl.ds(pl.multiple_of(at * size, size), size)] = pack_pair(coef)

    leaf_loop(per, UNROLL, one)
    store_share(share_of(trans_ref[...], coefs[...]), part_ref, cp_ref)
    odd = pos_ref[0] % 2
    mx_ref[...] = v_ref[pl.ds(per // 2 * (1 - odd), per // 2)]
    mo_ref[...] = v_ref[pl.ds(per // 2 * odd, per // 2)]


def quad_kernel(pos_ref, own_ref, sib_ref, across_ref, both_ref, part_ref, *rest):
    quad_ref, sum_ref = rest[-2:]
    place = pos_ref[0] % 4
    rows = quad_ref.shape[1]
    size = part_ref.shape[0]
    quad_ref[place] = own_ref[:rows]
    total = part_ref[...]
    for flip, ref in ((1, sib_ref), (2, across_ref), (3, both_ref)):
        quad_ref[place ^ flip] = ref[:rows]
        for at in range(3):
            total += ref[rows + at * size : rows + (at + 1) * size].astype(F32)
    sum_ref[...] = total[None]


def list_entries(near_ref, list_ref, pos, half, want_own, first, rows):
    slots = near_ref.shape[0] - 1
    base = pos * 2 * half - half

    def put(at, n):
        entry = first * slots + at
        m = near_ref[1 + entry % slots, entry // slots] - base
        own = (m >= half) & (m < 3 * half)
        list_ref[n] = entry
        return n + jnp.where(own == want_own, 1, 0)

    n = lax.fori_loop(0, rows * slots, put, 0)
    for u in range(UNROLL):
        list_ref[n + u] = near_ref.shape[1] * slots
    return n


def near_entry(near_ref, list_ref, at, pos, half, own):
    slots = near_ref.shape[0] - 1
    per = near_ref.shape[1]
    entry = list_ref[at]
    leaf_at = entry // slots
    row = jnp.minimum(leaf_at, per - 1)
    m = near_ref[1 + entry % slots, row] - (pos * 2 * half - half)
    if own:
        place = jnp.clip(m - half, 0, per - 1)
    else:
        place = jnp.clip(jnp.where(m < half, m, m - 2 * half), 0, 2 * half - 1)
    return entry, leaf_at, row, place


def load_halves(target, from_sibling, from_beside, odd):
    half = from_sibling.shape[0]
    target[pl.ds(half * (1 - odd), half)] = from_sibling[...]
    target[pl.ds(half * odd, half)] = from_beside[...]


def self_kernel(e_ref, v_ref, cp_in, self_ref, near_out, cp_out, buffer, sems):
    per, _, leaf = v_ref.shape

    def copy_out(slot, at):
        return pltpu.make_async_copy(buffer.at[slot], self_ref.at[at], sems.at[slot])

    def trip(i, carry):
        for u in range(UNROLL):
            at = i * UNROLL + u
            slot = (i % 2) * UNROLL + u

            @pl.when(i >= 2)
            def _():
                copy_out(slot, at - 2 * UNROLL).wait()

        for u in range(UNROLL):
            at = i * UNROLL + u
            points = columns_of(e_ref, at, leaf)
            tile = tile_of(other_rows(points), own_rows(points))
            buffer[(i % 2) * UNROLL + u] = tile
            near_out[at] = dot(v_ref[at], tile, 1, 0)
        for u in range(UNROLL):
            copy_out((i % 2) * UNROLL + u, i * UNROLL + u).start()
        return carry

    trips = per // UNROLL
    lax.fori_loop(0, trips, trip, 0)
    for i in range(max(trips - 2, 0), trips):
        for u in range(UNROLL):
            copy_out((i % 2) * UNROLL + u, i * UNROLL + u).wait()


def own_kernel(pos_ref, near_ref, e_ref, v_ref, near_in, *rest):
    tile_ref, near_out, list_ref = rest[-3:]
    per, _, leaf = v_ref.shape
    half = per // 2
    pos = pos_ref[0]
    n = list_entries(near_ref, list_ref, pos, half, True, 0, 2 * half)

    def trip(i, carry):
        for u in range(UNROLL):
            entry, leaf_at, row, place = near_entry(near_ref, list_ref, i * UNROLL + u, pos, half, True)
            tile = tile_of(other_rows(columns_of(e_ref, place, leaf)), own_rows(columns_of(e_ref, row, leaf)))
            tile_ref[entry] = tile
            near_out[leaf_at] += dot(v_ref[place], tile, 1, 0)
        return carry

    lax.fori_loop(0, (n + UNROLL - 1) // UNROLL, trip, 0)


def own_again_kernel(pos_ref, near_ref, v_ref, tile_ref, self_hbm, near_out, list_ref, self_ref, sems):
    per = v_ref.shape[0]
    half = per // 2
    pos = pos_ref[0]
    copies = [
        pltpu.make_async_copy(self_hbm.at[pl.ds(at, UNROLL)], self_ref.at[pl.ds(at, UNROLL)], sems.at[at // UNROLL])
        for at in range(0, per, UNROLL)
    ]
    for copy in copies:
        copy.start()
    near_out[...] = jnp.zeros_like(near_out)
    n = list_entries(near_ref, list_ref, pos, half, True, 0, 2 * half)

    def trip(i, carry):
        for u in range(UNROLL):
            entry, leaf_at, _, place = near_entry(near_ref, list_ref, i * UNROLL + u, pos, half, True)
            near_out[leaf_at] += dot(v_ref[place], tile_ref[entry], 1, 0)
        return carry

    lax.fori_loop(0, (n + UNROLL - 1) // UNROLL, trip, 0)
    for i, copy in enumerate(copies):
        copy.wait()
        for u in range(UNROLL):
            at = i * UNROLL + u
            near_out[at] += dot(v_ref[at], self_ref[at], 1, 0)


def load_coefficients(cw, sources):
    devices, rows, _ = sources[0].shape
    per = rows // cw.shape[1]
    for slot, source in enumerate(sources):
        for device in range(devices):
            for at in range(per):
                cw[(slot * devices + device) * per + at] = source[device, at * cw.shape[1] : (at + 1) * cw.shape[1]]


def coarse_rows(coarse_ref, sum_refs, fc):
    rank = coarse_ref.shape[1]
    acc = jnp.zeros((rank, rank), F32)
    for at in range(coarse_ref.shape[0]):
        packed = sum_refs[0][at]
        for ref in sum_refs[1:]:
            packed += ref[at]
        total = jnp.concatenate([packed[:, :rank], packed[:, rank:]], axis=0)
        for piece in split3(total):
            acc += dot(coarse_ref[at], piece, 1, 0)
    fc[...] = jnp.concatenate(split3(acc), axis=1)


def far_sum(l, pos, far_ref, cw, coup_ref, moved, basis_ref):
    per, rank, _ = basis_ref.shape
    odd = pos % 2
    picks = []
    for s in range(far_ref.shape[0]):
        leaf_id = far_ref[s, l]
        device = leaf_id // per
        gap = device // 4 - pos // 4
        slot = jnp.where(gap == 0, 0, jnp.where((gap < 0) == (odd == 0), 1, 2))
        picks.append(cw[(slot * 4 + device % 4) * per + leaf_id % per])
    wide = dot(coup_ref[l], jnp.concatenate(picks, axis=0), 1, 0)
    combined = wide[:rank, :rank] + wide[rank:, rank:] + moved
    return dot(combined.astype(BF16), basis_ref[l], 0, 0)


def store_moved(trans, fc, mv):
    count, rank, _ = trans.shape
    wide = dot(trans.reshape(count * rank, rank), fc[...], 1, 0)
    mv[...] = wide[:, :rank] + wide[:, rank : 2 * rank] + wide[:, 2 * rank :]


def foreign_kernel(
    pos_ref, near_ref, e_ref, ex_ref, eo_ref, vx_ref, vo_ref, tile_in, near_in, tile_ref, near_out, list_ref, vw,
):
    half, _, leaf = vx_ref.shape
    pos = pos_ref[0]
    odd = pos % 2
    load_halves(vw, vx_ref, vo_ref, odd)
    n = list_entries(near_ref, list_ref, pos, half, False, 0, 2 * half)

    def trip(i, carry):
        for u in range(UNROLL):
            entry, leaf_at, row, place = near_entry(near_ref, list_ref, i * UNROLL + u, pos, half, False)
            beneath = place < half
            from_x = beneath == (odd == 1)
            within = jnp.where(beneath, place, place - half)
            points = jnp.where(from_x, columns_of(ex_ref, within, leaf), columns_of(eo_ref, within, leaf))
            tile = tile_of(other_rows(points), own_rows(columns_of(e_ref, row, leaf)))
            tile_ref[entry] = tile
            near_out[leaf_at] += dot(vw[place], tile, 1, 0)
        return carry

    lax.fori_loop(0, (n + UNROLL - 1) // UNROLL, trip, 0)


def far_first_kernel(
    last, pos_ref, far_ref, rs_ref, sc_ref, basis_ref, coup_ref, trans_ref, near_ref, *rest,
):
    per, rank, leaf = basis_ref.shape
    half = per // 2
    size = rank // 2
    pos = pos_ref[0]
    odd = pos % 2
    first = half * ((1 - odd) if last else odd)
    if last:
        cw, mv, u_in, q_before, cp_before, share_before, msg_before = rest[:7]
        u_ref, mx_ref, q_ref, cp_ref, part_ref, msg_ref, coefs, acc_uu, acc_ru = rest[7:]
    else:
        coarse_ref, sum_a, sum_b, c0, c1, c2 = rest[:6]
        cw, mv, u_ref, mx_ref, cp_ref, share_ref, msg_ref, fc, coefs, acc_uu, acc_ru = rest[6:]
        load_coefficients(cw, (c0, c1, c2))
        coarse_rows(coarse_ref, (sum_a, sum_b), fc)
        store_moved(trans_ref[...], fc, mv)
    acc_uu[...] = jnp.zeros_like(acc_uu)
    acc_ru[...] = jnp.zeros_like(acc_ru)
    cp_first = first * size if last else 0

    def one(j):
        l = first + j
        far = far_sum(l, pos, far_ref, cw, coup_ref, mv[pl.ds(pl.multiple_of(l * rank, rank), rank)], basis_ref)
        right = columns_of(rs_ref, l, leaf)
        scale = columns_of(sc_ref, l, leaf)
        image = RIDGE_TERM * (right * scale) + (near_ref[l] + far)
        u_ref[:, pl.ds(pl.multiple_of(l * leaf, leaf), leaf)] = image
        acc_uu[...] += lane_groups(image * image)
        acc_ru[...] += lane_groups(right * image)
        rounded = (image * scale).astype(BF16)
        mx_ref[j] = rounded
        coef = leaf_coefficients(basis_ref[l], rounded)
        coefs[pl.ds(pl.multiple_of(j * rank, rank), rank)] = coef
        cp_ref[pl.ds(pl.multiple_of(cp_first + j * size, size), size)] = pack_pair(coef)

    leaf_loop(half, FAR_UNROLL, one)
    share = share_of(trans_ref[pl.ds(first, half)], coefs[...])
    lane = lax.broadcasted_iota(jnp.int32, msg_ref.shape, 1)
    out = jnp.where(lane == 0, jnp.sum(acc_uu[...], axis=1, keepdims=True), 0.0)
    out = jnp.where(lane == 1, jnp.sum(acc_ru[...], axis=1, keepdims=True), out)
    if last:
        other = half - first
        cp_ref[pl.ds(pl.multiple_of(other * size, size), half * size)] = cp_before[...]
        q_ref[pl.ds(other, half)] = q_before[...]
        q_ref[pl.ds(first, half)] = mx_ref[...]
        store_share(share + share_before[...], part_ref, cp_ref)
        msg_ref[...] = out + msg_before[...]
    else:
        share_ref[...] = share
        msg_ref[...] = out


def near_again_kernel(pos_ref, near_ref, vx_ref, vo_ref, tile_ref, near_in, near_out, list_ref, vw):
    half = vx_ref.shape[0]
    pos = pos_ref[0]
    load_halves(vw, vx_ref, vo_ref, pos % 2)
    n = list_entries(near_ref, list_ref, pos, half, False, 0, 2 * half)

    def trip(i, carry):
        for u in range(UNROLL):
            entry, leaf_at, _, place = near_entry(near_ref, list_ref, i * UNROLL + u, pos, half, False)
            near_out[leaf_at] += dot(vw[place], tile_ref[entry], 1, 0)
        return carry

    lax.fori_loop(0, (n + UNROLL - 1) // UNROLL, trip, 0)


def far_again_kernel(
    pos_ref, far_ref, rs_ref, sc_ref, u_ref, basis_ref, coup_ref, trans_ref,
    coarse_ref, sum_a, sum_b, c0, c1, c2, near_ref, prev_ref, w_ref, msg_ref,
    cw, fc, mv, acc_uw, acc_ww, acc_rw,
):
    per, rank, leaf = basis_ref.shape
    pos = pos_ref[0]
    load_coefficients(cw, (c0, c1, c2))
    coarse_rows(coarse_ref, (sum_a, sum_b), fc)
    store_moved(trans_ref[...], fc, mv)
    for acc in (acc_uw, acc_ww, acc_rw):
        acc[...] = jnp.zeros_like(acc)

    def one(l):
        far = far_sum(l, pos, far_ref, cw, coup_ref, mv[pl.ds(pl.multiple_of(l * rank, rank), rank)], basis_ref)
        image = columns_of(u_ref, l, leaf)
        second = RIDGE_TERM * (image * columns_of(sc_ref, l, leaf)) + (near_ref[l] + far)
        w_ref[:, pl.ds(pl.multiple_of(l * leaf, leaf), leaf)] = second
        acc_uw[...] += lane_groups(image * second)
        acc_ww[...] += lane_groups(second * second)
        acc_rw[...] += lane_groups(columns_of(rs_ref, l, leaf) * second)

    leaf_loop(per, FAR_UNROLL, one)
    lane = lax.broadcasted_iota(jnp.int32, msg_ref.shape, 1)
    out = prev_ref[...]
    for at, acc in enumerate((acc_uw, acc_ww, acc_rw)):
        out = jnp.where(lane == 2 + at, jnp.sum(acc[...], axis=1, keepdims=True), out)
    msg_ref[...] = out


def call(kernel, name, in_specs, out_shape, scratch, args, aliases=None, flops=0, out_specs=None, limit=VMEM_LIMIT):
    return pl.pallas_call(
        kernel,
        in_specs=in_specs,
        out_specs=out_specs or [WHOLE] * len(out_shape),
        out_shape=out_shape,
        scratch_shapes=scratch,
        input_output_aliases=aliases or {},
        compiler_params=pltpu.CompilerParams(vmem_limit_bytes=limit),
        cost_estimate=pl.CostEstimate(flops=flops, bytes_accessed=0, transcendentals=0),
        name=name,
    )(*args)


def two_clusters():
    return CDEV == 8 and lax.axis_size("leaf") == 2 * CDEV


def other_clusters(plane_sum):
    count = lax.axis_size("leaf")
    if two_clusters():
        return involution(plane_sum, lambda i: i ^ (12 if i % 2 else 8))
    mask = 4
    while mask < CDEV:
        plane_sum = plane_sum + involution(plane_sum, lambda i: i ^ mask)
        mask *= 2
    sums = plane_sum
    while mask < count:
        sums = jnp.concatenate([sums, involution(sums, lambda i: i ^ mask)], axis=0)
        mask *= 2
    return sums[1:]


def pass_kernel(*refs):
    pass


def after(values, *before):
    return call(
        pass_kernel, "after", [WHOLE] * len(values) + [ANYWHERE] * len(before),
        [pltpu.VMEM(value.shape, value.dtype) for value in values], [], (*values, *before),
        aliases={at: at for at in range(len(values))},
    )


def first_messages(cp):
    return sibling(cp), across(cp)


def second_messages(position, cp, got, part, *before):
    rows = cp.shape[0] - 3 * part.shape[0]
    got = (*got, sibling(got[1]))
    quad, plane_sum = call(
        quad_kernel, "quad", [SCALAR] + [WHOLE] * 5 + [ANYWHERE] * len(before),
        [pltpu.VMEM((4, rows, cp.shape[1]), BF16), pltpu.VMEM((1,) + part.shape, F32)],
        [], (position, cp, *got, part, *before),
    )
    return quad, two_chips(quad), other_clusters(plane_sum)


def last_messages(quad, mine):
    other = sibling(mine) if two_clusters() else jnp.zeros_like(mine)
    return (quad, sibling(quad)), (mine, other)


def body(
    right_side, scaling, embeddings, near_leaves, far_leaves, leaf_basis, leaf_coupling,
    transfer, coarse_coupling,
):
    columns, local_points = right_side.shape
    per, rank, leaf = leaf_basis.shape
    features = embeddings.shape[0]
    slots = near_leaves.shape[1] - 1
    far_count = far_leaves.shape[1]
    half = per // 2
    margin = half * leaf
    size = rank // 2
    count = lax.axis_size("leaf")
    pos = lax.axis_index("leaf")
    position = pos.reshape(1).astype(jnp.int32)
    near_rows = near_leaves.T
    far_rows = far_leaves.T
    coarse_count = count // CDEV

    margin_shape = pltpu.VMEM((features, margin), F32)
    ex, eo = call(
        margins_kernel, "margins", [SCALAR, ANYWHERE], [margin_shape] * 2,
        [pltpu.SemaphoreType.DMA((2,))], (position, embeddings), limit=WIDE_LIMIT,
    )
    e_sibling = sibling(ex)
    e_beside = beside(eo)

    scale_row = scaling.reshape(1, local_points)
    leaf_shape = pltpu.VMEM((per, columns, leaf), BF16)
    cp_shape = pltpu.VMEM((per * size + 3 * size, 2 * columns), BF16)
    part_shape = pltpu.VMEM((size, 2 * columns), F32)
    self_shape = pltpu.HBM((4 * per, leaf, leaf), BF16)
    trans_shape = pltpu.VMEM((per, rank, rank), BF16)
    half_shape = pltpu.VMEM((half, columns, leaf), BF16)
    share_shape = pltpu.VMEM((rank, columns), F32)
    cp_half_shape = pltpu.VMEM((half * size, 2 * columns), BF16)
    half_coefs_shape = pltpu.VMEM((half * rank, columns), BF16)
    moved_shape = pltpu.VMEM((per * rank, columns), F32)
    tile_shape = pltpu.VMEM((per * slots + 1, leaf, leaf), BF16)
    near_shape = pltpu.VMEM((per + 1, columns, leaf), F32)
    wide_shape = pltpu.VMEM((columns, local_points), F32)
    msg_shape = pltpu.VMEM((columns, 128), F32)
    coefs_shape = pltpu.VMEM((per * rank, columns), BF16)
    acc_shape = pltpu.VMEM((columns, 128), F32)
    list_shape = pltpu.SMEM((per * slots + UNROLL,), jnp.int32)
    window = [
        pltpu.VMEM((2 * half, columns, leaf), BF16),
        pltpu.VMEM((12 * per, size, 2 * columns), BF16),
        pltpu.VMEM((rank, 3 * columns), BF16),
    ]

    v, cp, part, trans, mx, mo = call(
        prep_kernel, "prep", [SCALAR] + [OUTSIDE] * 4,
        [leaf_shape, cp_shape, part_shape, trans_shape, half_shape, half_shape],
        [pltpu.VMEM(right_side.shape, F32), pltpu.VMEM(scale_row.shape, F32), pltpu.VMEM(leaf_basis.shape, BF16),
         pltpu.VMEM(transfer.shape, BF16), coefs_shape, pltpu.VMEM((per * rank * rank // 128, 128), F32), pltpu.VMEM((per, rank, 128), F32), pltpu.SemaphoreType.DMA((4,))],
        (position, right_side, scale_row, leaf_basis, transfer), limit=WIDE_LIMIT,
    )
    tself, near, cp = call(
        self_kernel, "self_tiles", [WHOLE] * 3, [self_shape, near_shape, cp_shape],
        [pltpu.VMEM((2 * UNROLL, leaf, leaf), BF16), pltpu.SemaphoreType.DMA((2 * UNROLL,))],
        (embeddings, v, cp), out_specs=[OUTSIDE, WHOLE, WHOLE], aliases={2: 2},
    )
    got = first_messages(cp)
    vo = beside(mo)
    coup, coarse = call(
        relayout_kernel, "relayout", [SCALAR] + [WHOLE] * 2 + [ANYWHERE],
        [pltpu.VMEM((per, 2 * rank, far_count * size), BF16), pltpu.VMEM((coarse_count - 1, rank, rank), BF16)],
        [
            pltpu.VMEM((far_count * rank * rank // 128, 128), F32),
            pltpu.VMEM((2, far_count // 4, rank, 128), F32),
            pltpu.VMEM((size, 128), F32), pltpu.VMEM((rank, 128), F32),
        ],
        (position, leaf_coupling, coarse_coupling, cp),
    )
    tiles, near = call(
        own_kernel, "own_tiles", [SCALAR] * 2 + [WHOLE] * 3 + [ANYWHERE] * 2, [tile_shape, near_shape], [list_shape],
        (position, near_rows, embeddings, v, near, coup, e_beside), aliases={4: 1}, flops=2 * per * leaf * leaf * 320,
    )
    got = (got[0], *after(got[1:], near))
    quad, far_quad, mine = second_messages(position, cp, got, part, vo)
    vx = sibling(mx)
    tiles, near = call(
        foreign_kernel, "foreign_tiles", [SCALAR] * 2 + [WHOLE] * 7, [tile_shape, near_shape],
        [list_shape, window[0]],
        (position, near_rows, embeddings, e_sibling, e_beside, vx, vo, tiles, near),
        aliases={7: 0, 8: 1}, flops=2 * per * leaf * leaf * 320,
    )
    coefs, sums = last_messages(*after((far_quad, mine), near))
    common = (position, far_rows, right_side, scale_row, leaf_basis, coup, trans, near)
    cw, mv, image, mo, cp_half, share, msg = call(
        functools.partial(far_first_kernel, False), "far_half", [SCALAR] * 2 + [WHOLE] * 12,
        [window[1], moved_shape, wide_shape, half_shape, cp_half_shape, share_shape, msg_shape],
        [window[2], half_coefs_shape, acc_shape, acc_shape],
        (*common, coarse, *sums, quad, *coefs), flops=per * leaf * leaf * 32,
    )
    vo = beside(mo)
    image, mx, q, cp, part, msg = call(
        functools.partial(far_first_kernel, True), "other_half", [SCALAR] * 2 + [WHOLE] * 13,
        [wide_shape, half_shape, leaf_shape, cp_shape, part_shape, msg_shape],
        [half_coefs_shape, acc_shape, acc_shape],
        (*common, cw, mv, image, mo, cp_half, share, msg), aliases={10: 0}, flops=per * leaf * leaf * 32,
    )
    got = first_messages(cp)
    (near,) = call(
        own_again_kernel, "own_again", [SCALAR] * 2 + [WHOLE] * 2 + [OUTSIDE], [near_shape],
        [list_shape, pltpu.VMEM((per, leaf, leaf), BF16), pltpu.SemaphoreType.DMA((per // UNROLL,))],
        (position, near_rows, q, tiles, tself), flops=2 * per * leaf * leaf * 64,
    )
    got = (got[0], *after(got[1:], near))
    quad, far_quad, mine = second_messages(position, cp, got, part, vo)
    vx = sibling(mx)
    (near,) = call(
        near_again_kernel, "near_again", [SCALAR] * 2 + [WHOLE] * 4, [near_shape], [list_shape, window[0]],
        (position, near_rows, vx, vo, tiles, near), aliases={5: 0}, flops=2 * per * leaf * leaf * 64,
    )
    coefs, sums = last_messages(*after((far_quad, mine), near))
    second, msg = call(
        far_again_kernel, "far_again", [SCALAR] * 2 + [WHOLE] * 14, [wide_shape, msg_shape],
        window[1:] + [moved_shape] + [acc_shape] * 3,
        (position, far_rows, right_side, scale_row, image, leaf_basis, coup, trans,
         coarse, *sums, quad, *coefs, near, msg), flops=per * leaf * leaf * 64,
    )

    mask = 1
    while mask < count:
        msg = msg + involution(msg, lambda i: i ^ mask)
        mask *= 2
    uu, ru, uw, ww, rw = [msg[:, k : k + 1] for k in range(5)]
    step_one = ru / (uu + EPSILON)
    beta = -(uu - step_one * uw) / (uu + EPSILON)
    lead = 1.0 + beta
    curvature = lead * lead * uu - 2.0 * lead * step_one * uw + step_one * step_one * ww
    aligned = lead * (ru - step_one * uu) - step_one * (rw - step_one * uw)
    step_two = aligned / (curvature + EPSILON)
    first_weight = step_one + step_two * lead
    second_weight = step_two * step_one
    solution = scale_row * (first_weight * right_side - second_weight * image)
    residual = right_side - first_weight * image + second_weight * second
    return (solution, residual)


def solution(mesh):
    return jax.shard_map(
        body,
        mesh=mesh,
        in_specs=(
            P(None, ("groups", "leaf")),
            P(("groups", "leaf")),
            P(None, ("groups", "leaf")),
            P(("groups", "leaf"), None),
            P(("groups", "leaf"), None),
            P(("groups", "leaf"), None, None),
            P(("groups", "leaf"), None, None),
            P(("groups", "leaf"), None),
            P("groups", None, None),
        ),
        out_specs=(P(None, ("groups", "leaf")), P(None, ("groups", "leaf"))),
        check_vma=False,
    )
```

```python
import math

import jax
import jax.numpy as jnp
from jax import lax
from jax.experimental import pallas as pl
from jax.experimental.pallas import tpu as pltpu
from jax.sharding import PartitionSpec as P

FARDEV = 4
CDEV = 8
KERNEL_SCALE = 0.0625
RIDGE_TERM = 1.0
EPSILON = 1e-06
F32 = jnp.float32
BF16 = jnp.bfloat16
HALF_SCALE = math.sqrt(2.0 * KERNEL_SCALE * math.log2(math.e))
UNROLL = 4
FAR_UNROLL = 8
RELAY_UNROLL = 4
VMEM_LIMIT = 12 * 1024 * 1024
WIDE_LIMIT = 54 * 1024 * 1024
SELF_LIMIT = 28 * 1024 * 1024
WHOLE = pl.BlockSpec(memory_space=pltpu.VMEM)
ANYWHERE = pl.BlockSpec(memory_space=pl.ANY)
OUTSIDE = pl.BlockSpec(memory_space=pltpu.HBM)
SCALAR = pl.BlockSpec(memory_space=pltpu.SMEM)


def involution(value, partner):
    count = lax.axis_size("leaf")
    pairs = [(i, partner(i)) for i in range(count) if 0 <= partner(i) < count]
    return lax.ppermute(value, "leaf", pairs)


def sibling(value):
    return involution(value, lambda i: i ^ 1)


def beside(value):
    return involution(value, lambda i: i + 1 if i % 2 else i - 1)


def across(value):
    return involution(value, lambda i: i ^ 2)


def two_chips(value):
    return involution(value, lambda i: i + 3 if i % 2 else i - 3)


def dot(a, b, ca, cb):
    return lax.dot_general(a, b, (((ca,), (cb,)), ((), ())), preferred_element_type=F32)


def split3(value):
    high = value.astype(BF16)
    rest = value - high.astype(F32)
    mid = rest.astype(BF16)
    low = (rest - mid.astype(F32)).astype(BF16)
    return high, mid, low


def point_pieces(points):
    scaled = points * HALF_SCALE
    high, mid, low = split3(scaled)
    square = 0.5 * jnp.sum(scaled * scaled, axis=0, keepdims=True)
    s_high, s_mid, s_low = split3(square)
    return high, mid, low, s_high.astype(F32), s_mid.astype(F32), s_low.astype(F32)


def norm_rows(first, second, third, width, swap, sign):
    row = lax.broadcasted_iota(jnp.int32, (16, width), 0)
    base = 3 if swap else 0
    ones = 0 if swap else 3
    out = jnp.where((row >= ones) & (row < ones + 3), sign, 0.0)
    for at, piece in enumerate((first, second, third)):
        out = jnp.where(row == base + at, sign * piece, out)
    return out.astype(BF16)


def own_rows(points):
    high, mid, low, a, b, c = point_pieces(points)
    norms = norm_rows(a, b, c, points.shape[1], False, 1.0)
    return jnp.concatenate([high, mid, high, mid, low, high, norms], axis=0)


def other_rows(points):
    high, mid, low, a, b, c = point_pieces(points)
    norms = norm_rows(a, b, c, points.shape[1], True, -1.0)
    return jnp.concatenate([high, high, mid, mid, high, low, norms], axis=0)


def tile_of(other, own):
    return jnp.exp2(dot(other, own, 0, 0)).astype(BF16)


def pack_pair(block):
    half = block.shape[0] // 2
    return jnp.concatenate([block[:half], block[half:]], axis=1)


def lane_groups(value):
    total = value[:, :128]
    for at in range(128, value.shape[1], 128):
        total += value[:, at : at + 128]
    return total


def leaf_coefficients(basis, rounded):
    return dot(basis, rounded, 1, 1).astype(BF16)


def share_of(trans, coefs):
    count, rank, _ = trans.shape
    return dot(trans.reshape(count * rank, rank), coefs, 0, 0)


def columns_of(ref, at, width):
    return ref[:, pl.ds(pl.multiple_of(at * width, width), width)]


def leaf_loop(count, unroll, fn):
    def trip(i, carry):
        for u in range(unroll):
            fn(i * unroll + u)
        return carry

    lax.fori_loop(0, count // unroll, trip, 0)


def store_share(total, part_ref, cp_ref):
    packed = pack_pair(total)
    part_ref[...] = packed
    size = packed.shape[0]
    rows = cp_ref.shape[0] - 3 * size
    for at, piece in enumerate(split3(packed)):
        cp_ref[rows + at * size : rows + (at + 1) * size] = piece


def store_square(flat, target):
    pairs = flat.shape[0]
    target[pl.ds(0, pairs, stride=2)] = flat
    target[pl.ds(1, pairs, stride=2)] = pltpu.roll(flat, 64, 1)


def relayout_kernel(pos_ref, coup_ref, coarse_ref, wait_ref, out_ref, coarse_out, by_slots, by_rows, flat, square):
    per, slots, entries = coup_ref.shape
    rank = out_ref.shape[1] // 2
    quarter = rank // 2
    pairs = entries // 128
    lane = lax.broadcasted_iota(jnp.int32, (pairs, 128), 1) // quarter

    def one(l, by_slot, by_row):
        wide = coup_ref[l].astype(F32)
        for k in range(pairs):
            by_slot[k * slots : (k + 1) * slots] = wide[:, k * 128 : (k + 1) * 128]
        rows = [by_slot[pl.ds(s, pairs, stride=slots)] for s in range(slots)]
        turned = [[rows[s] if t == 0 else pltpu.roll(rows[s], t * quarter, 1) for t in range(4)] for s in range(slots)]
        for half in range(2):
            for parity in range(2):
                chunk = 2 * parity + half
                for group in range(slots // 4):
                    out = turned[4 * group][(0 - chunk) % 4]
                    for r in range(1, 4):
                        out = jnp.where(lane == r, turned[4 * group + r][(r - chunk) % 4], out)
                    by_row[half, group, pl.ds(parity, pairs, stride=2)] = out
        for half in range(2):
            for group in range(slots // 4):
                out_ref[l, half * rank : (half + 1) * rank, group * 128 : (group + 1) * 128] = by_row[half, group].astype(BF16)

    def trip(i, carry):
        for u in range(by_slots.shape[0]):
            one(i * by_slots.shape[0] + u, by_slots.at[u], by_rows.at[u])
        return carry

    lax.fori_loop(0, per // by_slots.shape[0], trip, 0)
    cluster = pos_ref[0] // CDEV
    wide = coarse_ref[cluster].astype(F32)
    number = lax.broadcasted_iota(jnp.int32, wide.shape, 0)
    for at in range(coarse_out.shape[0]):
        row = jnp.sum(jnp.where(number == (cluster ^ (at + 1)), wide, 0.0), axis=0, keepdims=True)
        for k in range(pairs):
            flat[k : k + 1] = row[:, k * 128 : (k + 1) * 128]
        store_square(flat[...], square)
        coarse_out[at] = square[:, :rank].astype(BF16)


def prep_kernel(
    pos_ref, rs_hbm, sc_hbm, basis_hbm, transfer_hbm, e_hbm, v_ref, cp_ref, part_ref, trans_ref, mx_ref, mo_ref,
    rs_ref, sc_ref, basis_ref, transfer_ref, e_ref, points, coefs, by_leaf, squares, sems,
):
    per, rank, leaf = basis_ref.shape
    columns, features = rs_ref.shape[0], e_ref.shape[0]
    size = rank // 2
    copies = [
        pltpu.make_async_copy(source, target, sems.at[at])
        for at, (source, target) in enumerate(
            ((transfer_hbm, transfer_ref), (sc_hbm, sc_ref), (rs_hbm, rs_ref), (basis_hbm, basis_ref), (e_hbm, e_ref))
        )
    ]
    for copy in copies:
        copy.start()
    copies[0].wait()
    wide = transfer_ref[...].astype(F32)
    for k in range(rank * rank // 128):
        by_leaf[k * per : (k + 1) * per] = wide[:, k * 128 : (k + 1) * 128]
    for at in range(per):
        store_square(by_leaf[pl.ds(at, rank * rank // 128, stride=per)], squares.at[at])
    trans_ref[...] = squares[:, :, :rank].astype(BF16)
    for copy in copies[1:]:
        copy.wait()

    def one(at):
        rounded = (columns_of(rs_ref, at, leaf) * columns_of(sc_ref, at, leaf)).astype(BF16)
        v_ref[at] = rounded
        here = columns_of(e_ref, at, leaf)
        high = here.astype(BF16)
        points[at, :features] = high
        points[at, features:] = (here - high.astype(F32)).astype(BF16)
        coef = leaf_coefficients(basis_ref[at], rounded)
        coefs[pl.ds(pl.multiple_of(at * rank, rank), rank)] = coef
        cp_ref[pl.ds(pl.multiple_of(at * size, size), size)] = pack_pair(coef)

    leaf_loop(per, UNROLL, one)
    store_share(share_of(trans_ref[...], coefs[...]), part_ref, cp_ref)
    odd = pos_ref[0] % 2
    half = per // 2
    for ref, first in ((mx_ref, half * (1 - odd)), (mo_ref, half * odd)):
        ref[:, :columns] = v_ref[pl.ds(first, half)]
        ref[:, columns:] = points[pl.ds(first, half)]


def quad_kernel(pos_ref, own_ref, sib_ref, across_ref, both_ref, part_ref, *rest):
    quad_ref, sum_ref = rest[-2:]
    place = pos_ref[0] % 4
    rows = quad_ref.shape[1]
    size = part_ref.shape[0]
    quad_ref[place] = own_ref[:rows]
    total = part_ref[...]
    for flip, ref in ((1, sib_ref), (2, across_ref), (3, both_ref)):
        quad_ref[place ^ flip] = ref[:rows]
        for at in range(3):
            total += ref[rows + at * size : rows + (at + 1) * size].astype(F32)
    sum_ref[...] = total[None]


def list_entries(near_ref, list_ref, pos, half, own_part):
    slots = near_ref.shape[0] - 1
    total = near_ref.shape[1] * slots
    base = pos * 2 * half - half

    def put(entry, carry):
        n, seen = carry
        m = near_ref[1 + entry % slots, entry // slots] - base
        own = (m >= half) & (m < 3 * half)
        early = own & (seen < 2 * half)
        list_ref[n] = entry
        return n + jnp.where(early == own_part, 1, 0), seen + jnp.where(own, 1, 0)

    n, _ = lax.fori_loop(0, total, put, (0, 0))
    for u in range(UNROLL):
        list_ref[n + u] = total
    return n


def near_entry(near_ref, list_ref, at, pos, half):
    slots = near_ref.shape[0] - 1
    entry = list_ref[at]
    leaf_at = entry // slots
    row = jnp.minimum(leaf_at, near_ref.shape[1] - 1)
    m = near_ref[1 + entry % slots, row] - (pos * 2 * half - half)
    return entry, leaf_at, row, jnp.clip(m, 0, 4 * half - 1)


def load_window(target, own, from_sibling, from_beside, odd):
    half = from_sibling.shape[0]
    rows = target.shape[1]
    target[pl.ds(half, 2 * half)] = own[...]
    target[pl.ds(3 * half * (1 - odd), half)] = from_sibling[:, :rows]
    target[pl.ds(3 * half * odd, half)] = from_beside[:, :rows]


def self_kernel(e_ref, v_ref, wait_ref, self_ref, near_out, buffer, sems):
    per, _, leaf = v_ref.shape

    def copy_out(slot, at):
        return pltpu.make_async_copy(buffer.at[slot], self_ref.at[at], sems.at[slot])

    def trip(i, carry):
        for u in range(UNROLL):
            at = i * UNROLL + u
            slot = (i % 2) * UNROLL + u

            @pl.when(i >= 2)
            def _():
                copy_out(slot, at - 2 * UNROLL).wait()

        for u in range(UNROLL):
            at = i * UNROLL + u
            points = columns_of(e_ref, at, leaf)
            tile = tile_of(other_rows(points), own_rows(points))
            buffer[(i % 2) * UNROLL + u] = tile
            near_out[at] = dot(v_ref[at], tile, 1, 0)
        for u in range(UNROLL):
            copy_out((i % 2) * UNROLL + u, i * UNROLL + u).start()
        return carry

    trips = per // UNROLL
    lax.fori_loop(0, trips, trip, 0)
    for i in range(max(trips - 2, 0), trips):
        for u in range(UNROLL):
            copy_out((i % 2) * UNROLL + u, i * UNROLL + u).wait()


def own_kernel(pos_ref, near_ref, e_ref, v_ref, near_in, *rest):
    tile_ref, near_out, list_ref = rest[-3:]
    per, _, leaf = v_ref.shape
    half = per // 2
    pos = pos_ref[0]
    n = list_entries(near_ref, list_ref, pos, half, True)

    def trip(i, carry):
        for u in range(UNROLL):
            entry, leaf_at, row, m = near_entry(near_ref, list_ref, i * UNROLL + u, pos, half)
            place = jnp.clip(m - half, 0, 2 * half - 1)
            tile = tile_of(other_rows(columns_of(e_ref, place, leaf)), own_rows(columns_of(e_ref, row, leaf)))
            tile_ref[entry] = tile
            near_out[leaf_at] += dot(v_ref[place], tile, 1, 0)
        return carry

    lax.fori_loop(0, (n + UNROLL - 1) // UNROLL, trip, 0)


def own_again_kernel(pos_ref, near_ref, v_ref, tile_ref, near_out, list_ref):
    half = v_ref.shape[0] // 2
    pos = pos_ref[0]
    near_out[...] = jnp.zeros_like(near_out)
    n = list_entries(near_ref, list_ref, pos, half, True)

    def trip(i, carry):
        for u in range(UNROLL):
            entry, leaf_at, _, m = near_entry(near_ref, list_ref, i * UNROLL + u, pos, half)
            place = jnp.clip(m - half, 0, 2 * half - 1)
            near_out[leaf_at] += dot(v_ref[place], tile_ref[entry], 1, 0)
        return carry

    lax.fori_loop(0, (n + UNROLL - 1) // UNROLL, trip, 0)


def self_again_kernel(v_ref, self_hbm, near_in, wait_ref, near_out, self_ref, sems):
    per = v_ref.shape[0]
    copies = [
        pltpu.make_async_copy(self_hbm.at[pl.ds(at, UNROLL)], self_ref.at[pl.ds(at, UNROLL)], sems.at[at // UNROLL])
        for at in range(0, per, UNROLL)
    ]
    for copy in copies:
        copy.start()
    for i, copy in enumerate(copies):
        copy.wait()
        for u in range(UNROLL):
            at = i * UNROLL + u
            near_out[at] += dot(v_ref[at], self_ref[at], 1, 0)


def load_coefficients(cw, sources):
    devices, rows, _ = sources[0].shape
    per = rows // cw.shape[1]
    for slot, source in enumerate(sources):
        for device in range(devices):
            for at in range(per):
                cw[(slot * devices + device) * per + at] = source[device, at * cw.shape[1] : (at + 1) * cw.shape[1]]


def coarse_rows(coarse_ref, sum_refs, fc):
    rank = coarse_ref.shape[1]
    acc = jnp.zeros((rank, rank), F32)
    for at in range(coarse_ref.shape[0]):
        packed = sum_refs[0][at]
        for ref in sum_refs[1:]:
            packed += ref[at]
        total = jnp.concatenate([packed[:, :rank], packed[:, rank:]], axis=0)
        for piece in split3(total):
            acc += dot(coarse_ref[at], piece, 1, 0)
    fc[...] = jnp.concatenate(split3(acc), axis=1)


def far_sum(l, pos, far_ref, cw, coup_ref, moved, basis_ref):
    per, rank, _ = basis_ref.shape
    odd = pos % 2
    picks = []
    for s in range(far_ref.shape[0]):
        leaf_id = far_ref[s, l]
        device = leaf_id // per
        gap = device // 4 - pos // 4
        slot = jnp.where(gap == 0, 0, jnp.where((gap < 0) == (odd == 0), 1, 2))
        picks.append(cw[(slot * 4 + device % 4) * per + leaf_id % per])
    wide = dot(coup_ref[l], jnp.concatenate(picks, axis=0), 1, 0)
    combined = wide[:rank, :rank] + wide[rank:, rank:] + moved
    return dot(combined.astype(BF16), basis_ref[l], 0, 0)


def store_moved(trans, fc, mv):
    count, rank, _ = trans.shape
    wide = dot(trans.reshape(count * rank, rank), fc[...], 1, 0)
    mv[...] = wide[:, :rank] + wide[:, rank : 2 * rank] + wide[:, 2 * rank :]


def foreign_kernel(
    pos_ref, near_ref, e_ref, v_ref, vx_ref, vo_ref, tile_in, near_in, tile_ref, near_out, list_ref, vw,
):
    half, _, leaf = vx_ref.shape
    _, columns, _ = v_ref.shape
    features = e_ref.shape[0]
    pos = pos_ref[0]
    odd = pos % 2
    load_window(vw, v_ref, vx_ref, vo_ref, odd)
    n = list_entries(near_ref, list_ref, pos, half, False)

    def points_of(ref, at):
        high = ref[at, columns : columns + features].astype(F32)
        return high + ref[at, columns + features :].astype(F32)

    def trip(i, carry):
        for u in range(UNROLL):
            entry, leaf_at, row, m = near_entry(near_ref, list_ref, i * UNROLL + u, pos, half)
            own = (m >= half) & (m < 3 * half)
            from_x = (m < half) == (odd == 1)
            within = m % half
            points = jnp.where(from_x, points_of(vx_ref, within), points_of(vo_ref, within))
            points = jnp.where(own, columns_of(e_ref, jnp.clip(m - half, 0, 2 * half - 1), leaf), points)
            tile = tile_of(other_rows(points), own_rows(columns_of(e_ref, row, leaf)))
            tile_ref[entry] = tile
            near_out[leaf_at] += dot(vw[m], tile, 1, 0)
        return carry

    lax.fori_loop(0, (n + UNROLL - 1) // UNROLL, trip, 0)


def far_first_kernel(
    pos_ref, far_ref, rs_ref, sc_ref, basis_ref, coup_ref, trans_ref, near_ref, coarse_ref, sum_a, sum_b, c0, c1, c2,
    u_ref, q_ref, cp_ref, part_ref, msg_ref, mx_ref, mo_ref, cw, fc, mv, coefs, acc_uu, acc_ru,
):
    per, rank, leaf = basis_ref.shape
    half = per // 2
    size = rank // 2
    pos = pos_ref[0]
    odd = pos % 2
    load_coefficients(cw, (c0, c1, c2))
    coarse_rows(coarse_ref, (sum_a, sum_b), fc)
    store_moved(trans_ref[...], fc, mv)
    acc_uu[...] = jnp.zeros_like(acc_uu)
    acc_ru[...] = jnp.zeros_like(acc_ru)

    def one(l):
        rows = pl.ds(pl.multiple_of(l * rank, rank), rank)
        far = far_sum(l, pos, far_ref, cw, coup_ref, mv[rows], basis_ref)
        right = columns_of(rs_ref, l, leaf)
        scale = columns_of(sc_ref, l, leaf)
        image = RIDGE_TERM * (right * scale) + (near_ref[l] + far)
        u_ref[:, pl.ds(pl.multiple_of(l * leaf, leaf), leaf)] = image
        acc_uu[...] += lane_groups(image * image)
        acc_ru[...] += lane_groups(right * image)
        rounded = (image * scale).astype(BF16)
        q_ref[l] = rounded
        coef = leaf_coefficients(basis_ref[l], rounded)
        coefs[rows] = coef
        cp_ref[pl.ds(pl.multiple_of(l * size, size), size)] = pack_pair(coef)

    leaf_loop(per, FAR_UNROLL, one)
    store_share(share_of(trans_ref[...], coefs[...]), part_ref, cp_ref)
    mx_ref[...] = q_ref[pl.ds(half * (1 - odd), half)]
    mo_ref[...] = q_ref[pl.ds(half * odd, half)]
    lane = lax.broadcasted_iota(jnp.int32, msg_ref.shape, 1)
    out = jnp.where(lane == 0, jnp.sum(acc_uu[...], axis=1, keepdims=True), 0.0)
    msg_ref[...] = jnp.where(lane == 1, jnp.sum(acc_ru[...], axis=1, keepdims=True), out)


def near_again_kernel(pos_ref, near_ref, q_ref, vx_ref, vo_ref, tile_ref, near_in, near_out, list_ref, vw):
    half = vx_ref.shape[0]
    pos = pos_ref[0]
    load_window(vw, q_ref, vx_ref, vo_ref, pos % 2)
    n = list_entries(near_ref, list_ref, pos, half, False)

    def trip(i, carry):
        for u in range(UNROLL):
            entry, leaf_at, _, m = near_entry(near_ref, list_ref, i * UNROLL + u, pos, half)
            near_out[leaf_at] += dot(vw[m], tile_ref[entry], 1, 0)
        return carry

    lax.fori_loop(0, (n + UNROLL - 1) // UNROLL, trip, 0)


def far_again_kernel(
    pos_ref, far_ref, rs_ref, sc_ref, u_ref, basis_ref, coup_ref, trans_ref,
    coarse_ref, sum_a, sum_b, c0, c1, c2, near_ref, prev_ref, w_ref, msg_ref,
    cw, fc, mv, acc_uw, acc_ww, acc_rw,
):
    per, rank, leaf = basis_ref.shape
    pos = pos_ref[0]
    load_coefficients(cw, (c0, c1, c2))
    coarse_rows(coarse_ref, (sum_a, sum_b), fc)
    store_moved(trans_ref[...], fc, mv)
    for acc in (acc_uw, acc_ww, acc_rw):
        acc[...] = jnp.zeros_like(acc)

    def one(l):
        far = far_sum(l, pos, far_ref, cw, coup_ref, mv[pl.ds(pl.multiple_of(l * rank, rank), rank)], basis_ref)
        image = columns_of(u_ref, l, leaf)
        second = RIDGE_TERM * (image * columns_of(sc_ref, l, leaf)) + (near_ref[l] + far)
        w_ref[:, pl.ds(pl.multiple_of(l * leaf, leaf), leaf)] = second
        acc_uw[...] += lane_groups(image * second)
        acc_ww[...] += lane_groups(second * second)
        acc_rw[...] += lane_groups(columns_of(rs_ref, l, leaf) * second)

    leaf_loop(per, FAR_UNROLL, one)
    lane = lax.broadcasted_iota(jnp.int32, msg_ref.shape, 1)
    out = prev_ref[...]
    for at, acc in enumerate((acc_uw, acc_ww, acc_rw)):
        out = jnp.where(lane == 2 + at, jnp.sum(acc[...], axis=1, keepdims=True), out)
    msg_ref[...] = out


def call(kernel, name, in_specs, out_shape, scratch, args, aliases=None, flops=0, out_specs=None, limit=VMEM_LIMIT):
    return pl.pallas_call(
        kernel,
        in_specs=in_specs,
        out_specs=out_specs or [WHOLE] * len(out_shape),
        out_shape=out_shape,
        scratch_shapes=scratch,
        input_output_aliases=aliases or {},
        compiler_params=pltpu.CompilerParams(vmem_limit_bytes=limit),
        cost_estimate=pl.CostEstimate(flops=flops, bytes_accessed=0, transcendentals=0),
        name=name,
    )(*args)


def two_clusters():
    return CDEV == 8 and lax.axis_size("leaf") == 2 * CDEV


def other_clusters(plane_sum):
    count = lax.axis_size("leaf")
    if two_clusters():
        return involution(plane_sum, lambda i: i ^ (12 if i % 2 else 8))
    mask = 4
    while mask < CDEV:
        plane_sum = plane_sum + involution(plane_sum, lambda i: i ^ mask)
        mask *= 2
    sums = plane_sum
    while mask < count:
        sums = jnp.concatenate([sums, involution(sums, lambda i: i ^ mask)], axis=0)
        mask *= 2
    return sums[1:]


def pass_kernel(*refs):
    pass


def after(values, *before):
    return call(
        pass_kernel, "after", [WHOLE] * len(values) + [ANYWHERE] * len(before),
        [pltpu.VMEM(value.shape, value.dtype) for value in values], [], (*values, *before),
        aliases={at: at for at in range(len(values))},
    )


def first_messages(cp):
    return sibling(cp), across(cp)


def second_messages(position, cp, got, part, *before):
    rows = cp.shape[0] - 3 * part.shape[0]
    got = (*got, sibling(got[1]))
    quad, plane_sum = call(
        quad_kernel, "quad", [SCALAR] + [WHOLE] * 5 + [ANYWHERE] * len(before),
        [pltpu.VMEM((4, rows, cp.shape[1]), BF16), pltpu.VMEM((1,) + part.shape, F32)],
        [], (position, cp, *got, part, *before),
    )
    return quad, two_chips(quad), other_clusters(plane_sum)


def last_messages(quad, mine):
    other = sibling(mine) if two_clusters() else jnp.zeros_like(mine)
    return (quad, sibling(quad)), (mine, other)


def body(
    right_side, scaling, embeddings, near_leaves, far_leaves, leaf_basis, leaf_coupling,
    transfer, coarse_coupling,
):
    columns, local_points = right_side.shape
    per, rank, leaf = leaf_basis.shape
    features = embeddings.shape[0]
    slots = near_leaves.shape[1] - 1
    far_count = far_leaves.shape[1]
    half = per // 2
    size = rank // 2
    count = lax.axis_size("leaf")
    pos = lax.axis_index("leaf")
    position = pos.reshape(1).astype(jnp.int32)
    near_rows = near_leaves.T
    far_rows = far_leaves.T
    coarse_count = count // CDEV

    scale_row = scaling.reshape(1, local_points)
    leaf_shape = pltpu.VMEM((per, columns, leaf), BF16)
    cp_shape = pltpu.VMEM((per * size + 3 * size, 2 * columns), BF16)
    part_shape = pltpu.VMEM((size, 2 * columns), F32)
    self_shape = pltpu.HBM((8 * per, leaf, leaf), BF16)
    trans_shape = pltpu.VMEM((per, rank, rank), BF16)
    half_shape = pltpu.VMEM((half, columns, leaf), BF16)
    moved_shape = pltpu.VMEM((per * rank, columns), F32)
    tile_shape = pltpu.VMEM((per * slots + 1, leaf, leaf), BF16)
    near_shape = pltpu.VMEM((per + 1, columns, leaf), F32)
    wide_shape = pltpu.VMEM((columns, local_points), F32)
    msg_shape = pltpu.VMEM((columns, 128), F32)
    coefs_shape = pltpu.VMEM((per * rank, columns), BF16)
    acc_shape = pltpu.VMEM((columns, 128), F32)
    list_shape = pltpu.SMEM((per * slots + UNROLL,), jnp.int32)
    window = [
        pltpu.VMEM((4 * half, columns, leaf), BF16),
        pltpu.VMEM((12 * per, size, 2 * columns), BF16),
        pltpu.VMEM((rank, 3 * columns), BF16),
    ]

    both_shape = pltpu.VMEM((half, columns + 2 * features, leaf), BF16)
    v, cp, part, trans, mx, mo = call(
        prep_kernel, "prep", [SCALAR] + [OUTSIDE] * 5,
        [leaf_shape, cp_shape, part_shape, trans_shape, both_shape, both_shape],
        [pltpu.VMEM(right_side.shape, F32), pltpu.VMEM(scale_row.shape, F32), pltpu.VMEM(leaf_basis.shape, BF16),
         pltpu.VMEM(transfer.shape, BF16), pltpu.VMEM(embeddings.shape, F32),
         pltpu.VMEM((per, 2 * features, leaf), BF16), coefs_shape, pltpu.VMEM((per * rank * rank // 128, 128), F32), pltpu.VMEM((per, rank, 128), F32), pltpu.SemaphoreType.DMA((5,))],
        (position, right_side, scale_row, leaf_basis, transfer, embeddings), limit=WIDE_LIMIT,
    )
    got = first_messages(cp)
    coup, coarse = call(
        relayout_kernel, "relayout", [SCALAR] + [WHOLE] * 2 + [ANYWHERE],
        [pltpu.VMEM((per, 2 * rank, far_count * size), BF16), pltpu.VMEM((coarse_count - 1, rank, rank), BF16)],
        [
            pltpu.VMEM((RELAY_UNROLL, far_count * rank * rank // 128, 128), F32),
            pltpu.VMEM((RELAY_UNROLL, 2, far_count // 4, rank, 128), F32),
            pltpu.VMEM((size, 128), F32), pltpu.VMEM((rank, 128), F32),
        ],
        (position, leaf_coupling, coarse_coupling, cp),
    )
    across_cp, mo = after((got[1], mo), coup)
    got = (got[0], across_cp)
    vo = beside(mo)
    tself, near = call(
        self_kernel, "self_tiles", [WHOLE] * 2 + [ANYWHERE], [self_shape, near_shape],
        [pltpu.VMEM((2 * UNROLL, leaf, leaf), BF16), pltpu.SemaphoreType.DMA((2 * UNROLL,))],
        (embeddings, v, mo), out_specs=[OUTSIDE, WHOLE],
    )
    quad, far_quad, mine = second_messages(position, cp, got, part, near)
    (mx,) = after((mx,), quad)
    vx = sibling(mx)
    tiles, near = call(
        own_kernel, "own_tiles", [SCALAR] * 2 + [WHOLE] * 3 + [ANYWHERE], [tile_shape, near_shape], [list_shape],
        (position, near_rows, embeddings, v, near, quad), aliases={4: 1},
    )
    tiles, near = call(
        foreign_kernel, "foreign_tiles", [SCALAR] * 2 + [WHOLE] * 6, [tile_shape, near_shape],
        [list_shape, window[0]],
        (position, near_rows, embeddings, v, vx, vo, tiles, near), aliases={6: 0, 7: 1},
    )
    coefs, sums = last_messages(*after((far_quad, mine), near))
    image, q, cp, part, msg, mx, mo = call(
        far_first_kernel, "far_first", [SCALAR] * 2 + [WHOLE] * 12,
        [wide_shape, leaf_shape, cp_shape, part_shape, msg_shape, half_shape, half_shape],
        [*window[1:], moved_shape, coefs_shape, acc_shape, acc_shape],
        (position, far_rows, right_side, scale_row, leaf_basis, coup, trans, near, coarse, *sums, quad, *coefs),
    )
    got = first_messages(cp)
    (near,) = call(
        own_again_kernel, "own_again", [SCALAR] * 2 + [WHOLE] * 2, [near_shape], [list_shape],
        (position, near_rows, q, tiles),
    )
    across_cp, mo = after((got[1], mo), near)
    got = (got[0], across_cp)
    vo = beside(mo)
    quad, far_quad, mine = second_messages(position, cp, got, part)
    (mx,) = after((mx,), quad)
    vx = sibling(mx)
    (near,) = call(
        self_again_kernel, "self_again", [WHOLE, OUTSIDE, WHOLE, ANYWHERE], [near_shape],
        [pltpu.VMEM((per, leaf, leaf), BF16), pltpu.SemaphoreType.DMA((per // UNROLL,))],
        (q, tself, near, quad), aliases={2: 0},
    )
    (near,) = call(
        near_again_kernel, "near_again", [SCALAR] * 2 + [WHOLE] * 5, [near_shape], [list_shape, window[0]],
        (position, near_rows, q, vx, vo, tiles, near), aliases={6: 0},
    )
    coefs, sums = last_messages(*after((far_quad, mine), near))
    second, msg = call(
        far_again_kernel, "far_again", [SCALAR] * 2 + [WHOLE] * 14, [wide_shape, msg_shape],
        window[1:] + [moved_shape] + [acc_shape] * 3,
        (position, far_rows, right_side, scale_row, image, leaf_basis, coup, trans,
         coarse, *sums, quad, *coefs, near, msg),
    )

    mask = 1
    while mask < count:
        msg = msg + involution(msg, lambda i: i ^ mask)
        mask *= 2
    uu, ru, uw, ww, rw = [msg[:, k : k + 1] for k in range(5)]
    step_one = ru / (uu + EPSILON)
    beta = -(uu - step_one * uw) / (uu + EPSILON)
    lead = 1.0 + beta
    curvature = lead * lead * uu - 2.0 * lead * step_one * uw + step_one * step_one * ww
    aligned = lead * (ru - step_one * uu) - step_one * (rw - step_one * uw)
    step_two = aligned / (curvature + EPSILON)
    first_weight = step_one + step_two * lead
    second_weight = step_two * step_one
    solution = scale_row * (first_weight * right_side - second_weight * image)
    residual = right_side - first_weight * image + second_weight * second
    return (solution, residual)


def solution(mesh):
    return jax.shard_map(
        body,
        mesh=mesh,
        in_specs=(
            P(None, ("groups", "leaf")),
            P(("groups", "leaf")),
            P(None, ("groups", "leaf")),
            P(("groups", "leaf"), None),
            P(("groups", "leaf"), None),
            P(("groups", "leaf"), None, None),
            P(("groups", "leaf"), None, None),
            P(("groups", "leaf"), None),
            P("groups", None, None),
        ),
        out_specs=(P(None, ("groups", "leaf")), P(None, ("groups", "leaf"))),
        check_vma=False,
    )
```

```python
import math

import jax
import jax.numpy as jnp
from jax import lax
from jax.experimental import pallas as pl
from jax.experimental.pallas import tpu as pltpu
from jax.sharding import PartitionSpec as P

FARDEV = 4
CDEV = 8
KERNEL_SCALE = 0.0625
RIDGE_TERM = 1.0
EPSILON = 1e-06
F32 = jnp.float32
BF16 = jnp.bfloat16
HALF_SCALE = math.sqrt(2.0 * KERNEL_SCALE * math.log2(math.e))
UNROLL = 4
FAR_UNROLL = 8
RELAY_UNROLL = 4
VMEM_LIMIT = 12 * 1024 * 1024
WIDE_LIMIT = 54 * 1024 * 1024
SELF_LIMIT = 28 * 1024 * 1024
WHOLE = pl.BlockSpec(memory_space=pltpu.VMEM)
ANYWHERE = pl.BlockSpec(memory_space=pl.ANY)
OUTSIDE = pl.BlockSpec(memory_space=pltpu.HBM)
SCALAR = pl.BlockSpec(memory_space=pltpu.SMEM)


def involution(value, partner):
    count = lax.axis_size("leaf")
    pairs = [(i, partner(i)) for i in range(count) if 0 <= partner(i) < count]
    return lax.ppermute(value, "leaf", pairs)


def sibling(value):
    return involution(value, lambda i: i ^ 1)


def beside(value):
    return involution(value, lambda i: i + 1 if i % 2 else i - 1)


def across(value):
    return involution(value, lambda i: i ^ 2)


def two_chips(value):
    return involution(value, lambda i: i + 3 if i % 2 else i - 3)


def dot(a, b, ca, cb):
    return lax.dot_general(a, b, (((ca,), (cb,)), ((), ())), preferred_element_type=F32)


def split3(value):
    high = value.astype(BF16)
    rest = value - high.astype(F32)
    mid = rest.astype(BF16)
    low = (rest - mid.astype(F32)).astype(BF16)
    return high, mid, low


def point_pieces(points):
    scaled = points * HALF_SCALE
    high, mid, low = split3(scaled)
    square = 0.5 * jnp.sum(scaled * scaled, axis=0, keepdims=True)
    s_high, s_mid, s_low = split3(square)
    return high, mid, low, s_high.astype(F32), s_mid.astype(F32), s_low.astype(F32)


def norm_rows(first, second, third, width, swap, sign):
    row = lax.broadcasted_iota(jnp.int32, (16, width), 0)
    base = 3 if swap else 0
    ones = 0 if swap else 3
    out = jnp.where((row >= ones) & (row < ones + 3), sign, 0.0)
    for at, piece in enumerate((first, second, third)):
        out = jnp.where(row == base + at, sign * piece, out)
    return out.astype(BF16)


def own_rows(points):
    high, mid, low, a, b, c = point_pieces(points)
    norms = norm_rows(a, b, c, points.shape[1], False, 1.0)
    return jnp.concatenate([high, mid, high, mid, low, high, norms], axis=0)


def other_rows(points):
    high, mid, low, a, b, c = point_pieces(points)
    norms = norm_rows(a, b, c, points.shape[1], True, -1.0)
    return jnp.concatenate([high, high, mid, mid, high, low, norms], axis=0)


def tile_of(other, own):
    return jnp.exp2(dot(other, own, 0, 0)).astype(BF16)


def pack_pair(block):
    half = block.shape[0] // 2
    return jnp.concatenate([block[:half], block[half:]], axis=1)


def lane_groups(value):
    total = value[:, :128]
    for at in range(128, value.shape[1], 128):
        total += value[:, at : at + 128]
    return total


def leaf_coefficients(basis, rounded):
    return dot(basis, rounded, 1, 1).astype(BF16)


def share_of(trans, coefs):
    count, rank, _ = trans.shape
    return dot(trans.reshape(count * rank, rank), coefs, 0, 0)


def columns_of(ref, at, width):
    return ref[:, pl.ds(pl.multiple_of(at * width, width), width)]


def leaf_loop(count, unroll, fn):
    def trip(i, carry):
        for u in range(unroll):
            fn(i * unroll + u)
        return carry

    lax.fori_loop(0, count // unroll, trip, 0)


def store_share(total, part_ref, cp_ref):
    packed = pack_pair(total)
    part_ref[...] = packed
    size = packed.shape[0]
    rows = cp_ref.shape[0] - 3 * size
    for at, piece in enumerate(split3(packed)):
        cp_ref[rows + at * size : rows + (at + 1) * size] = piece


def store_square(flat, target):
    pairs = flat.shape[0]
    target[pl.ds(0, pairs, stride=2)] = flat
    target[pl.ds(1, pairs, stride=2)] = pltpu.roll(flat, 64, 1)


def relayout_kernel(
    pos_ref, near_ref, coup_ref, coarse_ref, wait_ref, out_ref, coarse_out, lists, by_slots, by_rows, flat, square
):
    per, slots, entries = coup_ref.shape
    rank = out_ref.shape[1] // 2
    quarter = rank // 2
    pairs = entries // 128
    lane = lax.broadcasted_iota(jnp.int32, (pairs, 128), 1) // quarter

    def one(l, by_slot, by_row):
        wide = coup_ref[l].astype(F32)
        for k in range(pairs):
            by_slot[k * slots : (k + 1) * slots] = wide[:, k * 128 : (k + 1) * 128]
        rows = [by_slot[pl.ds(s, pairs, stride=slots)] for s in range(slots)]
        turned = [[rows[s] if t == 0 else pltpu.roll(rows[s], t * quarter, 1) for t in range(4)] for s in range(slots)]
        for half in range(2):
            for parity in range(2):
                chunk = 2 * parity + half
                for group in range(slots // 4):
                    out = turned[4 * group][(0 - chunk) % 4]
                    for r in range(1, 4):
                        out = jnp.where(lane == r, turned[4 * group + r][(r - chunk) % 4], out)
                    by_row[half, group, pl.ds(parity, pairs, stride=2)] = out
        for half in range(2):
            for group in range(slots // 4):
                out_ref[l, half * rank : (half + 1) * rank, group * 128 : (group + 1) * 128] = by_row[half, group].astype(BF16)

    def trip(i, carry):
        for u in range(by_slots.shape[0]):
            one(i * by_slots.shape[0] + u, by_slots.at[u], by_rows.at[u])
        return carry

    lax.fori_loop(0, per // by_slots.shape[0], trip, 0)
    build_lists(near_ref, lists, pos_ref[0], per // 2)
    cluster = pos_ref[0] // CDEV
    wide = coarse_ref[cluster].astype(F32)
    number = lax.broadcasted_iota(jnp.int32, wide.shape, 0)
    for at in range(coarse_out.shape[0]):
        row = jnp.sum(jnp.where(number == (cluster ^ (at + 1)), wide, 0.0), axis=0, keepdims=True)
        for k in range(pairs):
            flat[k : k + 1] = row[:, k * 128 : (k + 1) * 128]
        store_square(flat[...], square)
        coarse_out[at] = square[:, :rank].astype(BF16)


def prep_kernel(
    pos_ref, rs_hbm, sc_hbm, basis_hbm, transfer_hbm, e_hbm, v_ref, cp_ref, part_ref, trans_ref, mx_ref, mo_ref,
    rs_ref, sc_ref, basis_ref, transfer_ref, e_ref, points, coefs, by_leaf, squares, sems,
):
    per, rank, leaf = basis_ref.shape
    columns, features = rs_ref.shape[0], e_ref.shape[0]
    size = rank // 2
    copies = [
        pltpu.make_async_copy(source, target, sems.at[at])
        for at, (source, target) in enumerate(
            ((transfer_hbm, transfer_ref), (sc_hbm, sc_ref), (rs_hbm, rs_ref), (basis_hbm, basis_ref), (e_hbm, e_ref))
        )
    ]
    for copy in copies:
        copy.start()
    copies[0].wait()
    wide = transfer_ref[...].astype(F32)
    for k in range(rank * rank // 128):
        by_leaf[k * per : (k + 1) * per] = wide[:, k * 128 : (k + 1) * 128]
    for at in range(per):
        store_square(by_leaf[pl.ds(at, rank * rank // 128, stride=per)], squares.at[at])
    trans_ref[...] = squares[:, :, :rank].astype(BF16)
    for copy in copies[1:]:
        copy.wait()

    def one(at):
        rounded = (columns_of(rs_ref, at, leaf) * columns_of(sc_ref, at, leaf)).astype(BF16)
        v_ref[at] = rounded
        here = columns_of(e_ref, at, leaf)
        high = here.astype(BF16)
        points[at, :features] = high
        points[at, features:] = (here - high.astype(F32)).astype(BF16)
        coef = leaf_coefficients(basis_ref[at], rounded)
        coefs[pl.ds(pl.multiple_of(at * rank, rank), rank)] = coef
        cp_ref[pl.ds(pl.multiple_of(at * size, size), size)] = pack_pair(coef)

    leaf_loop(per, UNROLL, one)
    store_share(share_of(trans_ref[...], coefs[...]), part_ref, cp_ref)
    odd = pos_ref[0] % 2
    half = per // 2
    for ref, first in ((mx_ref, half * (1 - odd)), (mo_ref, half * odd)):
        ref[:, :columns] = v_ref[pl.ds(first, half)]
        ref[:, columns:] = points[pl.ds(first, half)]


def quad_kernel(pos_ref, own_ref, sib_ref, across_ref, both_ref, part_ref, *rest):
    quad_ref, sum_ref = rest[-2:]
    place = pos_ref[0] % 4
    rows = quad_ref.shape[1]
    size = part_ref.shape[0]
    quad_ref[place] = own_ref[:rows]
    total = part_ref[...]
    for flip, ref in ((1, sib_ref), (2, across_ref), (3, both_ref)):
        quad_ref[place ^ flip] = ref[:rows]
        for at in range(3):
            total += ref[rows + at * size : rows + (at + 1) * size].astype(F32)
    sum_ref[...] = total[None]


def build_lists(near_ref, lists, pos, half):
    slots = near_ref.shape[0] - 1
    total = near_ref.shape[1] * slots
    base = pos * 2 * half - half

    def put(entry, counts):
        m = near_ref[1 + entry % slots, entry // slots] - base
        own = (m >= half) & (m < 3 * half)
        low = (m < half) == (pos % 2 == 1)
        takes = (own, ~own & low, ~own & ~low, own | low)
        for kind, count in enumerate(counts):
            lists[kind, count] = entry * 4 * half + m
        return tuple(count + jnp.where(take, 1, 0) for count, take in zip(counts, takes))

    counts = lax.fori_loop(0, total, put, (0, 0, 0, 0))
    for kind, count in enumerate(counts):
        for u in range(UNROLL):
            lists[kind, count + u] = total * 4 * half + half
        lists[kind, lists.shape[1] - 1] = count


def near_entry(lists, kind, at, tile_ref, half):
    slots = (tile_ref.shape[0] - 1) // (2 * half)
    value = lists[kind, at]
    entry = value // (4 * half)
    leaf_at = entry // slots
    return entry, leaf_at, jnp.minimum(leaf_at, 2 * half - 1), value % (4 * half)


def self_kernel(e_ref, v_ref, wait_ref, self_ref, near_out, buffer, sems):
    per, _, leaf = v_ref.shape

    def copy_out(slot, at):
        return pltpu.make_async_copy(buffer.at[slot], self_ref.at[at], sems.at[slot])

    def trip(i, carry):
        for u in range(UNROLL):
            at = i * UNROLL + u
            slot = (i % 2) * UNROLL + u

            @pl.when(i >= 2)
            def _():
                copy_out(slot, at - 2 * UNROLL).wait()

        for u in range(UNROLL):
            at = i * UNROLL + u
            points = columns_of(e_ref, at, leaf)
            tile = tile_of(other_rows(points), own_rows(points))
            buffer[(i % 2) * UNROLL + u] = tile
            near_out[at] = dot(v_ref[at], tile, 1, 0)
        for u in range(UNROLL):
            copy_out((i % 2) * UNROLL + u, i * UNROLL + u).start()
        return carry

    trips = per // UNROLL
    lax.fori_loop(0, trips, trip, 0)
    for i in range(max(trips - 2, 0), trips):
        for u in range(UNROLL):
            copy_out((i % 2) * UNROLL + u, i * UNROLL + u).wait()


def points_of(ref, at, columns, features):
    high = ref[at, columns : columns + features].astype(F32)
    return high + ref[at, columns + features :].astype(F32)


def own_kernel(pos_ref, lists, e_ref, v_ref, vx_ref, near_in, wait_ref, tile_ref, near_out, vw):
    per, columns, leaf = v_ref.shape
    half = per // 2
    vw[:per] = v_ref[...]
    vw[per:] = vx_ref[:, :columns]
    n = lists[3, lists.shape[1] - 1]

    def trip(i, carry):
        for u in range(UNROLL):
            entry, leaf_at, row, m = near_entry(lists, 3, i * UNROLL + u, tile_ref, half)
            own = (m >= half) & (m < 3 * half)
            place = jnp.clip(m - half, 0, per - 1)
            points = jnp.where(
                own, columns_of(e_ref, place, leaf), points_of(vx_ref, m % half, columns, e_ref.shape[0])
            )
            tile = tile_of(other_rows(points), own_rows(columns_of(e_ref, row, leaf)))
            tile_ref[entry] = tile
            near_out[leaf_at] += dot(vw[jnp.where(own, place, per + m % half)], tile, 1, 0)
        return carry

    lax.fori_loop(0, (n + UNROLL - 1) // UNROLL, trip, 0)


def own_again_kernel(pos_ref, lists, v_ref, tile_ref, near_out):
    half = v_ref.shape[0] // 2
    near_out[...] = jnp.zeros_like(near_out)
    n = lists[0, lists.shape[1] - 1]

    def trip(i, carry):
        for u in range(UNROLL):
            entry, leaf_at, _, m = near_entry(lists, 0, i * UNROLL + u, tile_ref, half)
            place = jnp.clip(m - half, 0, 2 * half - 1)
            near_out[leaf_at] += dot(v_ref[place], tile_ref[entry], 1, 0)
        return carry

    lax.fori_loop(0, (n + UNROLL - 1) // UNROLL, trip, 0)


def self_again_kernel(
    pos_ref, lists, v_ref, vx_ref, tile_ref, self_hbm, near_in, wait_ref, near_out, self_ref, sems,
):
    per = v_ref.shape[0]
    half = per // 2
    copies = [
        pltpu.make_async_copy(self_hbm.at[pl.ds(at, UNROLL)], self_ref.at[pl.ds(at, UNROLL)], sems.at[at // UNROLL])
        for at in range(0, per, UNROLL)
    ]
    for copy in copies:
        copy.start()
    n = lists[1, lists.shape[1] - 1]

    def trip(i, carry):
        for u in range(UNROLL):
            entry, leaf_at, _, m = near_entry(lists, 1, i * UNROLL + u, tile_ref, half)
            near_out[leaf_at] += dot(vx_ref[m % half], tile_ref[entry], 1, 0)
        return carry

    lax.fori_loop(0, (n + UNROLL - 1) // UNROLL, trip, 0)
    for i, copy in enumerate(copies):
        copy.wait()
        for u in range(UNROLL):
            at = i * UNROLL + u
            near_out[at] += dot(v_ref[at], self_ref[at], 1, 0)


def load_coefficients(cw, sources):
    devices, rows, _ = sources[0].shape
    per = rows // cw.shape[1]
    for slot, source in enumerate(sources):
        for device in range(devices):
            for at in range(per):
                cw[(slot * devices + device) * per + at] = source[device, at * cw.shape[1] : (at + 1) * cw.shape[1]]


def coarse_rows(coarse_ref, sum_refs, fc):
    rank = coarse_ref.shape[1]
    acc = jnp.zeros((rank, rank), F32)
    for at in range(coarse_ref.shape[0]):
        packed = sum_refs[0][at]
        for ref in sum_refs[1:]:
            packed += ref[at]
        total = jnp.concatenate([packed[:, :rank], packed[:, rank:]], axis=0)
        for piece in split3(total):
            acc += dot(coarse_ref[at], piece, 1, 0)
    fc[...] = jnp.concatenate(split3(acc), axis=1)


def far_sum(l, pos, far_ref, cw, coup_ref, moved, basis_ref):
    per, rank, _ = basis_ref.shape
    odd = pos % 2
    picks = []
    for s in range(far_ref.shape[0]):
        leaf_id = far_ref[s, l]
        device = leaf_id // per
        gap = device // 4 - pos // 4
        slot = jnp.where(gap == 0, 0, jnp.where((gap < 0) == (odd == 0), 1, 2))
        picks.append(cw[(slot * 4 + device % 4) * per + leaf_id % per])
    wide = dot(coup_ref[l], jnp.concatenate(picks, axis=0), 1, 0)
    combined = wide[:rank, :rank] + wide[rank:, rank:] + moved
    return dot(combined.astype(BF16), basis_ref[l], 0, 0)


def store_moved(trans, fc, mv):
    count, rank, _ = trans.shape
    wide = dot(trans.reshape(count * rank, rank), fc[...], 1, 0)
    mv[...] = wide[:, :rank] + wide[:, rank : 2 * rank] + wide[:, 2 * rank :]


def foreign_kernel(pos_ref, lists, e_ref, vo_ref, tile_in, near_in, tile_ref, near_out):
    half, _, leaf = vo_ref.shape
    features = e_ref.shape[0]
    columns = vo_ref.shape[1] - 2 * features
    n = lists[2, lists.shape[1] - 1]

    def trip(i, carry):
        for u in range(UNROLL):
            entry, leaf_at, row, m = near_entry(lists, 2, i * UNROLL + u, tile_ref, half)
            points = points_of(vo_ref, m % half, columns, features)
            tile = tile_of(other_rows(points), own_rows(columns_of(e_ref, row, leaf)))
            tile_ref[entry] = tile
            near_out[leaf_at] += dot(vo_ref[m % half, :columns], tile, 1, 0)
        return carry

    lax.fori_loop(0, (n + UNROLL - 1) // UNROLL, trip, 0)


def far_first_kernel(
    pos_ref, far_ref, rs_ref, sc_ref, basis_ref, coup_ref, trans_ref, near_ref, coarse_ref, sum_a, sum_b, c0, c1, c2,
    u_ref, q_ref, cp_ref, part_ref, msg_ref, mx_ref, mo_ref, cw, fc, mv, coefs, acc_uu, acc_ru,
):
    per, rank, leaf = basis_ref.shape
    half = per // 2
    size = rank // 2
    pos = pos_ref[0]
    odd = pos % 2
    load_coefficients(cw, (c0, c1, c2))
    coarse_rows(coarse_ref, (sum_a, sum_b), fc)
    store_moved(trans_ref[...], fc, mv)
    acc_uu[...] = jnp.zeros_like(acc_uu)
    acc_ru[...] = jnp.zeros_like(acc_ru)

    def one(l):
        rows = pl.ds(pl.multiple_of(l * rank, rank), rank)
        far = far_sum(l, pos, far_ref, cw, coup_ref, mv[rows], basis_ref)
        right = columns_of(rs_ref, l, leaf)
        scale = columns_of(sc_ref, l, leaf)
        image = RIDGE_TERM * (right * scale) + (near_ref[l] + far)
        u_ref[:, pl.ds(pl.multiple_of(l * leaf, leaf), leaf)] = image
        acc_uu[...] += lane_groups(image * image)
        acc_ru[...] += lane_groups(right * image)
        rounded = (image * scale).astype(BF16)
        q_ref[l] = rounded
        coef = leaf_coefficients(basis_ref[l], rounded)
        coefs[rows] = coef
        cp_ref[pl.ds(pl.multiple_of(l * size, size), size)] = pack_pair(coef)

    leaf_loop(per, FAR_UNROLL, one)
    store_share(share_of(trans_ref[...], coefs[...]), part_ref, cp_ref)
    mx_ref[...] = q_ref[pl.ds(half * (1 - odd), half)]
    mo_ref[...] = q_ref[pl.ds(half * odd, half)]
    lane = lax.broadcasted_iota(jnp.int32, msg_ref.shape, 1)
    out = jnp.where(lane == 0, jnp.sum(acc_uu[...], axis=1, keepdims=True), 0.0)
    msg_ref[...] = jnp.where(lane == 1, jnp.sum(acc_ru[...], axis=1, keepdims=True), out)


def near_again_kernel(pos_ref, lists, vo_ref, tile_ref, near_in, near_out):
    half = vo_ref.shape[0]
    n = lists[2, lists.shape[1] - 1]

    def trip(i, carry):
        for u in range(UNROLL):
            entry, leaf_at, _, m = near_entry(lists, 2, i * UNROLL + u, tile_ref, half)
            near_out[leaf_at] += dot(vo_ref[m % half], tile_ref[entry], 1, 0)
        return carry

    lax.fori_loop(0, (n + UNROLL - 1) // UNROLL, trip, 0)


def far_again_kernel(
    pos_ref, far_ref, rs_ref, sc_ref, u_ref, basis_ref, coup_ref, trans_ref,
    coarse_ref, sum_a, sum_b, c0, c1, c2, near_ref, prev_ref, w_ref, msg_ref,
    cw, fc, mv, acc_uw, acc_ww, acc_rw,
):
    per, rank, leaf = basis_ref.shape
    pos = pos_ref[0]
    load_coefficients(cw, (c0, c1, c2))
    coarse_rows(coarse_ref, (sum_a, sum_b), fc)
    store_moved(trans_ref[...], fc, mv)
    for acc in (acc_uw, acc_ww, acc_rw):
        acc[...] = jnp.zeros_like(acc)

    def one(l):
        far = far_sum(l, pos, far_ref, cw, coup_ref, mv[pl.ds(pl.multiple_of(l * rank, rank), rank)], basis_ref)
        image = columns_of(u_ref, l, leaf)
        second = RIDGE_TERM * (image * columns_of(sc_ref, l, leaf)) + (near_ref[l] + far)
        w_ref[:, pl.ds(pl.multiple_of(l * leaf, leaf), leaf)] = second
        acc_uw[...] += lane_groups(image * second)
        acc_ww[...] += lane_groups(second * second)
        acc_rw[...] += lane_groups(columns_of(rs_ref, l, leaf) * second)

    leaf_loop(per, FAR_UNROLL, one)
    lane = lax.broadcasted_iota(jnp.int32, msg_ref.shape, 1)
    out = prev_ref[...]
    for at, acc in enumerate((acc_uw, acc_ww, acc_rw)):
        out = jnp.where(lane == 2 + at, jnp.sum(acc[...], axis=1, keepdims=True), out)
    msg_ref[...] = out


def call(kernel, name, in_specs, out_shape, scratch, args, aliases=None, flops=0, out_specs=None, limit=VMEM_LIMIT):
    return pl.pallas_call(
        kernel,
        in_specs=in_specs,
        out_specs=out_specs or [WHOLE] * len(out_shape),
        out_shape=out_shape,
        scratch_shapes=scratch,
        input_output_aliases=aliases or {},
        compiler_params=pltpu.CompilerParams(vmem_limit_bytes=limit),
        cost_estimate=pl.CostEstimate(flops=flops, bytes_accessed=0, transcendentals=0),
        name=name,
    )(*args)


def two_clusters():
    return CDEV == 8 and lax.axis_size("leaf") == 2 * CDEV


def other_clusters(plane_sum):
    count = lax.axis_size("leaf")
    if two_clusters():
        return involution(plane_sum, lambda i: i ^ (12 if i % 2 else 8))
    mask = 4
    while mask < CDEV:
        plane_sum = plane_sum + involution(plane_sum, lambda i: i ^ mask)
        mask *= 2
    sums = plane_sum
    while mask < count:
        sums = jnp.concatenate([sums, involution(sums, lambda i: i ^ mask)], axis=0)
        mask *= 2
    return sums[1:]


def pass_kernel(*refs):
    pass


def after(values, *before):
    return call(
        pass_kernel, "after", [WHOLE] * len(values) + [ANYWHERE] * len(before),
        [pltpu.VMEM(value.shape, value.dtype) for value in values], [], (*values, *before),
        aliases={at: at for at in range(len(values))},
    )


def first_messages(cp):
    return sibling(cp), across(cp)


def second_messages(position, cp, got, part, *before):
    rows = cp.shape[0] - 3 * part.shape[0]
    got = (*got, sibling(got[1]))
    quad, plane_sum = call(
        quad_kernel, "quad", [SCALAR] + [WHOLE] * 5 + [ANYWHERE] * len(before),
        [pltpu.VMEM((4, rows, cp.shape[1]), BF16), pltpu.VMEM((1,) + part.shape, F32)],
        [], (position, cp, *got, part, *before),
    )
    return quad, two_chips(quad), other_clusters(plane_sum)


def last_messages(quad, mine):
    other = sibling(mine) if two_clusters() else jnp.zeros_like(mine)
    return (quad, sibling(quad)), (mine, other)


def body(
    right_side, scaling, embeddings, near_leaves, far_leaves, leaf_basis, leaf_coupling,
    transfer, coarse_coupling,
):
    columns, local_points = right_side.shape
    per, rank, leaf = leaf_basis.shape
    features = embeddings.shape[0]
    slots = near_leaves.shape[1] - 1
    far_count = far_leaves.shape[1]
    half = per // 2
    size = rank // 2
    count = lax.axis_size("leaf")
    pos = lax.axis_index("leaf")
    position = pos.reshape(1).astype(jnp.int32)
    near_rows = near_leaves.T
    far_rows = far_leaves.T
    coarse_count = count // CDEV

    scale_row = scaling.reshape(1, local_points)
    leaf_shape = pltpu.VMEM((per, columns, leaf), BF16)
    cp_shape = pltpu.VMEM((per * size + 3 * size, 2 * columns), BF16)
    part_shape = pltpu.VMEM((size, 2 * columns), F32)
    self_shape = pltpu.HBM((8 * per, leaf, leaf), BF16)
    trans_shape = pltpu.VMEM((per, rank, rank), BF16)
    half_shape = pltpu.VMEM((half, columns, leaf), BF16)
    moved_shape = pltpu.VMEM((per * rank, columns), F32)
    tile_shape = pltpu.VMEM((per * slots + 1, leaf, leaf), BF16)
    near_shape = pltpu.VMEM((per + 1, columns, leaf), F32)
    wide_shape = pltpu.VMEM((columns, local_points), F32)
    msg_shape = pltpu.VMEM((columns, 128), F32)
    coefs_shape = pltpu.VMEM((per * rank, columns), BF16)
    acc_shape = pltpu.VMEM((columns, 128), F32)
    window = [
        pltpu.VMEM((12 * per, size, 2 * columns), BF16),
        pltpu.VMEM((rank, 3 * columns), BF16),
    ]

    both_shape = pltpu.VMEM((half, columns + 2 * features, leaf), BF16)
    v, cp, part, trans, mx, mo = call(
        prep_kernel, "prep", [SCALAR] + [OUTSIDE] * 5,
        [leaf_shape, cp_shape, part_shape, trans_shape, both_shape, both_shape],
        [pltpu.VMEM(right_side.shape, F32), pltpu.VMEM(scale_row.shape, F32), pltpu.VMEM(leaf_basis.shape, BF16),
         pltpu.VMEM(transfer.shape, BF16), pltpu.VMEM(embeddings.shape, F32),
         pltpu.VMEM((per, 2 * features, leaf), BF16), coefs_shape, pltpu.VMEM((per * rank * rank // 128, 128), F32), pltpu.VMEM((per, rank, 128), F32), pltpu.SemaphoreType.DMA((5,))],
        (position, right_side, scale_row, leaf_basis, transfer, embeddings), limit=WIDE_LIMIT,
    )
    got = first_messages(cp)
    coup, coarse, lists = call(
        relayout_kernel, "relayout", [SCALAR] * 2 + [WHOLE] * 2 + [ANYWHERE],
        [pltpu.VMEM((per, 2 * rank, far_count * size), BF16), pltpu.VMEM((coarse_count - 1, rank, rank), BF16),
         jax.ShapeDtypeStruct((4, per * slots + 2 * UNROLL), jnp.int32)],
        [
            pltpu.VMEM((RELAY_UNROLL, far_count * rank * rank // 128, 128), F32),
            pltpu.VMEM((RELAY_UNROLL, 2, far_count // 4, rank, 128), F32),
            pltpu.VMEM((size, 128), F32), pltpu.VMEM((rank, 128), F32),
        ],
        (position, near_rows, leaf_coupling, coarse_coupling, cp), out_specs=[WHOLE, WHOLE, SCALAR],
    )
    across_cp, mo, mx = after((got[1], mo, mx), coup)
    got = (got[0], across_cp)
    vo = beside(mo)
    vx = sibling(mx)
    tself, near = call(
        self_kernel, "self_tiles", [WHOLE] * 2 + [ANYWHERE], [self_shape, near_shape],
        [pltpu.VMEM((2 * UNROLL, leaf, leaf), BF16), pltpu.SemaphoreType.DMA((2 * UNROLL,))],
        (embeddings, v, mo), out_specs=[OUTSIDE, WHOLE],
    )
    quad, far_quad, mine = second_messages(position, cp, got, part, near)
    tiles, near = call(
        own_kernel, "own_tiles", [SCALAR] * 2 + [WHOLE] * 4 + [ANYWHERE], [tile_shape, near_shape],
        [pltpu.VMEM((per + half, columns, leaf), BF16)],
        (position, lists, embeddings, v, vx, near, quad), aliases={5: 1},
    )
    coefs, sums = last_messages(*after((far_quad, mine), near))
    tiles, near = call(
        foreign_kernel, "foreign_tiles", [SCALAR] * 2 + [WHOLE] * 4, [tile_shape, near_shape], [],
        (position, lists, embeddings, vo, tiles, near), aliases={4: 0, 5: 1},
    )
    image, q, cp, part, msg, mx, mo = call(
        far_first_kernel, "far_first", [SCALAR] * 2 + [WHOLE] * 12,
        [wide_shape, leaf_shape, cp_shape, part_shape, msg_shape, half_shape, half_shape],
        [*window, moved_shape, coefs_shape, acc_shape, acc_shape],
        (position, far_rows, right_side, scale_row, leaf_basis, coup, trans, near, coarse, *sums, quad, *coefs),
    )
    got = first_messages(cp)
    (near,) = call(
        own_again_kernel, "own_again", [SCALAR] * 2 + [WHOLE] * 2, [near_shape], [],
        (position, lists, q, tiles),
    )
    across_cp, mo = after((got[1], mo), near)
    got = (got[0], across_cp)
    vo = beside(mo)
    quad, far_quad, mine = second_messages(position, cp, got, part)
    vx = sibling(mx)
    (near,) = call(
        self_again_kernel, "self_again", [SCALAR] * 2 + [WHOLE] * 3 + [OUTSIDE, WHOLE, ANYWHERE], [near_shape],
        [pltpu.VMEM((per, leaf, leaf), BF16), pltpu.SemaphoreType.DMA((per // UNROLL,))],
        (position, lists, q, vx, tiles, tself, near, quad), aliases={6: 0},
    )
    coefs, sums = last_messages(*after((far_quad, mine), near, vo))
    (near,) = call(
        near_again_kernel, "near_again", [SCALAR] * 2 + [WHOLE] * 3, [near_shape], [],
        (position, lists, vo, tiles, near), aliases={4: 0},
    )
    second, msg = call(
        far_again_kernel, "far_again", [SCALAR] * 2 + [WHOLE] * 14, [wide_shape, msg_shape],
        window + [moved_shape] + [acc_shape] * 3,
        (position, far_rows, right_side, scale_row, image, leaf_basis, coup, trans,
         coarse, *sums, quad, *coefs, near, msg),
    )

    mask = 1
    while mask < count:
        msg = msg + involution(msg, lambda i: i ^ mask)
        mask *= 2
    uu, ru, uw, ww, rw = [msg[:, k : k + 1] for k in range(5)]
    step_one = ru / (uu + EPSILON)
    beta = -(uu - step_one * uw) / (uu + EPSILON)
    lead = 1.0 + beta
    curvature = lead * lead * uu - 2.0 * lead * step_one * uw + step_one * step_one * ww
    aligned = lead * (ru - step_one * uu) - step_one * (rw - step_one * uw)
    step_two = aligned / (curvature + EPSILON)
    first_weight = step_one + step_two * lead
    second_weight = step_two * step_one
    solution = scale_row * (first_weight * right_side - second_weight * image)
    residual = right_side - first_weight * image + second_weight * second
    return (solution, residual)


def solution(mesh):
    return jax.shard_map(
        body,
        mesh=mesh,
        in_specs=(
            P(None, ("groups", "leaf")),
            P(("groups", "leaf")),
            P(None, ("groups", "leaf")),
            P(("groups", "leaf"), None),
            P(("groups", "leaf"), None),
            P(("groups", "leaf"), None, None),
            P(("groups", "leaf"), None, None),
            P(("groups", "leaf"), None),
            P("groups", None, None),
        ),
        out_specs=(P(None, ("groups", "leaf")), P(None, ("groups", "leaf"))),
        check_vma=False,
    )
```

```python
import math

import jax
import jax.numpy as jnp
from jax import lax
from jax.experimental import pallas as pl
from jax.experimental.pallas import tpu as pltpu
from jax.sharding import PartitionSpec as P

FARDEV = 4
CDEV = 8
KERNEL_SCALE = 0.0625
RIDGE_TERM = 1.0
EPSILON = 1e-06
F32 = jnp.float32
BF16 = jnp.bfloat16
HALF_SCALE = math.sqrt(2.0 * KERNEL_SCALE * math.log2(math.e))
UNROLL = 4
FAR_UNROLL = 16
RELAY_UNROLL = 4
VMEM_LIMIT = 13 * 1024 * 1024
WIDE_LIMIT = 54 * 1024 * 1024
SELF_LIMIT = 28 * 1024 * 1024
WHOLE = pl.BlockSpec(memory_space=pltpu.VMEM)
ANYWHERE = pl.BlockSpec(memory_space=pl.ANY)
OUTSIDE = pl.BlockSpec(memory_space=pltpu.HBM)
SCALAR = pl.BlockSpec(memory_space=pltpu.SMEM)


def involution(value, partner):
    count = lax.axis_size("leaf")
    pairs = [(i, partner(i)) for i in range(count) if 0 <= partner(i) < count]
    return lax.ppermute(value, "leaf", pairs)


def sibling(value):
    return involution(value, lambda i: i ^ 1)


def beside(value):
    return involution(value, lambda i: i + 1 if i % 2 else i - 1)


def across(value):
    return involution(value, lambda i: i ^ 2)


def two_chips(value):
    return involution(value, lambda i: i + 3 if i % 2 else i - 3)


def dot(a, b, ca, cb):
    return lax.dot_general(a, b, (((ca,), (cb,)), ((), ())), preferred_element_type=F32)


def split3(value):
    high = value.astype(BF16)
    rest = value - high.astype(F32)
    mid = rest.astype(BF16)
    low = (rest - mid.astype(F32)).astype(BF16)
    return high, mid, low


def point_pieces(points):
    scaled = points * HALF_SCALE
    high, mid, low = split3(scaled)
    square = 0.5 * jnp.sum(scaled * scaled, axis=0, keepdims=True)
    s_high, s_mid, s_low = split3(square)
    return high, mid, low, s_high.astype(F32), s_mid.astype(F32), s_low.astype(F32)


def norm_rows(first, second, third, width, swap, sign):
    row = lax.broadcasted_iota(jnp.int32, (16, width), 0)
    base = 3 if swap else 0
    ones = 0 if swap else 3
    out = jnp.where((row >= ones) & (row < ones + 3), sign, 0.0)
    for at, piece in enumerate((first, second, third)):
        out = jnp.where(row == base + at, sign * piece, out)
    return out.astype(BF16)


def own_rows(points):
    high, mid, low, a, b, c = point_pieces(points)
    norms = norm_rows(a, b, c, points.shape[1], False, 1.0)
    return jnp.concatenate([high, mid, high, mid, low, high, norms], axis=0)


def other_rows(points):
    high, mid, low, a, b, c = point_pieces(points)
    norms = norm_rows(a, b, c, points.shape[1], True, -1.0)
    return jnp.concatenate([high, high, mid, mid, high, low, norms], axis=0)


def tile_of(other, own):
    return jnp.exp2(dot(other, own, 0, 0)).astype(BF16)


def pack_pair(block):
    half = block.shape[0] // 2
    return jnp.concatenate([block[:half], block[half:]], axis=1)


def lane_groups(value):
    total = value[:, :128]
    for at in range(128, value.shape[1], 128):
        total += value[:, at : at + 128]
    return total


def leaf_coefficients(basis, rounded):
    return dot(basis, rounded, 1, 1).astype(BF16)


def share_of(trans, coefs):
    count, rank, _ = trans.shape
    return dot(trans.reshape(count * rank, rank), coefs, 0, 0)


def columns_of(ref, at, width):
    return ref[:, pl.ds(pl.multiple_of(at * width, width), width)]


def leaf_loop(count, unroll, fn):
    def trip(i, carry):
        for u in range(unroll):
            fn(i * unroll + u)
        return carry

    lax.fori_loop(0, count // unroll, trip, 0)


def store_share(total, part_ref, cp_ref):
    packed = pack_pair(total)
    part_ref[...] = packed
    size = packed.shape[0]
    rows = cp_ref.shape[0] - 3 * size
    for at, piece in enumerate(split3(packed)):
        cp_ref[rows + at * size : rows + (at + 1) * size] = piece


def store_square(flat, target):
    pairs = flat.shape[0]
    target[pl.ds(0, pairs, stride=2)] = flat
    target[pl.ds(1, pairs, stride=2)] = pltpu.roll(flat, 64, 1)


def relayout_kernel(
    pos_ref, near_ref, coup_ref, coarse_ref, wait_ref, out_ref, coarse_out, lists, by_slots, by_rows, flat, square
):
    per, slots, entries = coup_ref.shape
    rank = out_ref.shape[1] // 2
    quarter = rank // 2
    pairs = entries // 128
    lane = lax.broadcasted_iota(jnp.int32, (pairs, 128), 1) // quarter

    def one(l, by_slot, by_row):
        wide = coup_ref[l].astype(F32)
        for k in range(pairs):
            by_slot[k * slots : (k + 1) * slots] = wide[:, k * 128 : (k + 1) * 128]
        rows = [by_slot[pl.ds(s, pairs, stride=slots)] for s in range(slots)]
        turned = [[rows[s] if t == 0 else pltpu.roll(rows[s], t * quarter, 1) for t in range(4)] for s in range(slots)]
        for half in range(2):
            for parity in range(2):
                chunk = 2 * parity + half
                for group in range(slots // 4):
                    out = turned[4 * group][(0 - chunk) % 4]
                    for r in range(1, 4):
                        out = jnp.where(lane == r, turned[4 * group + r][(r - chunk) % 4], out)
                    by_row[half, group, pl.ds(parity, pairs, stride=2)] = out
        for half in range(2):
            for group in range(slots // 4):
                out_ref[l, half * rank : (half + 1) * rank, group * 128 : (group + 1) * 128] = by_row[half, group].astype(BF16)

    def trip(i, carry):
        for u in range(by_slots.shape[0]):
            one(i * by_slots.shape[0] + u, by_slots.at[u], by_rows.at[u])
        return carry

    lax.fori_loop(0, per // by_slots.shape[0], trip, 0)
    build_lists(near_ref, lists, pos_ref[0], per // 2)
    cluster = pos_ref[0] // CDEV
    wide = coarse_ref[cluster].astype(F32)
    number = lax.broadcasted_iota(jnp.int32, wide.shape, 0)
    for at in range(coarse_out.shape[0]):
        row = jnp.sum(jnp.where(number == (cluster ^ (at + 1)), wide, 0.0), axis=0, keepdims=True)
        for k in range(pairs):
            flat[k : k + 1] = row[:, k * 128 : (k + 1) * 128]
        store_square(flat[...], square)
        coarse_out[at] = square[:, :rank].astype(BF16)


def prep_kernel(
    pos_ref, rs_hbm, sc_hbm, basis_hbm, transfer_hbm, e_hbm, v_ref, cp_ref, part_ref, trans_ref, mx_ref, mo_ref,
    rs_ref, sc_ref, basis_ref, transfer_ref, e_ref, points, coefs, by_leaf, squares, sems,
):
    per, rank, leaf = basis_ref.shape
    columns, features = rs_ref.shape[0], e_ref.shape[0]
    size = rank // 2
    groups = per // UNROLL
    width = UNROLL * leaf
    small = [
        pltpu.make_async_copy(transfer_hbm, transfer_ref, sems.at[0, 0]),
        pltpu.make_async_copy(sc_hbm, sc_ref, sems.at[0, 1]),
    ]
    copies = []
    for group in range(groups):
        cols, rows = pl.ds(group * width, width), pl.ds(group * UNROLL, UNROLL)
        copies.append([
            pltpu.make_async_copy(rs_hbm.at[:, cols], rs_ref.at[:, cols], sems.at[group + 1, 0]),
            pltpu.make_async_copy(basis_hbm.at[rows], basis_ref.at[rows], sems.at[group + 1, 1]),
            pltpu.make_async_copy(e_hbm.at[:, cols], e_ref.at[:, cols], sems.at[group + 1, 2]),
        ])
    for copy in small + sum(copies, []):
        copy.start()
    small[0].wait()
    wide = transfer_ref[...].astype(F32)
    for k in range(rank * rank // 128):
        by_leaf[k * per : (k + 1) * per] = wide[:, k * 128 : (k + 1) * 128]
    for at in range(per):
        store_square(by_leaf[pl.ds(at, rank * rank // 128, stride=per)], squares.at[at])
    trans_ref[...] = squares[:, :, :rank].astype(BF16)
    small[1].wait()

    def one(at):
        rounded = (rs_ref[:, at * leaf : (at + 1) * leaf] * sc_ref[:, at * leaf : (at + 1) * leaf]).astype(BF16)
        v_ref[at] = rounded
        here = e_ref[:, at * leaf : (at + 1) * leaf]
        high = here.astype(BF16)
        points[at, :features] = high
        points[at, features:] = (here - high.astype(F32)).astype(BF16)
        coef = leaf_coefficients(basis_ref[at], rounded)
        coefs[pl.ds(at * rank, rank)] = coef
        cp_ref[pl.ds(at * size, size)] = pack_pair(coef)

    for group in range(groups):
        for copy in copies[group]:
            copy.wait()
        for u in range(UNROLL):
            one(group * UNROLL + u)
    store_share(share_of(trans_ref[...], coefs[...]), part_ref, cp_ref)
    odd = pos_ref[0] % 2
    half = per // 2
    for ref, first in ((mx_ref, half * (1 - odd)), (mo_ref, half * odd)):
        ref[:, :columns] = v_ref[pl.ds(first, half)]
        ref[:, columns:] = points[pl.ds(first, half)]


def quad_kernel(pos_ref, own_ref, sib_ref, across_ref, both_ref, part_ref, *rest):
    quad_ref, sum_ref = rest[-2:]
    place = pos_ref[0] % 4
    rows = quad_ref.shape[1]
    size = part_ref.shape[0]
    quad_ref[place] = own_ref[:rows]
    total = part_ref[...]
    for flip, ref in ((1, sib_ref), (2, across_ref), (3, both_ref)):
        quad_ref[place ^ flip] = ref[:rows]
        for at in range(3):
            total += ref[rows + at * size : rows + (at + 1) * size].astype(F32)
    sum_ref[...] = total[None]


def build_lists(near_ref, lists, pos, half):
    slots = near_ref.shape[0] - 1
    per = near_ref.shape[1]
    base = pos * 2 * half - half
    odd = pos % 2 == 1

    def put(leaf, counts):
        for slot in range(slots):
            m = near_ref[1 + slot, leaf] - base
            own = (m >= half) & (m < 3 * half)
            low = (m < half) == odd
            value = (leaf << 16) | ((leaf * slots + slot) << 8) | m
            for kind, count in enumerate(counts):
                lists[kind, count] = value
            takes = (own, ~own & low, ~own & ~low, own | low)
            counts = tuple(count + jnp.where(take, 1, 0) for count, take in zip(counts, takes))
        return counts

    counts = lax.fori_loop(0, per, put, (0, 0, 0, 0))
    for kind, count in enumerate(counts):
        for u in range(UNROLL):
            lists[kind, count + u] = (per << 16) | ((per * slots) << 8) | half
        lists[kind, lists.shape[1] - 1] = count


def near_entry(lists, kind, at, half):
    value = lists[kind, at]
    leaf_at = value >> 16
    return (value >> 8) & 255, leaf_at, jnp.minimum(leaf_at, 2 * half - 1), value & 255


def self_kernel(e_ref, v_ref, wait_ref, self_ref, near_out, buffer, sems):
    per, _, leaf = v_ref.shape
    copies = []
    for at in range(per):
        points = e_ref[:, at * leaf : (at + 1) * leaf]
        tile = tile_of(other_rows(points), own_rows(points))
        buffer[at] = tile
        near_out[at] = dot(v_ref[at], tile, 1, 0)
        copies.append(pltpu.make_async_copy(buffer.at[at], self_ref.at[at], sems.at[at]))
        copies[-1].start()
    for copy in copies:
        copy.wait()


def points_of(ref, at, columns, features):
    high = ref[at, columns : columns + features].astype(F32)
    return high + ref[at, columns + features :].astype(F32)


def own_kernel(pos_ref, lists, e_ref, v_ref, vx_ref, near_in, wait_ref, tile_ref, near_out, vw):
    per, columns, leaf = v_ref.shape
    half = per // 2
    vw[:per] = v_ref[...]
    vw[per:] = vx_ref[:, :columns]
    n = lists[3, lists.shape[1] - 1]

    def trip(i, carry):
        for u in range(UNROLL):
            entry, leaf_at, row, m = near_entry(lists, 3, i * UNROLL + u, half)
            own = (m >= half) & (m < 3 * half)
            place = jnp.clip(m - half, 0, per - 1)
            points = jnp.where(
                own, columns_of(e_ref, place, leaf), points_of(vx_ref, m % half, columns, e_ref.shape[0])
            )
            tile = tile_of(other_rows(points), own_rows(columns_of(e_ref, row, leaf)))
            tile_ref[entry] = tile
            near_out[leaf_at] += dot(vw[jnp.where(own, place, per + m % half)], tile, 1, 0)
        return carry

    lax.fori_loop(0, (n + UNROLL - 1) // UNROLL, trip, 0)


def own_again_kernel(pos_ref, lists, v_ref, tile_ref, near_out):
    half = v_ref.shape[0] // 2
    near_out[...] = jnp.zeros_like(near_out)
    n = lists[0, lists.shape[1] - 1]

    def trip(i, carry):
        for u in range(UNROLL):
            entry, leaf_at, _, m = near_entry(lists, 0, i * UNROLL + u, half)
            place = jnp.clip(m - half, 0, 2 * half - 1)
            near_out[leaf_at] += dot(v_ref[place], tile_ref[entry], 1, 0)
        return carry

    lax.fori_loop(0, (n + UNROLL - 1) // UNROLL, trip, 0)


def self_again_kernel(
    pos_ref, lists, v_ref, vx_ref, tile_ref, self_hbm, near_in, wait_ref, near_out, self_ref, sems,
):
    per = v_ref.shape[0]
    half = per // 2
    copies = [
        pltpu.make_async_copy(self_hbm.at[pl.ds(at, UNROLL)], self_ref.at[pl.ds(at, UNROLL)], sems.at[at // UNROLL])
        for at in range(0, per, UNROLL)
    ]
    for copy in copies:
        copy.start()
    n = lists[1, lists.shape[1] - 1]

    def trip(i, carry):
        for u in range(UNROLL):
            entry, leaf_at, _, m = near_entry(lists, 1, i * UNROLL + u, half)
            near_out[leaf_at] += dot(vx_ref[m % half], tile_ref[entry], 1, 0)
        return carry

    lax.fori_loop(0, (n + UNROLL - 1) // UNROLL, trip, 0)
    for i, copy in enumerate(copies):
        copy.wait()
        for u in range(UNROLL):
            at = i * UNROLL + u
            near_out[at] += dot(v_ref[at], self_ref[at], 1, 0)


def load_coefficients(cw, sources):
    devices, rows, _ = sources[0].shape
    per = rows // cw.shape[1]
    for slot, source in enumerate(sources):
        for device in range(devices):
            for at in range(per):
                cw[(slot * devices + device) * per + at] = source[device, at * cw.shape[1] : (at + 1) * cw.shape[1]]


def coarse_rows(coarse_ref, sum_refs, fc):
    rank = coarse_ref.shape[1]
    acc = jnp.zeros((rank, rank), F32)
    for at in range(coarse_ref.shape[0]):
        packed = sum_refs[0][at]
        for ref in sum_refs[1:]:
            packed += ref[at]
        total = jnp.concatenate([packed[:, :rank], packed[:, rank:]], axis=0)
        for piece in split3(total):
            acc += dot(coarse_ref[at], piece, 1, 0)
    fc[...] = jnp.concatenate(split3(acc), axis=1)


def far_sum(l, pos, far_ref, cw, coup_ref, moved, basis_ref):
    per, rank, _ = basis_ref.shape
    odd = pos % 2
    picks = []
    for s in range(far_ref.shape[0]):
        leaf_id = far_ref[s, l]
        device = leaf_id // per
        gap = device // 4 - pos // 4
        slot = jnp.where(gap == 0, 0, jnp.where((gap < 0) == (odd == 0), 1, 2))
        picks.append(cw[(slot * 4 + device % 4) * per + leaf_id % per])
    wide = dot(coup_ref[l], jnp.concatenate(picks, axis=0), 1, 0)
    combined = wide[:rank, :rank] + wide[rank:, rank:] + moved
    return dot(combined.astype(BF16), basis_ref[l], 0, 0)


def store_moved(trans, fc, mv):
    count, rank, _ = trans.shape
    wide = dot(trans.reshape(count * rank, rank), fc[...], 1, 0)
    mv[...] = wide[:, :rank] + wide[:, rank : 2 * rank] + wide[:, 2 * rank :]


def foreign_kernel(pos_ref, lists, e_ref, vo_ref, tile_in, near_in, tile_ref, near_out):
    half, _, leaf = vo_ref.shape
    features = e_ref.shape[0]
    columns = vo_ref.shape[1] - 2 * features
    n = lists[2, lists.shape[1] - 1]

    def trip(i, carry):
        for u in range(UNROLL):
            entry, leaf_at, row, m = near_entry(lists, 2, i * UNROLL + u, half)
            points = points_of(vo_ref, m % half, columns, features)
            tile = tile_of(other_rows(points), own_rows(columns_of(e_ref, row, leaf)))
            tile_ref[entry] = tile
            near_out[leaf_at] += dot(vo_ref[m % half, :columns], tile, 1, 0)
        return carry

    lax.fori_loop(0, (n + UNROLL - 1) // UNROLL, trip, 0)


def far_first_kernel(
    pos_ref, far_ref, rs_ref, sc_ref, basis_ref, coup_ref, trans_ref, near_ref, coarse_ref, sum_a, sum_b, c0, c1, c2,
    u_ref, q_ref, cp_ref, part_ref, msg_ref, mx_ref, mo_ref, cw, fc, mv, coefs, acc_uu, acc_ru,
):
    per, rank, leaf = basis_ref.shape
    half = per // 2
    size = rank // 2
    pos = pos_ref[0]
    odd = pos % 2
    load_coefficients(cw, (c0, c1, c2))
    coarse_rows(coarse_ref, (sum_a, sum_b), fc)
    store_moved(trans_ref[...], fc, mv)
    acc_uu[...] = jnp.zeros_like(acc_uu)
    acc_ru[...] = jnp.zeros_like(acc_ru)

    def one(l):
        rows = pl.ds(pl.multiple_of(l * rank, rank), rank)
        far = far_sum(l, pos, far_ref, cw, coup_ref, mv[rows], basis_ref)
        right = columns_of(rs_ref, l, leaf)
        scale = columns_of(sc_ref, l, leaf)
        image = RIDGE_TERM * (right * scale) + (near_ref[l] + far)
        u_ref[:, pl.ds(pl.multiple_of(l * leaf, leaf), leaf)] = image
        acc_uu[...] += lane_groups(image * image)
        acc_ru[...] += lane_groups(right * image)
        rounded = (image * scale).astype(BF16)
        q_ref[l] = rounded
        coef = leaf_coefficients(basis_ref[l], rounded)
        coefs[rows] = coef
        cp_ref[pl.ds(pl.multiple_of(l * size, size), size)] = pack_pair(coef)

    leaf_loop(per, FAR_UNROLL, one)
    store_share(share_of(trans_ref[...], coefs[...]), part_ref, cp_ref)
    mx_ref[...] = q_ref[pl.ds(half * (1 - odd), half)]
    mo_ref[...] = q_ref[pl.ds(half * odd, half)]
    lane = lax.broadcasted_iota(jnp.int32, msg_ref.shape, 1)
    out = jnp.where(lane == 0, jnp.sum(acc_uu[...], axis=1, keepdims=True), 0.0)
    msg_ref[...] = jnp.where(lane == 1, jnp.sum(acc_ru[...], axis=1, keepdims=True), out)


def near_again_kernel(pos_ref, lists, vo_ref, tile_ref, near_in, near_out):
    half = vo_ref.shape[0]
    n = lists[2, lists.shape[1] - 1]

    def trip(i, carry):
        for u in range(UNROLL):
            entry, leaf_at, _, m = near_entry(lists, 2, i * UNROLL + u, half)
            near_out[leaf_at] += dot(vo_ref[m % half], tile_ref[entry], 1, 0)
        return carry

    lax.fori_loop(0, (n + UNROLL - 1) // UNROLL, trip, 0)


def far_again_kernel(
    pos_ref, far_ref, rs_ref, sc_ref, u_ref, basis_ref, coup_ref, trans_ref,
    coarse_ref, sum_a, sum_b, c0, c1, c2, near_ref, prev_ref, w_ref, msg_ref,
    cw, fc, mv, acc_uw, acc_ww, acc_rw,
):
    per, rank, leaf = basis_ref.shape
    pos = pos_ref[0]
    load_coefficients(cw, (c0, c1, c2))
    coarse_rows(coarse_ref, (sum_a, sum_b), fc)
    store_moved(trans_ref[...], fc, mv)
    for acc in (acc_uw, acc_ww, acc_rw):
        acc[...] = jnp.zeros_like(acc)

    def one(l):
        far = far_sum(l, pos, far_ref, cw, coup_ref, mv[pl.ds(pl.multiple_of(l * rank, rank), rank)], basis_ref)
        image = columns_of(u_ref, l, leaf)
        second = RIDGE_TERM * (image * columns_of(sc_ref, l, leaf)) + (near_ref[l] + far)
        w_ref[:, pl.ds(pl.multiple_of(l * leaf, leaf), leaf)] = second
        acc_uw[...] += lane_groups(image * second)
        acc_ww[...] += lane_groups(second * second)
        acc_rw[...] += lane_groups(columns_of(rs_ref, l, leaf) * second)

    leaf_loop(per, FAR_UNROLL, one)
    lane = lax.broadcasted_iota(jnp.int32, msg_ref.shape, 1)
    out = prev_ref[...]
    for at, acc in enumerate((acc_uw, acc_ww, acc_rw)):
        out = jnp.where(lane == 2 + at, jnp.sum(acc[...], axis=1, keepdims=True), out)
    msg_ref[...] = out


def call(kernel, name, in_specs, out_shape, scratch, args, aliases=None, flops=0, out_specs=None, limit=VMEM_LIMIT):
    return pl.pallas_call(
        kernel,
        in_specs=in_specs,
        out_specs=out_specs or [WHOLE] * len(out_shape),
        out_shape=out_shape,
        scratch_shapes=scratch,
        input_output_aliases=aliases or {},
        compiler_params=pltpu.CompilerParams(vmem_limit_bytes=limit),
        cost_estimate=pl.CostEstimate(flops=flops, bytes_accessed=0, transcendentals=0),
        name=name,
    )(*args)


def two_clusters():
    return CDEV == 8 and lax.axis_size("leaf") == 2 * CDEV


def other_clusters(plane_sum):
    count = lax.axis_size("leaf")
    if two_clusters():
        return involution(plane_sum, lambda i: i ^ (12 if i % 2 else 8))
    mask = 4
    while mask < CDEV:
        plane_sum = plane_sum + involution(plane_sum, lambda i: i ^ mask)
        mask *= 2
    sums = plane_sum
    while mask < count:
        sums = jnp.concatenate([sums, involution(sums, lambda i: i ^ mask)], axis=0)
        mask *= 2
    return sums[1:]


def pass_kernel(*refs):
    pass


def after(values, *before):
    return call(
        pass_kernel, "after", [WHOLE] * len(values) + [ANYWHERE] * len(before),
        [pltpu.VMEM(value.shape, value.dtype) for value in values], [], (*values, *before),
        aliases={at: at for at in range(len(values))},
    )


def first_messages(cp):
    return sibling(cp), across(cp)


def second_messages(position, cp, got, part, *before):
    rows = cp.shape[0] - 3 * part.shape[0]
    got = (*got, sibling(got[1]))
    quad, plane_sum = call(
        quad_kernel, "quad", [SCALAR] + [WHOLE] * 5 + [ANYWHERE] * len(before),
        [pltpu.VMEM((4, rows, cp.shape[1]), BF16), pltpu.VMEM((1,) + part.shape, F32)],
        [], (position, cp, *got, part, *before),
    )
    return quad, two_chips(quad), other_clusters(plane_sum)


def last_messages(quad, mine):
    other = sibling(mine) if two_clusters() else jnp.zeros_like(mine)
    return (quad, sibling(quad)), (mine, other)


def body(
    right_side, scaling, embeddings, near_leaves, far_leaves, leaf_basis, leaf_coupling,
    transfer, coarse_coupling,
):
    columns, local_points = right_side.shape
    per, rank, leaf = leaf_basis.shape
    features = embeddings.shape[0]
    slots = near_leaves.shape[1] - 1
    far_count = far_leaves.shape[1]
    half = per // 2
    size = rank // 2
    count = lax.axis_size("leaf")
    pos = lax.axis_index("leaf")
    position = pos.reshape(1).astype(jnp.int32)
    near_rows = near_leaves.T
    far_rows = far_leaves.T
    coarse_count = count // CDEV

    scale_row = scaling.reshape(1, local_points)
    leaf_shape = pltpu.VMEM((per, columns, leaf), BF16)
    cp_shape = pltpu.VMEM((per * size + 3 * size, 2 * columns), BF16)
    part_shape = pltpu.VMEM((size, 2 * columns), F32)
    self_shape = pltpu.HBM((8 * per, leaf, leaf), BF16)
    trans_shape = pltpu.VMEM((per, rank, rank), BF16)
    half_shape = pltpu.VMEM((half, columns, leaf), BF16)
    moved_shape = pltpu.VMEM((per * rank, columns), F32)
    tile_shape = pltpu.VMEM((per * slots + 1, leaf, leaf), BF16)
    near_shape = pltpu.VMEM((per + 1, columns, leaf), F32)
    wide_shape = pltpu.VMEM((columns, local_points), F32)
    msg_shape = pltpu.VMEM((columns, 128), F32)
    coefs_shape = pltpu.VMEM((per * rank, columns), BF16)
    acc_shape = pltpu.VMEM((columns, 128), F32)
    window = [
        pltpu.VMEM((12 * per, size, 2 * columns), BF16),
        pltpu.VMEM((rank, 3 * columns), BF16),
    ]

    both_shape = pltpu.VMEM((half, columns + 2 * features, leaf), BF16)
    v, cp, part, trans, mx, mo = call(
        prep_kernel, "prep", [SCALAR] + [OUTSIDE] * 5,
        [leaf_shape, cp_shape, part_shape, trans_shape, both_shape, both_shape],
        [pltpu.VMEM(right_side.shape, F32), pltpu.VMEM(scale_row.shape, F32), pltpu.VMEM(leaf_basis.shape, BF16),
         pltpu.VMEM(transfer.shape, BF16), pltpu.VMEM(embeddings.shape, F32),
         pltpu.VMEM((per, 2 * features, leaf), BF16), coefs_shape, pltpu.VMEM((per * rank * rank // 128, 128), F32), pltpu.VMEM((per, rank, 128), F32), pltpu.SemaphoreType.DMA((per // UNROLL + 1, 3))],
        (position, right_side, scale_row, leaf_basis, transfer, embeddings), limit=WIDE_LIMIT,
    )
    got = first_messages(cp)
    coup, coarse, lists = call(
        relayout_kernel, "relayout", [SCALAR] * 2 + [WHOLE] * 2 + [ANYWHERE],
        [pltpu.VMEM((per, 2 * rank, far_count * size), BF16), pltpu.VMEM((coarse_count - 1, rank, rank), BF16),
         jax.ShapeDtypeStruct((4, per * slots + 2 * UNROLL), jnp.int32)],
        [
            pltpu.VMEM((RELAY_UNROLL, far_count * rank * rank // 128, 128), F32),
            pltpu.VMEM((RELAY_UNROLL, 2, far_count // 4, rank, 128), F32),
            pltpu.VMEM((size, 128), F32), pltpu.VMEM((rank, 128), F32),
        ],
        (position, near_rows, leaf_coupling, coarse_coupling, cp), out_specs=[WHOLE, WHOLE, SCALAR],
    )
    across_cp, mo, mx = after((got[1], mo, mx), coup)
    got = (got[0], across_cp)
    vo = beside(mo)
    vx = sibling(mx)
    tself, near = call(
        self_kernel, "self_tiles", [WHOLE] * 2 + [ANYWHERE], [self_shape, near_shape],
        [pltpu.VMEM((per, leaf, leaf), BF16), pltpu.SemaphoreType.DMA((per,))],
        (embeddings, v, mo), out_specs=[OUTSIDE, WHOLE],
    )
    quad, far_quad, mine = second_messages(position, cp, got, part, near)
    tiles, near = call(
        own_kernel, "own_tiles", [SCALAR] * 2 + [WHOLE] * 4 + [ANYWHERE], [tile_shape, near_shape],
        [pltpu.VMEM((per + half, columns, leaf), BF16)],
        (position, lists, embeddings, v, vx, near, quad), aliases={5: 1},
    )
    coefs, sums = last_messages(*after((far_quad, mine), near))
    tiles, near = call(
        foreign_kernel, "foreign_tiles", [SCALAR] * 2 + [WHOLE] * 4, [tile_shape, near_shape], [],
        (position, lists, embeddings, vo, tiles, near), aliases={4: 0, 5: 1},
    )
    image, q, cp, part, msg, mx, mo = call(
        far_first_kernel, "far_first", [SCALAR] * 2 + [WHOLE] * 12,
        [wide_shape, leaf_shape, cp_shape, part_shape, msg_shape, half_shape, half_shape],
        [*window, moved_shape, coefs_shape, acc_shape, acc_shape],
        (position, far_rows, right_side, scale_row, leaf_basis, coup, trans, near, coarse, *sums, quad, *coefs),
    )
    got = first_messages(cp)
    (near,) = call(
        own_again_kernel, "own_again", [SCALAR] * 2 + [WHOLE] * 2, [near_shape], [],
        (position, lists, q, tiles),
    )
    across_cp, mo = after((got[1], mo), near)
    got = (got[0], across_cp)
    vo = beside(mo)
    quad, far_quad, mine = second_messages(position, cp, got, part)
    vx = sibling(mx)
    (near,) = call(
        self_again_kernel, "self_again", [SCALAR] * 2 + [WHOLE] * 3 + [OUTSIDE, WHOLE, ANYWHERE], [near_shape],
        [pltpu.VMEM((per, leaf, leaf), BF16), pltpu.SemaphoreType.DMA((per // UNROLL,))],
        (position, lists, q, vx, tiles, tself, near, quad), aliases={6: 0},
    )
    coefs, sums = last_messages(*after((far_quad, mine), near, vo))
    (near,) = call(
        near_again_kernel, "near_again", [SCALAR] * 2 + [WHOLE] * 3, [near_shape], [],
        (position, lists, vo, tiles, near), aliases={4: 0},
    )
    second, msg = call(
        far_again_kernel, "far_again", [SCALAR] * 2 + [WHOLE] * 14, [wide_shape, msg_shape],
        window + [moved_shape] + [acc_shape] * 3,
        (position, far_rows, right_side, scale_row, image, leaf_basis, coup, trans,
         coarse, *sums, quad, *coefs, near, msg),
    )

    mask = 1
    while mask < count:
        msg = msg + involution(msg, lambda i: i ^ mask)
        mask *= 2
    uu, ru, uw, ww, rw = [msg[:, k : k + 1] for k in range(5)]
    step_one = ru / (uu + EPSILON)
    beta = -(uu - step_one * uw) / (uu + EPSILON)
    lead = 1.0 + beta
    curvature = lead * lead * uu - 2.0 * lead * step_one * uw + step_one * step_one * ww
    aligned = lead * (ru - step_one * uu) - step_one * (rw - step_one * uw)
    step_two = aligned / (curvature + EPSILON)
    first_weight = step_one + step_two * lead
    second_weight = step_two * step_one
    solution = scale_row * (first_weight * right_side - second_weight * image)
    residual = right_side - first_weight * image + second_weight * second
    return (solution, residual)


def solution(mesh):
    return jax.shard_map(
        body,
        mesh=mesh,
        in_specs=(
            P(None, ("groups", "leaf")),
            P(("groups", "leaf")),
            P(None, ("groups", "leaf")),
            P(("groups", "leaf"), None),
            P(("groups", "leaf"), None),
            P(("groups", "leaf"), None, None),
            P(("groups", "leaf"), None, None),
            P(("groups", "leaf"), None),
            P("groups", None, None),
        ),
        out_specs=(P(None, ("groups", "leaf")), P(None, ("groups", "leaf"))),
        check_vma=False,
    )
```

```python
import math

import jax
import jax.numpy as jnp
from jax import lax
from jax.experimental import pallas as pl
from jax.experimental.pallas import tpu as pltpu
from jax.sharding import PartitionSpec as P

FARDEV = 4
CDEV = 8
KERNEL_SCALE = 0.0625
RIDGE_TERM = 1.0
EPSILON = 1e-06
F32 = jnp.float32
BF16 = jnp.bfloat16
HALF_SCALE = math.sqrt(2.0 * KERNEL_SCALE * math.log2(math.e))
UNROLL = 4
FAR_UNROLL = 16
RELAY_UNROLL = 4
VMEM_LIMIT = 13 * 1024 * 1024
WIDE_LIMIT = 54 * 1024 * 1024
SELF_LIMIT = 28 * 1024 * 1024
WHOLE = pl.BlockSpec(memory_space=pltpu.VMEM)
ANYWHERE = pl.BlockSpec(memory_space=pl.ANY)
OUTSIDE = pl.BlockSpec(memory_space=pltpu.HBM)
SCALAR = pl.BlockSpec(memory_space=pltpu.SMEM)


def involution(value, partner):
    count = lax.axis_size("leaf")
    pairs = [(i, partner(i)) for i in range(count) if 0 <= partner(i) < count]
    return lax.ppermute(value, "leaf", pairs)


def sibling(value):
    return involution(value, lambda i: i ^ 1)


def beside(value):
    return involution(value, lambda i: i + 1 if i % 2 else i - 1)


def across(value):
    return involution(value, lambda i: i ^ 2)


def two_chips(value):
    return involution(value, lambda i: i + 3 if i % 2 else i - 3)


def dot(a, b, ca, cb):
    return lax.dot_general(a, b, (((ca,), (cb,)), ((), ())), preferred_element_type=F32)


def split3(value):
    high = value.astype(BF16)
    rest = value - high.astype(F32)
    mid = rest.astype(BF16)
    low = (rest - mid.astype(F32)).astype(BF16)
    return high, mid, low


def point_pieces(points):
    scaled = points * HALF_SCALE
    high, mid, low = split3(scaled)
    square = 0.5 * jnp.sum(scaled * scaled, axis=0, keepdims=True)
    s_high, s_mid, s_low = split3(square)
    return high, mid, low, s_high.astype(F32), s_mid.astype(F32), s_low.astype(F32)


def norm_rows(first, second, third, width, swap, sign):
    row = lax.broadcasted_iota(jnp.int32, (16, width), 0)
    base = 3 if swap else 0
    ones = 0 if swap else 3
    out = jnp.where((row >= ones) & (row < ones + 3), sign, 0.0)
    for at, piece in enumerate((first, second, third)):
        out = jnp.where(row == base + at, sign * piece, out)
    return out.astype(BF16)


def own_rows(points):
    high, mid, low, a, b, c = point_pieces(points)
    norms = norm_rows(a, b, c, points.shape[1], False, 1.0)
    return jnp.concatenate([high, mid, high, mid, low, high, norms], axis=0)


def other_rows(points):
    high, mid, low, a, b, c = point_pieces(points)
    norms = norm_rows(a, b, c, points.shape[1], True, -1.0)
    return jnp.concatenate([high, high, mid, mid, high, low, norms], axis=0)


def tile_of(other, own):
    return jnp.exp2(dot(other, own, 0, 0)).astype(BF16)


def pack_pair(block):
    half = block.shape[0] // 2
    return jnp.concatenate([block[:half], block[half:]], axis=1)


def lane_groups(value):
    total = value[:, :128]
    for at in range(128, value.shape[1], 128):
        total += value[:, at : at + 128]
    return total


def as_rows(parts, first, count):
    lane = lax.broadcasted_iota(jnp.int32, parts[0].shape, 1)
    out = jnp.zeros(parts[0].shape, F32)
    for at, part in enumerate(parts):
        out = jnp.where(lane == first + at, jnp.sum(part[...], axis=1, keepdims=True), out)
    return out.T[:count]


def leaf_coefficients(basis, rounded):
    return dot(basis, rounded, 1, 1).astype(BF16)


def share_of(trans, coefs):
    count, rank, _ = trans.shape
    return dot(trans.reshape(count * rank, rank), coefs, 0, 0)


def columns_of(ref, at, width):
    return ref[:, pl.ds(pl.multiple_of(at * width, width), width)]


def leaf_loop(count, unroll, fn):
    def trip(i, carry):
        for u in range(unroll):
            fn(i * unroll + u)
        return carry

    lax.fori_loop(0, count // unroll, trip, 0)


def store_share(total, part_ref, cp_ref):
    packed = pack_pair(total)
    part_ref[...] = packed
    size = packed.shape[0]
    rows = cp_ref.shape[0] - 3 * size
    for at, piece in enumerate(split3(packed)):
        cp_ref[rows + at * size : rows + (at + 1) * size] = piece


def store_square(flat, target):
    pairs = flat.shape[0]
    target[pl.ds(0, pairs, stride=2)] = flat
    target[pl.ds(1, pairs, stride=2)] = pltpu.roll(flat, 64, 1)


def relayout_kernel(
    pos_ref, near_ref, coup_ref, coarse_ref, wait_ref, out_ref, coarse_out, lists, by_slots, by_rows, flat, square
):
    per, slots, entries = coup_ref.shape
    rank = out_ref.shape[1] // 2
    quarter = rank // 2
    pairs = entries // 128
    lane = lax.broadcasted_iota(jnp.int32, (pairs, 128), 1) // quarter

    def one(l, by_slot, by_row):
        wide = coup_ref[l].astype(F32)
        for k in range(pairs):
            by_slot[k * slots : (k + 1) * slots] = wide[:, k * 128 : (k + 1) * 128]
        rows = [by_slot[pl.ds(s, pairs, stride=slots)] for s in range(slots)]
        turned = [[rows[s] if t == 0 else pltpu.roll(rows[s], t * quarter, 1) for t in range(4)] for s in range(slots)]
        for half in range(2):
            for parity in range(2):
                chunk = 2 * parity + half
                for group in range(slots // 4):
                    out = turned[4 * group][(0 - chunk) % 4]
                    for r in range(1, 4):
                        out = jnp.where(lane == r, turned[4 * group + r][(r - chunk) % 4], out)
                    by_row[half, group, pl.ds(parity, pairs, stride=2)] = out
        for half in range(2):
            for group in range(slots // 4):
                out_ref[l, half * rank : (half + 1) * rank, group * 128 : (group + 1) * 128] = by_row[half, group].astype(BF16)

    def trip(i, carry):
        for u in range(by_slots.shape[0]):
            one(i * by_slots.shape[0] + u, by_slots.at[u], by_rows.at[u])
        return carry

    lax.fori_loop(0, per // by_slots.shape[0], trip, 0)
    build_lists(near_ref, lists, pos_ref[0], per // 2)
    cluster = pos_ref[0] // CDEV
    wide = coarse_ref[cluster].astype(F32)
    number = lax.broadcasted_iota(jnp.int32, wide.shape, 0)
    for at in range(coarse_out.shape[0]):
        row = jnp.sum(jnp.where(number == (cluster ^ (at + 1)), wide, 0.0), axis=0, keepdims=True)
        for k in range(pairs):
            flat[k : k + 1] = row[:, k * 128 : (k + 1) * 128]
        store_square(flat[...], square)
        coarse_out[at] = square[:, :rank].astype(BF16)


def prep_kernel(
    pos_ref, rs_hbm, sc_hbm, basis_hbm, transfer_hbm, e_hbm, v_ref, cp_ref, part_ref, trans_ref, mx_ref, mo_ref,
    rs_ref, sc_ref, basis_ref, transfer_ref, e_ref, points, coefs, by_leaf, squares, sems,
):
    per, rank, leaf = basis_ref.shape
    columns, features = rs_ref.shape[0], e_ref.shape[0]
    size = rank // 2
    groups = per // UNROLL
    width = UNROLL * leaf
    small = [
        pltpu.make_async_copy(transfer_hbm, transfer_ref, sems.at[0, 0]),
        pltpu.make_async_copy(sc_hbm, sc_ref, sems.at[0, 1]),
    ]
    copies = []
    for group in range(groups):
        cols, rows = pl.ds(group * width, width), pl.ds(group * UNROLL, UNROLL)
        copies.append([
            pltpu.make_async_copy(rs_hbm.at[:, cols], rs_ref.at[:, cols], sems.at[group + 1, 0]),
            pltpu.make_async_copy(basis_hbm.at[rows], basis_ref.at[rows], sems.at[group + 1, 1]),
            pltpu.make_async_copy(e_hbm.at[:, cols], e_ref.at[:, cols], sems.at[group + 1, 2]),
        ])
    for copy in small + sum(copies, []):
        copy.start()
    small[0].wait()
    wide = transfer_ref[...].astype(F32)
    for k in range(rank * rank // 128):
        by_leaf[k * per : (k + 1) * per] = wide[:, k * 128 : (k + 1) * 128]
    for at in range(per):
        store_square(by_leaf[pl.ds(at, rank * rank // 128, stride=per)], squares.at[at])
    trans_ref[...] = squares[:, :, :rank].astype(BF16)
    small[1].wait()

    def one(at):
        rounded = (rs_ref[:, at * leaf : (at + 1) * leaf] * sc_ref[:, at * leaf : (at + 1) * leaf]).astype(BF16)
        v_ref[at] = rounded
        here = e_ref[:, at * leaf : (at + 1) * leaf]
        high = here.astype(BF16)
        points[at, :features] = high
        points[at, features:] = (here - high.astype(F32)).astype(BF16)
        coef = leaf_coefficients(basis_ref[at], rounded)
        coefs[pl.ds(at * rank, rank)] = coef
        cp_ref[pl.ds(at * size, size)] = pack_pair(coef)

    for group in range(groups):
        for copy in copies[group]:
            copy.wait()
        for u in range(UNROLL):
            one(group * UNROLL + u)
    store_share(share_of(trans_ref[...], coefs[...]), part_ref, cp_ref)
    odd = pos_ref[0] % 2
    half = per // 2
    for ref, first in ((mx_ref, half * (1 - odd)), (mo_ref, half * odd)):
        ref[:, :columns] = v_ref[pl.ds(first, half)]
        ref[:, columns:] = points[pl.ds(first, half)]


def quad_kernel(pos_ref, own_ref, sib_ref, across_ref, both_ref, part_ref, *rest):
    quad_ref, sum_ref = rest[-2:]
    place = pos_ref[0] % 4
    rows = quad_ref.shape[1]
    size = part_ref.shape[0]
    quad_ref[place] = own_ref[:rows]
    total = part_ref[...]
    for flip, ref in ((1, sib_ref), (2, across_ref), (3, both_ref)):
        quad_ref[place ^ flip] = ref[:rows]
        for at in range(3):
            total += ref[rows + at * size : rows + (at + 1) * size].astype(F32)
    sum_ref[...] = total[None]


def build_lists(near_ref, lists, pos, half):
    slots = near_ref.shape[0] - 1
    per = near_ref.shape[1]
    base = pos * 2 * half - half
    odd = pos % 2 == 1

    def put(leaf, counts):
        for slot in range(slots):
            m = near_ref[1 + slot, leaf] - base
            own = (m >= half) & (m < 3 * half)
            low = (m < half) == odd
            value = (leaf << 16) | ((leaf * slots + slot) << 8) | m
            for kind, count in enumerate(counts):
                lists[kind, count] = value
            takes = (own, ~own & low, ~own & ~low, own | low)
            counts = tuple(count + jnp.where(take, 1, 0) for count, take in zip(counts, takes))
        return counts

    counts = lax.fori_loop(0, per, put, (0, 0, 0, 0))
    for kind, count in enumerate(counts):
        for u in range(UNROLL):
            lists[kind, count + u] = (per << 16) | ((per * slots) << 8) | half
        lists[kind, lists.shape[1] - 1] = count


def near_entry(lists, kind, at, half):
    value = lists[kind, at]
    leaf_at = value >> 16
    return (value >> 8) & 255, leaf_at, jnp.minimum(leaf_at, 2 * half - 1), value & 255


def self_kernel(e_ref, v_ref, wait_ref, self_ref, near_out, buffer, sems):
    per, _, leaf = v_ref.shape
    copies = []
    for at in range(per):
        points = e_ref[:, at * leaf : (at + 1) * leaf]
        tile = tile_of(other_rows(points), own_rows(points))
        buffer[at] = tile
        near_out[at] = dot(v_ref[at], tile, 1, 0)
        copies.append(pltpu.make_async_copy(buffer.at[at], self_ref.at[at], sems.at[at]))
        copies[-1].start()
    for copy in copies:
        copy.wait()


def points_of(ref, at, columns, features):
    high = ref[at, columns : columns + features].astype(F32)
    return high + ref[at, columns + features :].astype(F32)


def own_kernel(pos_ref, lists, e_ref, v_ref, vx_ref, near_in, wait_ref, tile_ref, near_out, vw):
    per, columns, leaf = v_ref.shape
    half = per // 2
    vw[:per] = v_ref[...]
    vw[per:] = vx_ref[:, :columns]
    n = lists[3, lists.shape[1] - 1]

    def trip(i, carry):
        for u in range(UNROLL):
            entry, leaf_at, row, m = near_entry(lists, 3, i * UNROLL + u, half)
            own = (m >= half) & (m < 3 * half)
            place = jnp.clip(m - half, 0, per - 1)
            points = jnp.where(
                own, columns_of(e_ref, place, leaf), points_of(vx_ref, m % half, columns, e_ref.shape[0])
            )
            tile = tile_of(other_rows(points), own_rows(columns_of(e_ref, row, leaf)))
            tile_ref[entry] = tile
            near_out[leaf_at] += dot(vw[jnp.where(own, place, per + m % half)], tile, 1, 0)
        return carry

    lax.fori_loop(0, (n + UNROLL - 1) // UNROLL, trip, 0)


def own_again_kernel(pos_ref, lists, v_ref, tile_ref, near_out):
    half = v_ref.shape[0] // 2
    near_out[...] = jnp.zeros_like(near_out)
    n = lists[0, lists.shape[1] - 1]

    def trip(i, carry):
        for u in range(UNROLL):
            entry, leaf_at, _, m = near_entry(lists, 0, i * UNROLL + u, half)
            place = jnp.clip(m - half, 0, 2 * half - 1)
            near_out[leaf_at] += dot(v_ref[place], tile_ref[entry], 1, 0)
        return carry

    lax.fori_loop(0, (n + UNROLL - 1) // UNROLL, trip, 0)


def self_again_kernel(
    pos_ref, lists, v_ref, vx_ref, tile_ref, self_hbm, near_in, wait_ref, near_out, self_ref, sems,
):
    per = v_ref.shape[0]
    half = per // 2
    copies = [
        pltpu.make_async_copy(self_hbm.at[pl.ds(at, UNROLL)], self_ref.at[pl.ds(at, UNROLL)], sems.at[at // UNROLL])
        for at in range(0, per, UNROLL)
    ]
    for copy in copies:
        copy.start()
    n = lists[1, lists.shape[1] - 1]

    def trip(i, carry):
        for u in range(UNROLL):
            entry, leaf_at, _, m = near_entry(lists, 1, i * UNROLL + u, half)
            near_out[leaf_at] += dot(vx_ref[m % half], tile_ref[entry], 1, 0)
        return carry

    lax.fori_loop(0, (n + UNROLL - 1) // UNROLL, trip, 0)
    for i, copy in enumerate(copies):
        copy.wait()
        for u in range(UNROLL):
            at = i * UNROLL + u
            near_out[at] += dot(v_ref[at], self_ref[at], 1, 0)


def load_coefficients(cw, sources):
    devices, rows, _ = sources[0].shape
    per = rows // cw.shape[1]
    for slot, source in enumerate(sources):
        for device in range(devices):
            for at in range(per):
                cw[(slot * devices + device) * per + at] = source[device, at * cw.shape[1] : (at + 1) * cw.shape[1]]


def coarse_rows(coarse_ref, sum_refs, fc):
    rank = coarse_ref.shape[1]
    acc = jnp.zeros((rank, rank), F32)
    for at in range(coarse_ref.shape[0]):
        packed = sum_refs[0][at]
        for ref in sum_refs[1:]:
            packed += ref[at]
        total = jnp.concatenate([packed[:, :rank], packed[:, rank:]], axis=0)
        for piece in split3(total):
            acc += dot(coarse_ref[at], piece, 1, 0)
    fc[...] = jnp.concatenate(split3(acc), axis=1)


def far_sum(l, pos, far_ref, cw, coup_ref, moved, basis_ref):
    per, rank, _ = basis_ref.shape
    odd = pos % 2
    picks = []
    for s in range(far_ref.shape[0]):
        leaf_id = far_ref[s, l]
        device = leaf_id // per
        gap = device // 4 - pos // 4
        slot = jnp.where(gap == 0, 0, jnp.where((gap < 0) == (odd == 0), 1, 2))
        picks.append(cw[(slot * 4 + device % 4) * per + leaf_id % per])
    wide = dot(coup_ref[l], jnp.concatenate(picks, axis=0), 1, 0)
    combined = wide[:rank, :rank] + wide[rank:, rank:] + moved
    return dot(combined.astype(BF16), basis_ref[l], 0, 0)


def store_moved(trans, fc, mv):
    count, rank, _ = trans.shape
    wide = dot(trans.reshape(count * rank, rank), fc[...], 1, 0)
    mv[...] = wide[:, :rank] + wide[:, rank : 2 * rank] + wide[:, 2 * rank :]


def foreign_kernel(pos_ref, lists, e_ref, vo_ref, tile_in, near_in, tile_ref, near_out):
    half, _, leaf = vo_ref.shape
    features = e_ref.shape[0]
    columns = vo_ref.shape[1] - 2 * features
    n = lists[2, lists.shape[1] - 1]

    def trip(i, carry):
        for u in range(UNROLL):
            entry, leaf_at, row, m = near_entry(lists, 2, i * UNROLL + u, half)
            points = points_of(vo_ref, m % half, columns, features)
            tile = tile_of(other_rows(points), own_rows(columns_of(e_ref, row, leaf)))
            tile_ref[entry] = tile
            near_out[leaf_at] += dot(vo_ref[m % half, :columns], tile, 1, 0)
        return carry

    lax.fori_loop(0, (n + UNROLL - 1) // UNROLL, trip, 0)


def far_first_kernel(
    pos_ref, far_ref, rs_ref, sc_ref, basis_ref, coup_ref, trans_ref, near_ref, coarse_ref, sum_a, sum_b, c0, c1, c2,
    u_ref, q_ref, cp_ref, part_ref, msg_ref, mx_ref, mo_ref, cw, fc, mv, coefs, acc_uu, acc_ru,
):
    per, rank, leaf = basis_ref.shape
    half = per // 2
    size = rank // 2
    pos = pos_ref[0]
    odd = pos % 2
    load_coefficients(cw, (c0, c1, c2))
    coarse_rows(coarse_ref, (sum_a, sum_b), fc)
    store_moved(trans_ref[...], fc, mv)
    acc_uu[...] = jnp.zeros_like(acc_uu)
    acc_ru[...] = jnp.zeros_like(acc_ru)

    def one(l):
        rows = pl.ds(pl.multiple_of(l * rank, rank), rank)
        far = far_sum(l, pos, far_ref, cw, coup_ref, mv[rows], basis_ref)
        right = columns_of(rs_ref, l, leaf)
        scale = columns_of(sc_ref, l, leaf)
        image = RIDGE_TERM * (right * scale) + (near_ref[l] + far)
        u_ref[:, pl.ds(pl.multiple_of(l * leaf, leaf), leaf)] = image
        acc_uu[...] += lane_groups(image * image)
        acc_ru[...] += lane_groups(right * image)
        rounded = (image * scale).astype(BF16)
        q_ref[l] = rounded
        coef = leaf_coefficients(basis_ref[l], rounded)
        coefs[rows] = coef
        cp_ref[pl.ds(pl.multiple_of(l * size, size), size)] = pack_pair(coef)

    leaf_loop(per, FAR_UNROLL, one)
    store_share(share_of(trans_ref[...], coefs[...]), part_ref, cp_ref)
    mx_ref[...] = q_ref[pl.ds(half * (1 - odd), half)]
    mo_ref[...] = q_ref[pl.ds(half * odd, half)]
    msg_ref[...] = as_rows((acc_uu, acc_ru), 0, msg_ref.shape[0])


def near_again_kernel(pos_ref, lists, vo_ref, tile_ref, near_in, near_out):
    half = vo_ref.shape[0]
    n = lists[2, lists.shape[1] - 1]

    def trip(i, carry):
        for u in range(UNROLL):
            entry, leaf_at, _, m = near_entry(lists, 2, i * UNROLL + u, half)
            near_out[leaf_at] += dot(vo_ref[m % half], tile_ref[entry], 1, 0)
        return carry

    lax.fori_loop(0, (n + UNROLL - 1) // UNROLL, trip, 0)


def far_again_kernel(
    pos_ref, far_ref, rs_ref, sc_ref, u_ref, basis_ref, coup_ref, trans_ref,
    coarse_ref, sum_a, sum_b, c0, c1, c2, near_ref, prev_ref, w_ref, msg_ref,
    cw, fc, mv, acc_uw, acc_ww, acc_rw,
):
    per, rank, leaf = basis_ref.shape
    pos = pos_ref[0]
    load_coefficients(cw, (c0, c1, c2))
    coarse_rows(coarse_ref, (sum_a, sum_b), fc)
    store_moved(trans_ref[...], fc, mv)
    for acc in (acc_uw, acc_ww, acc_rw):
        acc[...] = jnp.zeros_like(acc)

    def one(l):
        far = far_sum(l, pos, far_ref, cw, coup_ref, mv[pl.ds(pl.multiple_of(l * rank, rank), rank)], basis_ref)
        image = columns_of(u_ref, l, leaf)
        second = RIDGE_TERM * (image * columns_of(sc_ref, l, leaf)) + (near_ref[l] + far)
        w_ref[:, pl.ds(pl.multiple_of(l * leaf, leaf), leaf)] = second
        acc_uw[...] += lane_groups(image * second)
        acc_ww[...] += lane_groups(second * second)
        acc_rw[...] += lane_groups(columns_of(rs_ref, l, leaf) * second)

    leaf_loop(per, FAR_UNROLL, one)
    msg_ref[...] = prev_ref[...] + as_rows((acc_uw, acc_ww, acc_rw), 2, msg_ref.shape[0])


def call(kernel, name, in_specs, out_shape, scratch, args, aliases=None, flops=0, out_specs=None, limit=VMEM_LIMIT):
    return pl.pallas_call(
        kernel,
        in_specs=in_specs,
        out_specs=out_specs or [WHOLE] * len(out_shape),
        out_shape=out_shape,
        scratch_shapes=scratch,
        input_output_aliases=aliases or {},
        compiler_params=pltpu.CompilerParams(vmem_limit_bytes=limit),
        cost_estimate=pl.CostEstimate(flops=flops, bytes_accessed=0, transcendentals=0),
        name=name,
    )(*args)


def two_clusters():
    return CDEV == 8 and lax.axis_size("leaf") == 2 * CDEV


def other_clusters(plane_sum):
    count = lax.axis_size("leaf")
    if two_clusters():
        return involution(plane_sum, lambda i: i ^ (12 if i % 2 else 8))
    mask = 4
    while mask < CDEV:
        plane_sum = plane_sum + involution(plane_sum, lambda i: i ^ mask)
        mask *= 2
    sums = plane_sum
    while mask < count:
        sums = jnp.concatenate([sums, involution(sums, lambda i: i ^ mask)], axis=0)
        mask *= 2
    return sums[1:]


def pass_kernel(*refs):
    pass


def after(values, *before):
    return call(
        pass_kernel, "after", [WHOLE] * len(values) + [ANYWHERE] * len(before),
        [pltpu.VMEM(value.shape, value.dtype) for value in values], [], (*values, *before),
        aliases={at: at for at in range(len(values))},
    )


def first_messages(cp):
    return sibling(cp), across(cp)


def second_messages(position, cp, got, part, *before):
    rows = cp.shape[0] - 3 * part.shape[0]
    got = (*got, sibling(got[1]))
    quad, plane_sum = call(
        quad_kernel, "quad", [SCALAR] + [WHOLE] * 5 + [ANYWHERE] * len(before),
        [pltpu.VMEM((4, rows, cp.shape[1]), BF16), pltpu.VMEM((1,) + part.shape, F32)],
        [], (position, cp, *got, part, *before),
    )
    return quad, two_chips(quad), other_clusters(plane_sum)


def last_messages(quad, mine):
    other = sibling(mine) if two_clusters() else jnp.zeros_like(mine)
    return (quad, sibling(quad)), (mine, other)


def body(
    right_side, scaling, embeddings, near_leaves, far_leaves, leaf_basis, leaf_coupling,
    transfer, coarse_coupling,
):
    columns, local_points = right_side.shape
    per, rank, leaf = leaf_basis.shape
    features = embeddings.shape[0]
    slots = near_leaves.shape[1] - 1
    far_count = far_leaves.shape[1]
    half = per // 2
    size = rank // 2
    count = lax.axis_size("leaf")
    pos = lax.axis_index("leaf")
    position = pos.reshape(1).astype(jnp.int32)
    near_rows = near_leaves.T
    far_rows = far_leaves.T
    coarse_count = count // CDEV

    scale_row = scaling.reshape(1, local_points)
    leaf_shape = pltpu.VMEM((per, columns, leaf), BF16)
    cp_shape = pltpu.VMEM((per * size + 3 * size, 2 * columns), BF16)
    part_shape = pltpu.VMEM((size, 2 * columns), F32)
    self_shape = pltpu.HBM((8 * per, leaf, leaf), BF16)
    trans_shape = pltpu.VMEM((per, rank, rank), BF16)
    half_shape = pltpu.VMEM((half, columns, leaf), BF16)
    moved_shape = pltpu.VMEM((per * rank, columns), F32)
    tile_shape = pltpu.VMEM((per * slots + 1, leaf, leaf), BF16)
    near_shape = pltpu.VMEM((per + 1, columns, leaf), F32)
    wide_shape = pltpu.VMEM((columns, local_points), F32)
    msg_shape = pltpu.VMEM((8, columns), F32)
    coefs_shape = pltpu.VMEM((per * rank, columns), BF16)
    acc_shape = pltpu.VMEM((columns, 128), F32)
    window = [
        pltpu.VMEM((12 * per, size, 2 * columns), BF16),
        pltpu.VMEM((rank, 3 * columns), BF16),
    ]

    both_shape = pltpu.VMEM((half, columns + 2 * features, leaf), BF16)
    v, cp, part, trans, mx, mo = call(
        prep_kernel, "prep", [SCALAR] + [OUTSIDE] * 5,
        [leaf_shape, cp_shape, part_shape, trans_shape, both_shape, both_shape],
        [pltpu.VMEM(right_side.shape, F32), pltpu.VMEM(scale_row.shape, F32), pltpu.VMEM(leaf_basis.shape, BF16),
         pltpu.VMEM(transfer.shape, BF16), pltpu.VMEM(embeddings.shape, F32),
         pltpu.VMEM((per, 2 * features, leaf), BF16), coefs_shape, pltpu.VMEM((per * rank * rank // 128, 128), F32), pltpu.VMEM((per, rank, 128), F32), pltpu.SemaphoreType.DMA((per // UNROLL + 1, 3))],
        (position, right_side, scale_row, leaf_basis, transfer, embeddings), limit=WIDE_LIMIT,
    )
    got = first_messages(cp)
    coup, coarse, lists = call(
        relayout_kernel, "relayout", [SCALAR] * 2 + [WHOLE] * 2 + [ANYWHERE],
        [pltpu.VMEM((per, 2 * rank, far_count * size), BF16), pltpu.VMEM((coarse_count - 1, rank, rank), BF16),
         jax.ShapeDtypeStruct((4, per * slots + 2 * UNROLL), jnp.int32)],
        [
            pltpu.VMEM((RELAY_UNROLL, far_count * rank * rank // 128, 128), F32),
            pltpu.VMEM((RELAY_UNROLL, 2, far_count // 4, rank, 128), F32),
            pltpu.VMEM((size, 128), F32), pltpu.VMEM((rank, 128), F32),
        ],
        (position, near_rows, leaf_coupling, coarse_coupling, cp), out_specs=[WHOLE, WHOLE, SCALAR],
    )
    across_cp, mo, mx = after((got[1], mo, mx), coup)
    got = (got[0], across_cp)
    vo = beside(mo)
    vx = sibling(mx)
    tself, near = call(
        self_kernel, "self_tiles", [WHOLE] * 2 + [ANYWHERE], [self_shape, near_shape],
        [pltpu.VMEM((per, leaf, leaf), BF16), pltpu.SemaphoreType.DMA((per,))],
        (embeddings, v, mo), out_specs=[OUTSIDE, WHOLE],
    )
    quad, far_quad, mine = second_messages(position, cp, got, part, near)
    tiles, near = call(
        own_kernel, "own_tiles", [SCALAR] * 2 + [WHOLE] * 4 + [ANYWHERE], [tile_shape, near_shape],
        [pltpu.VMEM((per + half, columns, leaf), BF16)],
        (position, lists, embeddings, v, vx, near, quad), aliases={5: 1},
    )
    coefs, sums = last_messages(*after((far_quad, mine), near))
    tiles, near = call(
        foreign_kernel, "foreign_tiles", [SCALAR] * 2 + [WHOLE] * 4, [tile_shape, near_shape], [],
        (position, lists, embeddings, vo, tiles, near), aliases={4: 0, 5: 1},
    )
    image, q, cp, part, msg, mx, mo = call(
        far_first_kernel, "far_first", [SCALAR] * 2 + [WHOLE] * 12,
        [wide_shape, leaf_shape, cp_shape, part_shape, msg_shape, half_shape, half_shape],
        [*window, moved_shape, coefs_shape, acc_shape, acc_shape],
        (position, far_rows, right_side, scale_row, leaf_basis, coup, trans, near, coarse, *sums, quad, *coefs),
    )
    got = first_messages(cp)
    (near,) = call(
        own_again_kernel, "own_again", [SCALAR] * 2 + [WHOLE] * 2, [near_shape], [],
        (position, lists, q, tiles),
    )
    across_cp, mo = after((got[1], mo), near)
    got = (got[0], across_cp)
    vo = beside(mo)
    quad, far_quad, mine = second_messages(position, cp, got, part)
    vx = sibling(mx)
    (near,) = call(
        self_again_kernel, "self_again", [SCALAR] * 2 + [WHOLE] * 3 + [OUTSIDE, WHOLE, ANYWHERE], [near_shape],
        [pltpu.VMEM((per, leaf, leaf), BF16), pltpu.SemaphoreType.DMA((per // UNROLL,))],
        (position, lists, q, vx, tiles, tself, near, quad), aliases={6: 0},
    )
    coefs, sums = last_messages(*after((far_quad, mine), near, vo))
    (near,) = call(
        near_again_kernel, "near_again", [SCALAR] * 2 + [WHOLE] * 3, [near_shape], [],
        (position, lists, vo, tiles, near), aliases={4: 0},
    )
    second, msg = call(
        far_again_kernel, "far_again", [SCALAR] * 2 + [WHOLE] * 14, [wide_shape, msg_shape],
        window + [moved_shape] + [acc_shape] * 3,
        (position, far_rows, right_side, scale_row, image, leaf_basis, coup, trans,
         coarse, *sums, quad, *coefs, near, msg),
    )

    mask = 1
    while mask < count:
        msg = msg + involution(msg, lambda i: i ^ mask)
        mask *= 2
    uu, ru, uw, ww, rw = [msg[k][:, None] for k in range(5)]
    step_one = ru / (uu + EPSILON)
    beta = -(uu - step_one * uw) / (uu + EPSILON)
    lead = 1.0 + beta
    curvature = lead * lead * uu - 2.0 * lead * step_one * uw + step_one * step_one * ww
    aligned = lead * (ru - step_one * uu) - step_one * (rw - step_one * uw)
    step_two = aligned / (curvature + EPSILON)
    first_weight = step_one + step_two * lead
    second_weight = step_two * step_one
    solution = scale_row * (first_weight * right_side - second_weight * image)
    residual = right_side - first_weight * image + second_weight * second
    return (solution, residual)


def solution(mesh):
    return jax.shard_map(
        body,
        mesh=mesh,
        in_specs=(
            P(None, ("groups", "leaf")),
            P(("groups", "leaf")),
            P(None, ("groups", "leaf")),
            P(("groups", "leaf"), None),
            P(("groups", "leaf"), None),
            P(("groups", "leaf"), None, None),
            P(("groups", "leaf"), None, None),
            P(("groups", "leaf"), None),
            P("groups", None, None),
        ),
        out_specs=(P(None, ("groups", "leaf")), P(None, ("groups", "leaf"))),
        check_vma=False,
    )
```

```python
import math

import jax
import jax.numpy as jnp
from jax import lax
from jax.experimental import pallas as pl
from jax.experimental.pallas import tpu as pltpu
from jax.sharding import PartitionSpec as P

FARDEV = 4
CDEV = 8
KERNEL_SCALE = 0.0625
RIDGE_TERM = 1.0
EPSILON = 1e-06
F32 = jnp.float32
BF16 = jnp.bfloat16
HALF_SCALE = math.sqrt(2.0 * KERNEL_SCALE * math.log2(math.e))
UNROLL = 4
FAR_UNROLL = 16
RELAY_UNROLL = 4
VMEM_LIMIT = 13 * 1024 * 1024
WIDE_LIMIT = 54 * 1024 * 1024
SELF_LIMIT = 28 * 1024 * 1024
WHOLE = pl.BlockSpec(memory_space=pltpu.VMEM)
ANYWHERE = pl.BlockSpec(memory_space=pl.ANY)
OUTSIDE = pl.BlockSpec(memory_space=pltpu.HBM)
SCALAR = pl.BlockSpec(memory_space=pltpu.SMEM)


def involution(value, partner):
    count = lax.axis_size("leaf")
    pairs = [(i, partner(i)) for i in range(count) if 0 <= partner(i) < count]
    return lax.ppermute(value, "leaf", pairs)


def sibling(value):
    return involution(value, lambda i: i ^ 1)


def beside(value):
    return involution(value, lambda i: i + 1 if i % 2 else i - 1)


def across(value):
    return involution(value, lambda i: i ^ 2)


def two_chips(value):
    return involution(value, lambda i: i + 3 if i % 2 else i - 3)


def dot(a, b, ca, cb):
    return lax.dot_general(a, b, (((ca,), (cb,)), ((), ())), preferred_element_type=F32)


def split3(value):
    high = value.astype(BF16)
    rest = value - high.astype(F32)
    mid = rest.astype(BF16)
    low = (rest - mid.astype(F32)).astype(BF16)
    return high, mid, low


def point_pieces(points):
    scaled = points * HALF_SCALE
    high, mid, low = split3(scaled)
    square = 0.5 * jnp.sum(scaled * scaled, axis=0, keepdims=True)
    s_high, s_mid, s_low = split3(square)
    return high, mid, low, s_high.astype(F32), s_mid.astype(F32), s_low.astype(F32)


def norm_rows(first, second, third, width, swap, sign):
    row = lax.broadcasted_iota(jnp.int32, (16, width), 0)
    base = 3 if swap else 0
    ones = 0 if swap else 3
    out = jnp.where((row >= ones) & (row < ones + 3), sign, 0.0)
    for at, piece in enumerate((first, second, third)):
        out = jnp.where(row == base + at, sign * piece, out)
    return out.astype(BF16)


def own_rows(points):
    high, mid, low, a, b, c = point_pieces(points)
    norms = norm_rows(a, b, c, points.shape[1], False, 1.0)
    return jnp.concatenate([high, mid, high, mid, low, high, norms], axis=0)


def other_rows(points):
    high, mid, low, a, b, c = point_pieces(points)
    norms = norm_rows(a, b, c, points.shape[1], True, -1.0)
    return jnp.concatenate([high, high, mid, mid, high, low, norms], axis=0)


def tile_of(other, own):
    return jnp.exp2(dot(other, own, 0, 0)).astype(BF16)


def pack_pair(block):
    half = block.shape[0] // 2
    return jnp.concatenate([block[:half], block[half:]], axis=1)


def lane_groups(value):
    total = value[:, :128]
    for at in range(128, value.shape[1], 128):
        total += value[:, at : at + 128]
    return total


def as_rows(parts, first, count):
    lane = lax.broadcasted_iota(jnp.int32, parts[0].shape, 1)
    out = jnp.zeros(parts[0].shape, F32)
    for at, part in enumerate(parts):
        out = jnp.where(lane == first + at, jnp.sum(part[...], axis=1, keepdims=True), out)
    return out.T[:count]


def leaf_coefficients(basis, rounded):
    return dot(basis, rounded, 1, 1).astype(BF16)


def share_of(trans, coefs):
    count, rank, _ = trans.shape
    return dot(trans.reshape(count * rank, rank), coefs, 0, 0)


def columns_of(ref, at, width):
    return ref[:, pl.ds(pl.multiple_of(at * width, width), width)]


def leaf_loop(count, unroll, fn):
    def trip(i, carry):
        for u in range(unroll):
            fn(i * unroll + u)
        return carry

    lax.fori_loop(0, count // unroll, trip, 0)


def list_loop(count, fn):
    def four(i, carry):
        for u in range(UNROLL):
            fn(i * UNROLL + u)
        return carry

    def single(i, carry):
        fn(i)
        return carry

    whole_trips = count // UNROLL
    lax.fori_loop(0, whole_trips, four, 0)
    lax.fori_loop(whole_trips * UNROLL, count, single, 0)


def store_share(total, part_ref, cp_ref):
    packed = pack_pair(total)
    part_ref[...] = packed
    size = packed.shape[0]
    rows = cp_ref.shape[0] - 3 * size
    for at, piece in enumerate(split3(packed)):
        cp_ref[rows + at * size : rows + (at + 1) * size] = piece


def store_square(flat, target):
    pairs = flat.shape[0]
    target[pl.ds(0, pairs, stride=2)] = flat
    target[pl.ds(1, pairs, stride=2)] = pltpu.roll(flat, 64, 1)


def relayout_kernel(
    pos_ref, near_ref, coup_ref, coarse_ref, wait_ref, out_ref, coarse_out, lists, by_slots, by_rows, flat, square
):
    per, slots, entries = coup_ref.shape
    rank = out_ref.shape[1] // 2
    quarter = rank // 2
    pairs = entries // 128
    lane = lax.broadcasted_iota(jnp.int32, (pairs, 128), 1) // quarter

    def one(l, by_slot, by_row):
        wide = coup_ref[l].astype(F32)
        for k in range(pairs):
            by_slot[k * slots : (k + 1) * slots] = wide[:, k * 128 : (k + 1) * 128]
        rows = [by_slot[pl.ds(s, pairs, stride=slots)] for s in range(slots)]
        turned = [[rows[s] if t == 0 else pltpu.roll(rows[s], t * quarter, 1) for t in range(4)] for s in range(slots)]
        for half in range(2):
            for parity in range(2):
                chunk = 2 * parity + half
                for group in range(slots // 4):
                    out = turned[4 * group][(0 - chunk) % 4]
                    for r in range(1, 4):
                        out = jnp.where(lane == r, turned[4 * group + r][(r - chunk) % 4], out)
                    by_row[half, group, pl.ds(parity, pairs, stride=2)] = out
        for half in range(2):
            for group in range(slots // 4):
                out_ref[l, half * rank : (half + 1) * rank, group * 128 : (group + 1) * 128] = by_row[half, group].astype(BF16)

    def trip(i, carry):
        for u in range(by_slots.shape[0]):
            one(i * by_slots.shape[0] + u, by_slots.at[u], by_rows.at[u])
        return carry

    lax.fori_loop(0, per // by_slots.shape[0], trip, 0)
    build_lists(near_ref, lists, pos_ref[0], per // 2)
    cluster = pos_ref[0] // CDEV
    wide = coarse_ref[cluster].astype(F32)
    number = lax.broadcasted_iota(jnp.int32, wide.shape, 0)
    for at in range(coarse_out.shape[0]):
        row = jnp.sum(jnp.where(number == (cluster ^ (at + 1)), wide, 0.0), axis=0, keepdims=True)
        for k in range(pairs):
            flat[k : k + 1] = row[:, k * 128 : (k + 1) * 128]
        store_square(flat[...], square)
        coarse_out[at] = square[:, :rank].astype(BF16)


def prep_kernel(
    pos_ref, rs_hbm, sc_hbm, basis_hbm, transfer_hbm, e_hbm, v_ref, cp_ref, part_ref, trans_ref, mx_ref, mo_ref,
    rs_ref, sc_ref, basis_ref, transfer_ref, e_ref, points, coefs, by_leaf, squares, sems,
):
    per, rank, leaf = basis_ref.shape
    columns, features = rs_ref.shape[0], e_ref.shape[0]
    size = rank // 2
    groups = per // UNROLL
    width = UNROLL * leaf
    small = [
        pltpu.make_async_copy(transfer_hbm, transfer_ref, sems.at[0, 0]),
        pltpu.make_async_copy(sc_hbm, sc_ref, sems.at[0, 1]),
    ]
    copies = []
    for group in range(groups):
        cols, rows = pl.ds(group * width, width), pl.ds(group * UNROLL, UNROLL)
        copies.append([
            pltpu.make_async_copy(rs_hbm.at[:, cols], rs_ref.at[:, cols], sems.at[group + 1, 0]),
            pltpu.make_async_copy(basis_hbm.at[rows], basis_ref.at[rows], sems.at[group + 1, 1]),
            pltpu.make_async_copy(e_hbm.at[:, cols], e_ref.at[:, cols], sems.at[group + 1, 2]),
        ])
    for copy in small + sum(copies, []):
        copy.start()
    small[0].wait()
    wide = transfer_ref[...].astype(F32)
    for k in range(rank * rank // 128):
        by_leaf[k * per : (k + 1) * per] = wide[:, k * 128 : (k + 1) * 128]
    for at in range(per):
        store_square(by_leaf[pl.ds(at, rank * rank // 128, stride=per)], squares.at[at])
    trans_ref[...] = squares[:, :, :rank].astype(BF16)
    small[1].wait()

    def one(at):
        rounded = (rs_ref[:, at * leaf : (at + 1) * leaf] * sc_ref[:, at * leaf : (at + 1) * leaf]).astype(BF16)
        v_ref[at] = rounded
        here = e_ref[:, at * leaf : (at + 1) * leaf]
        high = here.astype(BF16)
        points[at, :features] = high
        points[at, features:] = (here - high.astype(F32)).astype(BF16)
        coef = leaf_coefficients(basis_ref[at], rounded)
        coefs[pl.ds(at * rank, rank)] = coef
        cp_ref[pl.ds(at * size, size)] = pack_pair(coef)

    for group in range(groups):
        for copy in copies[group]:
            copy.wait()
        for u in range(UNROLL):
            one(group * UNROLL + u)
    store_share(share_of(trans_ref[...], coefs[...]), part_ref, cp_ref)
    odd = pos_ref[0] % 2
    half = per // 2
    for ref, first in ((mx_ref, half * (1 - odd)), (mo_ref, half * odd)):
        ref[:, :columns] = v_ref[pl.ds(first, half)]
        ref[:, columns:] = points[pl.ds(first, half)]


def quad_kernel(pos_ref, own_ref, sib_ref, across_ref, both_ref, part_ref, *rest):
    quad_ref, sum_ref = rest[-2:]
    place = pos_ref[0] % 4
    rows = quad_ref.shape[1]
    size = part_ref.shape[0]
    quad_ref[place] = own_ref[:rows]
    total = part_ref[...]
    for flip, ref in ((1, sib_ref), (2, across_ref), (3, both_ref)):
        quad_ref[place ^ flip] = ref[:rows]
        for at in range(3):
            total += ref[rows + at * size : rows + (at + 1) * size].astype(F32)
    sum_ref[...] = total[None]


def build_lists(near_ref, lists, pos, half):
    slots = near_ref.shape[0] - 1
    per = near_ref.shape[1]
    base = pos * 2 * half - half
    odd = pos % 2 == 1

    def put(leaf, counts):
        for slot in range(slots):
            m = near_ref[1 + slot, leaf] - base
            own = (m >= half) & (m < 3 * half)
            low = (m < half) == odd
            value = (leaf << 16) | ((leaf * slots + slot) << 8) | m
            for kind, count in enumerate(counts):
                lists[kind, count] = value
            takes = (own, ~own & low, ~own & ~low, own | low)
            counts = tuple(count + jnp.where(take, 1, 0) for count, take in zip(counts, takes))
        return counts

    counts = lax.fori_loop(0, per, put, (0, 0, 0, 0))
    for kind, count in enumerate(counts):
        for u in range(UNROLL):
            lists[kind, count + u] = (per << 16) | ((per * slots) << 8) | half
        lists[kind, lists.shape[1] - 1] = count


def near_entry(lists, kind, at, half):
    value = lists[kind, at]
    leaf_at = value >> 16
    return (value >> 8) & 255, leaf_at, jnp.minimum(leaf_at, 2 * half - 1), value & 255


def self_kernel(e_ref, v_ref, wait_ref, self_ref, near_out, buffer, sems):
    per, _, leaf = v_ref.shape
    copies = []
    for at in range(per):
        points = e_ref[:, at * leaf : (at + 1) * leaf]
        tile = tile_of(other_rows(points), own_rows(points))
        buffer[at] = tile
        near_out[at] = dot(v_ref[at], tile, 1, 0)
        copies.append(pltpu.make_async_copy(buffer.at[at], self_ref.at[at], sems.at[at]))
        copies[-1].start()
    for copy in copies:
        copy.wait()


def points_of(ref, at, columns, features):
    high = ref[at, columns : columns + features].astype(F32)
    return high + ref[at, columns + features :].astype(F32)


def own_kernel(pos_ref, lists, e_ref, v_ref, vx_ref, near_in, wait_ref, tile_ref, near_out, vw):
    per, columns, leaf = v_ref.shape
    half = per // 2
    vw[:per] = v_ref[...]
    vw[per:] = vx_ref[:, :columns]
    n = lists[3, lists.shape[1] - 1]

    def one(at_entry):
        entry, leaf_at, row, m = near_entry(lists, 3, at_entry, half)
        own = (m >= half) & (m < 3 * half)
        place = jnp.clip(m - half, 0, per - 1)
        points = jnp.where(
            own, columns_of(e_ref, place, leaf), points_of(vx_ref, m % half, columns, e_ref.shape[0])
        )
        tile = tile_of(other_rows(points), own_rows(columns_of(e_ref, row, leaf)))
        tile_ref[entry] = tile
        near_out[leaf_at] += dot(vw[jnp.where(own, place, per + m % half)], tile, 1, 0)

    list_loop(n, one)


def own_again_kernel(pos_ref, lists, v_ref, tile_ref, near_out):
    half = v_ref.shape[0] // 2
    near_out[...] = jnp.zeros_like(near_out)
    n = lists[0, lists.shape[1] - 1]

    def one(at_entry):
        entry, leaf_at, _, m = near_entry(lists, 0, at_entry, half)
        place = jnp.clip(m - half, 0, 2 * half - 1)
        near_out[leaf_at] += dot(v_ref[place], tile_ref[entry], 1, 0)

    list_loop(n, one)


def self_again_kernel(
    pos_ref, lists, v_ref, vx_ref, tile_ref, self_hbm, near_in, wait_ref, near_out, self_ref, sems,
):
    per = v_ref.shape[0]
    half = per // 2
    copies = [
        pltpu.make_async_copy(self_hbm.at[pl.ds(at, UNROLL)], self_ref.at[pl.ds(at, UNROLL)], sems.at[at // UNROLL])
        for at in range(0, per, UNROLL)
    ]
    for copy in copies:
        copy.start()
    n = lists[1, lists.shape[1] - 1]

    def one(at_entry):
        entry, leaf_at, _, m = near_entry(lists, 1, at_entry, half)
        near_out[leaf_at] += dot(vx_ref[m % half], tile_ref[entry], 1, 0)

    list_loop(n, one)
    for i, copy in enumerate(copies):
        copy.wait()
        for u in range(UNROLL):
            at = i * UNROLL + u
            near_out[at] += dot(v_ref[at], self_ref[at], 1, 0)


def load_coefficients(cw, sources):
    devices, rows, _ = sources[0].shape
    per = rows // cw.shape[1]
    for slot, source in enumerate(sources):
        for device in range(devices):
            for at in range(per):
                cw[(slot * devices + device) * per + at] = source[device, at * cw.shape[1] : (at + 1) * cw.shape[1]]


def coarse_rows(coarse_ref, sum_refs, fc):
    rank = coarse_ref.shape[1]
    acc = jnp.zeros((rank, rank), F32)
    for at in range(coarse_ref.shape[0]):
        packed = sum_refs[0][at]
        for ref in sum_refs[1:]:
            packed += ref[at]
        total = jnp.concatenate([packed[:, :rank], packed[:, rank:]], axis=0)
        for piece in split3(total):
            acc += dot(coarse_ref[at], piece, 1, 0)
    fc[...] = jnp.concatenate(split3(acc), axis=1)


def far_sum(l, pos, far_ref, cw, coup_ref, moved, basis_ref):
    per, rank, _ = basis_ref.shape
    odd = pos % 2
    picks = []
    for s in range(far_ref.shape[0]):
        leaf_id = far_ref[s, l]
        device = leaf_id // per
        gap = device // 4 - pos // 4
        slot = jnp.where(gap == 0, 0, jnp.where((gap < 0) == (odd == 0), 1, 2))
        picks.append(cw[(slot * 4 + device % 4) * per + leaf_id % per])
    wide = dot(coup_ref[l], jnp.concatenate(picks, axis=0), 1, 0)
    combined = wide[:rank, :rank] + wide[rank:, rank:] + moved
    return dot(combined.astype(BF16), basis_ref[l], 0, 0)


def store_moved(trans, fc, mv):
    count, rank, _ = trans.shape
    wide = dot(trans.reshape(count * rank, rank), fc[...], 1, 0)
    mv[...] = wide[:, :rank] + wide[:, rank : 2 * rank] + wide[:, 2 * rank :]


def foreign_kernel(pos_ref, lists, e_ref, vo_ref, tile_in, near_in, tile_ref, near_out):
    half, _, leaf = vo_ref.shape
    features = e_ref.shape[0]
    columns = vo_ref.shape[1] - 2 * features
    n = lists[2, lists.shape[1] - 1]

    def one(at_entry):
        entry, leaf_at, row, m = near_entry(lists, 2, at_entry, half)
        points = points_of(vo_ref, m % half, columns, features)
        tile = tile_of(other_rows(points), own_rows(columns_of(e_ref, row, leaf)))
        tile_ref[entry] = tile
        near_out[leaf_at] += dot(vo_ref[m % half, :columns], tile, 1, 0)

    list_loop(n, one)


def far_first_kernel(
    pos_ref, far_ref, rs_ref, sc_ref, basis_ref, coup_ref, trans_ref, near_ref, coarse_ref, sum_a, sum_b, c0, c1, c2,
    u_ref, q_ref, cp_ref, part_ref, msg_ref, mx_ref, mo_ref, cw, fc, mv, coefs, acc_uu, acc_ru,
):
    per, rank, leaf = basis_ref.shape
    half = per // 2
    size = rank // 2
    pos = pos_ref[0]
    odd = pos % 2
    load_coefficients(cw, (c0, c1, c2))
    coarse_rows(coarse_ref, (sum_a, sum_b), fc)
    store_moved(trans_ref[...], fc, mv)
    acc_uu[...] = jnp.zeros_like(acc_uu)
    acc_ru[...] = jnp.zeros_like(acc_ru)

    def one(l):
        rows = pl.ds(pl.multiple_of(l * rank, rank), rank)
        far = far_sum(l, pos, far_ref, cw, coup_ref, mv[rows], basis_ref)
        right = columns_of(rs_ref, l, leaf)
        scale = columns_of(sc_ref, l, leaf)
        image = RIDGE_TERM * (right * scale) + (near_ref[l] + far)
        u_ref[:, pl.ds(pl.multiple_of(l * leaf, leaf), leaf)] = image
        acc_uu[...] += lane_groups(image * image)
        acc_ru[...] += lane_groups(right * image)
        rounded = (image * scale).astype(BF16)
        q_ref[l] = rounded
        coef = leaf_coefficients(basis_ref[l], rounded)
        coefs[rows] = coef
        cp_ref[pl.ds(pl.multiple_of(l * size, size), size)] = pack_pair(coef)

    leaf_loop(per, FAR_UNROLL, one)
    store_share(share_of(trans_ref[...], coefs[...]), part_ref, cp_ref)
    mx_ref[...] = q_ref[pl.ds(half * (1 - odd), half)]
    mo_ref[...] = q_ref[pl.ds(half * odd, half)]
    msg_ref[...] = as_rows((acc_uu, acc_ru), 0, msg_ref.shape[0])


def near_again_kernel(pos_ref, lists, vo_ref, tile_ref, near_in, near_out):
    half = vo_ref.shape[0]
    n = lists[2, lists.shape[1] - 1]

    def one(at_entry):
        entry, leaf_at, _, m = near_entry(lists, 2, at_entry, half)
        near_out[leaf_at] += dot(vo_ref[m % half], tile_ref[entry], 1, 0)

    list_loop(n, one)


def far_again_kernel(
    pos_ref, far_ref, rs_ref, sc_ref, u_ref, basis_ref, coup_ref, trans_ref,
    coarse_ref, sum_a, sum_b, c0, c1, c2, near_ref, prev_ref, w_ref, msg_ref,
    cw, fc, mv, acc_uw, acc_ww, acc_rw,
):
    per, rank, leaf = basis_ref.shape
    pos = pos_ref[0]
    load_coefficients(cw, (c0, c1, c2))
    coarse_rows(coarse_ref, (sum_a, sum_b), fc)
    store_moved(trans_ref[...], fc, mv)
    for acc in (acc_uw, acc_ww, acc_rw):
        acc[...] = jnp.zeros_like(acc)

    def one(l):
        far = far_sum(l, pos, far_ref, cw, coup_ref, mv[pl.ds(pl.multiple_of(l * rank, rank), rank)], basis_ref)
        image = columns_of(u_ref, l, leaf)
        second = RIDGE_TERM * (image * columns_of(sc_ref, l, leaf)) + (near_ref[l] + far)
        w_ref[:, pl.ds(pl.multiple_of(l * leaf, leaf), leaf)] = second
        acc_uw[...] += lane_groups(image * second)
        acc_ww[...] += lane_groups(second * second)
        acc_rw[...] += lane_groups(columns_of(rs_ref, l, leaf) * second)

    leaf_loop(per, FAR_UNROLL, one)
    msg_ref[...] = prev_ref[...] + as_rows((acc_uw, acc_ww, acc_rw), 2, msg_ref.shape[0])


def call(kernel, name, in_specs, out_shape, scratch, args, aliases=None, flops=0, out_specs=None, limit=VMEM_LIMIT):
    return pl.pallas_call(
        kernel,
        in_specs=in_specs,
        out_specs=out_specs or [WHOLE] * len(out_shape),
        out_shape=out_shape,
        scratch_shapes=scratch,
        input_output_aliases=aliases or {},
        compiler_params=pltpu.CompilerParams(vmem_limit_bytes=limit),
        cost_estimate=pl.CostEstimate(flops=flops, bytes_accessed=0, transcendentals=0),
        name=name,
    )(*args)


def two_clusters():
    return CDEV == 8 and lax.axis_size("leaf") == 2 * CDEV


def other_clusters(plane_sum):
    count = lax.axis_size("leaf")
    if two_clusters():
        return involution(plane_sum, lambda i: i ^ (12 if i % 2 else 8))
    mask = 4
    while mask < CDEV:
        plane_sum = plane_sum + involution(plane_sum, lambda i: i ^ mask)
        mask *= 2
    sums = plane_sum
    while mask < count:
        sums = jnp.concatenate([sums, involution(sums, lambda i: i ^ mask)], axis=0)
        mask *= 2
    return sums[1:]


def pass_kernel(*refs):
    pass


def after(values, *before):
    return call(
        pass_kernel, "after", [WHOLE] * len(values) + [ANYWHERE] * len(before),
        [pltpu.VMEM(value.shape, value.dtype) for value in values], [], (*values, *before),
        aliases={at: at for at in range(len(values))},
    )


def first_messages(cp):
    return sibling(cp), across(cp)


def second_messages(position, cp, got, part, *before):
    rows = cp.shape[0] - 3 * part.shape[0]
    got = (*got, sibling(got[1]))
    quad, plane_sum = call(
        quad_kernel, "quad", [SCALAR] + [WHOLE] * 5 + [ANYWHERE] * len(before),
        [pltpu.VMEM((4, rows, cp.shape[1]), BF16), pltpu.VMEM((1,) + part.shape, F32)],
        [], (position, cp, *got, part, *before),
    )
    return quad, two_chips(quad), other_clusters(plane_sum)


def last_messages(quad, mine):
    other = sibling(mine) if two_clusters() else jnp.zeros_like(mine)
    return (quad, sibling(quad)), (mine, other)


def body(
    right_side, scaling, embeddings, near_leaves, far_leaves, leaf_basis, leaf_coupling,
    transfer, coarse_coupling,
):
    columns, local_points = right_side.shape
    per, rank, leaf = leaf_basis.shape
    features = embeddings.shape[0]
    slots = near_leaves.shape[1] - 1
    far_count = far_leaves.shape[1]
    half = per // 2
    size = rank // 2
    count = lax.axis_size("leaf")
    pos = lax.axis_index("leaf")
    position = pos.reshape(1).astype(jnp.int32)
    near_rows = near_leaves.T
    far_rows = far_leaves.T
    coarse_count = count // CDEV

    scale_row = scaling.reshape(1, local_points)
    leaf_shape = pltpu.VMEM((per, columns, leaf), BF16)
    cp_shape = pltpu.VMEM((per * size + 3 * size, 2 * columns), BF16)
    part_shape = pltpu.VMEM((size, 2 * columns), F32)
    self_shape = pltpu.HBM((8 * per, leaf, leaf), BF16)
    trans_shape = pltpu.VMEM((per, rank, rank), BF16)
    half_shape = pltpu.VMEM((half, columns, leaf), BF16)
    moved_shape = pltpu.VMEM((per * rank, columns), F32)
    tile_shape = pltpu.VMEM((per * slots + 1, leaf, leaf), BF16)
    near_shape = pltpu.VMEM((per + 1, columns, leaf), F32)
    wide_shape = pltpu.VMEM((columns, local_points), F32)
    msg_shape = pltpu.VMEM((8, columns), F32)
    coefs_shape = pltpu.VMEM((per * rank, columns), BF16)
    acc_shape = pltpu.VMEM((columns, 128), F32)
    window = [
        pltpu.VMEM((12 * per, size, 2 * columns), BF16),
        pltpu.VMEM((rank, 3 * columns), BF16),
    ]

    both_shape = pltpu.VMEM((half, columns + 2 * features, leaf), BF16)
    v, cp, part, trans, mx, mo = call(
        prep_kernel, "prep", [SCALAR] + [OUTSIDE] * 5,
        [leaf_shape, cp_shape, part_shape, trans_shape, both_shape, both_shape],
        [pltpu.VMEM(right_side.shape, F32), pltpu.VMEM(scale_row.shape, F32), pltpu.VMEM(leaf_basis.shape, BF16),
         pltpu.VMEM(transfer.shape, BF16), pltpu.VMEM(embeddings.shape, F32),
         pltpu.VMEM((per, 2 * features, leaf), BF16), coefs_shape, pltpu.VMEM((per * rank * rank // 128, 128), F32), pltpu.VMEM((per, rank, 128), F32), pltpu.SemaphoreType.DMA((per // UNROLL + 1, 3))],
        (position, right_side, scale_row, leaf_basis, transfer, embeddings), limit=WIDE_LIMIT,
    )
    got = first_messages(cp)
    coup, coarse, lists = call(
        relayout_kernel, "relayout", [SCALAR] * 2 + [WHOLE] * 2 + [ANYWHERE],
        [pltpu.VMEM((per, 2 * rank, far_count * size), BF16), pltpu.VMEM((coarse_count - 1, rank, rank), BF16),
         jax.ShapeDtypeStruct((4, per * slots + 2 * UNROLL), jnp.int32)],
        [
            pltpu.VMEM((RELAY_UNROLL, far_count * rank * rank // 128, 128), F32),
            pltpu.VMEM((RELAY_UNROLL, 2, far_count // 4, rank, 128), F32),
            pltpu.VMEM((size, 128), F32), pltpu.VMEM((rank, 128), F32),
        ],
        (position, near_rows, leaf_coupling, coarse_coupling, cp), out_specs=[WHOLE, WHOLE, SCALAR],
    )
    across_cp, mo, mx = after((got[1], mo, mx), coup)
    got = (got[0], across_cp)
    vo = beside(mo)
    vx = sibling(mx)
    tself, near = call(
        self_kernel, "self_tiles", [WHOLE] * 2 + [ANYWHERE], [self_shape, near_shape],
        [pltpu.VMEM((per, leaf, leaf), BF16), pltpu.SemaphoreType.DMA((per,))],
        (embeddings, v, mo), out_specs=[OUTSIDE, WHOLE],
    )
    quad, far_quad, mine = second_messages(position, cp, got, part, near)
    tiles, near = call(
        own_kernel, "own_tiles", [SCALAR] * 2 + [WHOLE] * 4 + [ANYWHERE], [tile_shape, near_shape],
        [pltpu.VMEM((per + half, columns, leaf), BF16)],
        (position, lists, embeddings, v, vx, near, quad), aliases={5: 1},
    )
    coefs, sums = last_messages(*after((far_quad, mine), near))
    tiles, near = call(
        foreign_kernel, "foreign_tiles", [SCALAR] * 2 + [WHOLE] * 4, [tile_shape, near_shape], [],
        (position, lists, embeddings, vo, tiles, near), aliases={4: 0, 5: 1},
    )
    image, q, cp, part, msg, mx, mo = call(
        far_first_kernel, "far_first", [SCALAR] * 2 + [WHOLE] * 12,
        [wide_shape, leaf_shape, cp_shape, part_shape, msg_shape, half_shape, half_shape],
        [*window, moved_shape, coefs_shape, acc_shape, acc_shape],
        (position, far_rows, right_side, scale_row, leaf_basis, coup, trans, near, coarse, *sums, quad, *coefs),
    )
    got = first_messages(cp)
    (near,) = call(
        own_again_kernel, "own_again", [SCALAR] * 2 + [WHOLE] * 2, [near_shape], [],
        (position, lists, q, tiles),
    )
    across_cp, mo = after((got[1], mo), near)
    got = (got[0], across_cp)
    vo = beside(mo)
    quad, far_quad, mine = second_messages(position, cp, got, part)
    vx = sibling(mx)
    (near,) = call(
        self_again_kernel, "self_again", [SCALAR] * 2 + [WHOLE] * 3 + [OUTSIDE, WHOLE, ANYWHERE], [near_shape],
        [pltpu.VMEM((per, leaf, leaf), BF16), pltpu.SemaphoreType.DMA((per // UNROLL,))],
        (position, lists, q, vx, tiles, tself, near, quad), aliases={6: 0},
    )
    coefs, sums = last_messages(*after((far_quad, mine), near, vo))
    (near,) = call(
        near_again_kernel, "near_again", [SCALAR] * 2 + [WHOLE] * 3, [near_shape], [],
        (position, lists, vo, tiles, near), aliases={4: 0},
    )
    second, msg = call(
        far_again_kernel, "far_again", [SCALAR] * 2 + [WHOLE] * 14, [wide_shape, msg_shape],
        window + [moved_shape] + [acc_shape] * 3,
        (position, far_rows, right_side, scale_row, image, leaf_basis, coup, trans,
         coarse, *sums, quad, *coefs, near, msg),
    )

    mask = 1
    while mask < count:
        msg = msg + involution(msg, lambda i: i ^ mask)
        mask *= 2
    uu, ru, uw, ww, rw = [msg[k][:, None] for k in range(5)]
    step_one = ru / (uu + EPSILON)
    beta = -(uu - step_one * uw) / (uu + EPSILON)
    lead = 1.0 + beta
    curvature = lead * lead * uu - 2.0 * lead * step_one * uw + step_one * step_one * ww
    aligned = lead * (ru - step_one * uu) - step_one * (rw - step_one * uw)
    step_two = aligned / (curvature + EPSILON)
    first_weight = step_one + step_two * lead
    second_weight = step_two * step_one
    solution = scale_row * (first_weight * right_side - second_weight * image)
    residual = right_side - first_weight * image + second_weight * second
    return (solution, residual)


def solution(mesh):
    return jax.shard_map(
        body,
        mesh=mesh,
        in_specs=(
            P(None, ("groups", "leaf")),
            P(("groups", "leaf")),
            P(None, ("groups", "leaf")),
            P(("groups", "leaf"), None),
            P(("groups", "leaf"), None),
            P(("groups", "leaf"), None, None),
            P(("groups", "leaf"), None, None),
            P(("groups", "leaf"), None),
            P("groups", None, None),
        ),
        out_specs=(P(None, ("groups", "leaf")), P(None, ("groups", "leaf"))),
        check_vma=False,
    )
```

```python
import math

import jax
import jax.numpy as jnp
from jax import lax
from jax.experimental import pallas as pl
from jax.experimental.pallas import tpu as pltpu
from jax.sharding import PartitionSpec as P

FARDEV = 4
CDEV = 8
KERNEL_SCALE = 0.0625
RIDGE_TERM = 1.0
EPSILON = 1e-06
F32 = jnp.float32
BF16 = jnp.bfloat16
HALF_SCALE = math.sqrt(2.0 * KERNEL_SCALE * math.log2(math.e))
UNROLL = 4
FAR_UNROLL = 16
RELAY_UNROLL = 4
VMEM_LIMIT = 13 * 1024 * 1024
WIDE_LIMIT = 54 * 1024 * 1024
SELF_LIMIT = 28 * 1024 * 1024
WHOLE = pl.BlockSpec(memory_space=pltpu.VMEM)
ANYWHERE = pl.BlockSpec(memory_space=pl.ANY)
OUTSIDE = pl.BlockSpec(memory_space=pltpu.HBM)
SCALAR = pl.BlockSpec(memory_space=pltpu.SMEM)


def involution(value, partner):
    count = lax.axis_size("leaf")
    pairs = [(i, partner(i)) for i in range(count) if 0 <= partner(i) < count]
    return lax.ppermute(value, "leaf", pairs)


def sibling(value):
    return involution(value, lambda i: i ^ 1)


def beside(value):
    return involution(value, lambda i: i + 1 if i % 2 else i - 1)


def across(value):
    return involution(value, lambda i: i ^ 2)


def two_chips(value):
    return involution(value, lambda i: i + 3 if i % 2 else i - 3)


def dot(a, b, ca, cb):
    return lax.dot_general(a, b, (((ca,), (cb,)), ((), ())), preferred_element_type=F32)


def split3(value):
    high = value.astype(BF16)
    rest = value - high.astype(F32)
    mid = rest.astype(BF16)
    low = (rest - mid.astype(F32)).astype(BF16)
    return high, mid, low


def point_pieces(points):
    scaled = points * HALF_SCALE
    high, mid, low = split3(scaled)
    square = 0.5 * jnp.sum(scaled * scaled, axis=0, keepdims=True)
    s_high, s_mid, s_low = split3(square)
    return high, mid, low, s_high.astype(F32), s_mid.astype(F32), s_low.astype(F32)


def norm_rows(first, second, third, width, swap, sign):
    row = lax.broadcasted_iota(jnp.int32, (16, width), 0)
    base = 3 if swap else 0
    ones = 0 if swap else 3
    out = jnp.where((row >= ones) & (row < ones + 3), sign, 0.0)
    for at, piece in enumerate((first, second, third)):
        out = jnp.where(row == base + at, sign * piece, out)
    return out.astype(BF16)


def own_rows(points):
    high, mid, low, a, b, c = point_pieces(points)
    norms = norm_rows(a, b, c, points.shape[1], False, 1.0)
    return jnp.concatenate([high, mid, high, mid, low, high, norms], axis=0)


def other_rows(points):
    high, mid, low, a, b, c = point_pieces(points)
    norms = norm_rows(a, b, c, points.shape[1], True, -1.0)
    return jnp.concatenate([high, high, mid, mid, high, low, norms], axis=0)


def tile_of(other, own):
    return jnp.exp2(dot(other, own, 0, 0)).astype(BF16)


def pack_pair(block):
    half = block.shape[0] // 2
    return jnp.concatenate([block[:half], block[half:]], axis=1)


def lane_groups(value):
    total = value[:, :128]
    for at in range(128, value.shape[1], 128):
        total += value[:, at : at + 128]
    return total


def as_rows(parts, first, count):
    lane = lax.broadcasted_iota(jnp.int32, parts[0].shape, 1)
    out = jnp.zeros(parts[0].shape, F32)
    for at, part in enumerate(parts):
        out = jnp.where(lane == first + at, jnp.sum(part[...], axis=1, keepdims=True), out)
    return out.T[:count]


def leaf_coefficients(basis, rounded):
    return dot(basis, rounded, 1, 1).astype(BF16)


def share_of(trans, coefs):
    count, rank, _ = trans.shape
    return dot(trans.reshape(count * rank, rank), coefs, 0, 0)


def columns_of(ref, at, width):
    return ref[:, pl.ds(pl.multiple_of(at * width, width), width)]


def leaf_loop(count, unroll, fn):
    def trip(i, carry):
        for u in range(unroll):
            fn(i * unroll + u)
        return carry

    lax.fori_loop(0, count // unroll, trip, 0)


def list_loop(count, fn, group=UNROLL):
    def four(i, carry):
        for u in range(group):
            fn(i * group + u)
        return carry

    def single(i, carry):
        fn(i)
        return carry

    whole_trips = count // group
    lax.fori_loop(0, whole_trips, four, 0)
    lax.fori_loop(whole_trips * group, count, single, 0)


def store_share(total, part_ref, cp_ref):
    packed = pack_pair(total)
    part_ref[...] = packed
    size = packed.shape[0]
    rows = cp_ref.shape[0] - 3 * size
    for at, piece in enumerate(split3(packed)):
        cp_ref[rows + at * size : rows + (at + 1) * size] = piece


def store_square(flat, target):
    pairs = flat.shape[0]
    target[pl.ds(0, pairs, stride=2)] = flat
    target[pl.ds(1, pairs, stride=2)] = pltpu.roll(flat, 64, 1)


def relayout_kernel(
    pos_ref, near_ref, coup_ref, coarse_ref, wait_ref, out_ref, coarse_out, lists, by_slots, by_rows, flat, square
):
    per, slots, entries = coup_ref.shape
    rank = out_ref.shape[1] // 2
    quarter = rank // 2
    pairs = entries // 128
    lane = lax.broadcasted_iota(jnp.int32, (pairs, 128), 1) // quarter

    def one(l, by_slot, by_row):
        wide = coup_ref[l].astype(F32)
        for k in range(pairs):
            by_slot[k * slots : (k + 1) * slots] = wide[:, k * 128 : (k + 1) * 128]
        rows = [by_slot[pl.ds(s, pairs, stride=slots)] for s in range(slots)]
        turned = [[rows[s] if t == 0 else pltpu.roll(rows[s], t * quarter, 1) for t in range(4)] for s in range(slots)]
        for half in range(2):
            for parity in range(2):
                chunk = 2 * parity + half
                for group in range(slots // 4):
                    out = turned[4 * group][(0 - chunk) % 4]
                    for r in range(1, 4):
                        out = jnp.where(lane == r, turned[4 * group + r][(r - chunk) % 4], out)
                    by_row[half, group, pl.ds(parity, pairs, stride=2)] = out
        for half in range(2):
            for group in range(slots // 4):
                out_ref[l, half * rank : (half + 1) * rank, group * 128 : (group + 1) * 128] = by_row[half, group].astype(BF16)

    def trip(i, carry):
        for u in range(by_slots.shape[0]):
            one(i * by_slots.shape[0] + u, by_slots.at[u], by_rows.at[u])
        return carry

    lax.fori_loop(0, per // by_slots.shape[0], trip, 0)
    build_lists(near_ref, lists, pos_ref[0], per // 2)
    cluster = pos_ref[0] // CDEV
    wide = coarse_ref[cluster].astype(F32)
    number = lax.broadcasted_iota(jnp.int32, wide.shape, 0)
    for at in range(coarse_out.shape[0]):
        row = jnp.sum(jnp.where(number == (cluster ^ (at + 1)), wide, 0.0), axis=0, keepdims=True)
        for k in range(pairs):
            flat[k : k + 1] = row[:, k * 128 : (k + 1) * 128]
        store_square(flat[...], square)
        coarse_out[at] = square[:, :rank].astype(BF16)


def prep_kernel(
    pos_ref, rs_hbm, sc_hbm, basis_hbm, transfer_hbm, e_hbm, v_ref, cp_ref, part_ref, trans_ref, mx_ref, mo_ref,
    rs_ref, sc_ref, basis_ref, transfer_ref, e_ref, points, coefs, by_leaf, squares, sems,
):
    per, rank, leaf = basis_ref.shape
    columns, features = rs_ref.shape[0], e_ref.shape[0]
    size = rank // 2
    groups = per // UNROLL
    width = UNROLL * leaf
    small = [
        pltpu.make_async_copy(transfer_hbm, transfer_ref, sems.at[0, 0]),
        pltpu.make_async_copy(sc_hbm, sc_ref, sems.at[0, 1]),
    ]
    copies = []
    for group in range(groups):
        cols, rows = pl.ds(group * width, width), pl.ds(group * UNROLL, UNROLL)
        copies.append([
            pltpu.make_async_copy(rs_hbm.at[:, cols], rs_ref.at[:, cols], sems.at[group + 1, 0]),
            pltpu.make_async_copy(basis_hbm.at[rows], basis_ref.at[rows], sems.at[group + 1, 1]),
            pltpu.make_async_copy(e_hbm.at[:, cols], e_ref.at[:, cols], sems.at[group + 1, 2]),
        ])
    for copy in small + sum(copies, []):
        copy.start()
    small[0].wait()
    wide = transfer_ref[...].astype(F32)
    for k in range(rank * rank // 128):
        by_leaf[k * per : (k + 1) * per] = wide[:, k * 128 : (k + 1) * 128]
    for at in range(per):
        store_square(by_leaf[pl.ds(at, rank * rank // 128, stride=per)], squares.at[at])
    trans_ref[...] = squares[:, :, :rank].astype(BF16)
    small[1].wait()

    def one(at):
        rounded = (rs_ref[:, at * leaf : (at + 1) * leaf] * sc_ref[:, at * leaf : (at + 1) * leaf]).astype(BF16)
        v_ref[at] = rounded
        here = e_ref[:, at * leaf : (at + 1) * leaf]
        high = here.astype(BF16)
        points[at, :features] = high
        points[at, features:] = (here - high.astype(F32)).astype(BF16)
        coef = leaf_coefficients(basis_ref[at], rounded)
        coefs[pl.ds(at * rank, rank)] = coef
        cp_ref[pl.ds(at * size, size)] = pack_pair(coef)

    for group in range(groups):
        for copy in copies[group]:
            copy.wait()
        for u in range(UNROLL):
            one(group * UNROLL + u)
    store_share(share_of(trans_ref[...], coefs[...]), part_ref, cp_ref)
    odd = pos_ref[0] % 2
    half = per // 2
    for ref, first in ((mx_ref, half * (1 - odd)), (mo_ref, half * odd)):
        ref[:, :columns] = v_ref[pl.ds(first, half)]
        ref[:, columns:] = points[pl.ds(first, half)]


def quad_kernel(pos_ref, own_ref, sib_ref, across_ref, both_ref, part_ref, *rest):
    quad_ref, sum_ref = rest[-2:]
    place = pos_ref[0] % 4
    rows = quad_ref.shape[1]
    size = part_ref.shape[0]
    quad_ref[place] = own_ref[:rows]
    total = part_ref[...]
    for flip, ref in ((1, sib_ref), (2, across_ref), (3, both_ref)):
        quad_ref[place ^ flip] = ref[:rows]
        for at in range(3):
            total += ref[rows + at * size : rows + (at + 1) * size].astype(F32)
    sum_ref[...] = total[None]


def build_lists(near_ref, lists, pos, half):
    slots = near_ref.shape[0] - 1
    per = near_ref.shape[1]
    base = pos * 2 * half - half
    odd = pos % 2 == 1

    def put(leaf, counts):
        for slot in range(slots):
            m = near_ref[1 + slot, leaf] - base
            own = (m >= half) & (m < 3 * half)
            low = (m < half) == odd
            value = (leaf << 16) | ((leaf * slots + slot) << 8) | m
            for kind, count in enumerate(counts):
                lists[kind, count] = value
            takes = (own, ~own & low, ~own & ~low, own | low)
            counts = tuple(count + jnp.where(take, 1, 0) for count, take in zip(counts, takes))
        return counts

    counts = lax.fori_loop(0, per, put, (0, 0, 0, 0))
    for kind, count in enumerate(counts):
        for u in range(UNROLL):
            lists[kind, count + u] = (per << 16) | ((per * slots) << 8) | half
        lists[kind, lists.shape[1] - 1] = count


def near_entry(lists, kind, at, half):
    value = lists[kind, at]
    leaf_at = value >> 16
    return (value >> 8) & 255, leaf_at, jnp.minimum(leaf_at, 2 * half - 1), value & 255


def self_kernel(e_ref, v_ref, wait_ref, self_ref, near_out, buffer, sems):
    per, _, leaf = v_ref.shape
    copies = []
    for at in range(per):
        points = e_ref[:, at * leaf : (at + 1) * leaf]
        tile = tile_of(other_rows(points), own_rows(points))
        buffer[at] = tile
        near_out[at] = dot(v_ref[at], tile, 1, 0)
        copies.append(pltpu.make_async_copy(buffer.at[at], self_ref.at[at], sems.at[at]))
        copies[-1].start()
    for copy in copies:
        copy.wait()


def points_of(ref, at, columns, features):
    high = ref[at, columns : columns + features].astype(F32)
    return high + ref[at, columns + features :].astype(F32)


def own_kernel(pos_ref, lists, e_ref, v_ref, vx_ref, near_in, wait_ref, tile_ref, near_out, vw):
    per, columns, leaf = v_ref.shape
    half = per // 2
    vw[:per] = v_ref[...]
    vw[per:] = vx_ref[:, :columns]
    n = lists[3, lists.shape[1] - 1]

    def one(at_entry):
        entry, leaf_at, row, m = near_entry(lists, 3, at_entry, half)
        own = (m >= half) & (m < 3 * half)
        place = jnp.clip(m - half, 0, per - 1)
        points = jnp.where(
            own, columns_of(e_ref, place, leaf), points_of(vx_ref, m % half, columns, e_ref.shape[0])
        )
        tile = tile_of(other_rows(points), own_rows(columns_of(e_ref, row, leaf)))
        tile_ref[entry] = tile
        near_out[leaf_at] += dot(vw[jnp.where(own, place, per + m % half)], tile, 1, 0)

    list_loop(n, one, 8)


def own_again_kernel(pos_ref, lists, v_ref, tile_ref, near_out):
    half = v_ref.shape[0] // 2
    near_out[...] = jnp.zeros_like(near_out)
    n = lists[0, lists.shape[1] - 1]

    def one(at_entry):
        entry, leaf_at, _, m = near_entry(lists, 0, at_entry, half)
        place = jnp.clip(m - half, 0, 2 * half - 1)
        near_out[leaf_at] += dot(v_ref[place], tile_ref[entry], 1, 0)

    list_loop(n, one)


def self_again_kernel(
    pos_ref, lists, v_ref, vx_ref, tile_ref, self_hbm, near_in, wait_ref, near_out, self_ref, sems,
):
    per = v_ref.shape[0]
    half = per // 2
    copies = [
        pltpu.make_async_copy(self_hbm.at[pl.ds(at, UNROLL)], self_ref.at[pl.ds(at, UNROLL)], sems.at[at // UNROLL])
        for at in range(0, per, UNROLL)
    ]
    for copy in copies:
        copy.start()
    n = lists[1, lists.shape[1] - 1]

    def one(at_entry):
        entry, leaf_at, _, m = near_entry(lists, 1, at_entry, half)
        near_out[leaf_at] += dot(vx_ref[m % half], tile_ref[entry], 1, 0)

    list_loop(n, one)
    for i, copy in enumerate(copies):
        copy.wait()
        for u in range(UNROLL):
            at = i * UNROLL + u
            near_out[at] += dot(v_ref[at], self_ref[at], 1, 0)


def load_coefficients(cw, sources):
    devices, rows, _ = sources[0].shape
    per = rows // cw.shape[1]
    for slot, source in enumerate(sources):
        for device in range(devices):
            for at in range(per):
                cw[(slot * devices + device) * per + at] = source[device, at * cw.shape[1] : (at + 1) * cw.shape[1]]


def coarse_rows(coarse_ref, sum_refs, fc):
    rank = coarse_ref.shape[1]
    acc = jnp.zeros((rank, rank), F32)
    for at in range(coarse_ref.shape[0]):
        packed = sum_refs[0][at]
        for ref in sum_refs[1:]:
            packed += ref[at]
        total = jnp.concatenate([packed[:, :rank], packed[:, rank:]], axis=0)
        for piece in split3(total):
            acc += dot(coarse_ref[at], piece, 1, 0)
    fc[...] = jnp.concatenate(split3(acc), axis=1)


def far_sum(l, pos, far_ref, cw, coup_ref, moved, basis_ref):
    per, rank, _ = basis_ref.shape
    odd = pos % 2
    picks = []
    for s in range(far_ref.shape[0]):
        leaf_id = far_ref[s, l]
        device = leaf_id // per
        gap = device // 4 - pos // 4
        slot = jnp.where(gap == 0, 0, jnp.where((gap < 0) == (odd == 0), 1, 2))
        picks.append(cw[(slot * 4 + device % 4) * per + leaf_id % per])
    wide = dot(coup_ref[l], jnp.concatenate(picks, axis=0), 1, 0)
    combined = wide[:rank, :rank] + wide[rank:, rank:] + moved
    return dot(combined.astype(BF16), basis_ref[l], 0, 0)


def store_moved(trans, fc, mv):
    count, rank, _ = trans.shape
    wide = dot(trans.reshape(count * rank, rank), fc[...], 1, 0)
    mv[...] = wide[:, :rank] + wide[:, rank : 2 * rank] + wide[:, 2 * rank :]


def foreign_kernel(pos_ref, lists, e_ref, vo_ref, tile_in, near_in, wait_ref, tile_ref, near_out):
    half, _, leaf = vo_ref.shape
    features = e_ref.shape[0]
    columns = vo_ref.shape[1] - 2 * features
    n = lists[2, lists.shape[1] - 1]

    def one(at_entry):
        entry, leaf_at, row, m = near_entry(lists, 2, at_entry, half)
        points = points_of(vo_ref, m % half, columns, features)
        tile = tile_of(other_rows(points), own_rows(columns_of(e_ref, row, leaf)))
        tile_ref[entry] = tile
        near_out[leaf_at] += dot(vo_ref[m % half, :columns], tile, 1, 0)

    list_loop(n, one)


def setup_kernel(trans_ref, coarse_ref, sum_a, sum_b, c0, c1, c2, cw, mv, fc):
    load_coefficients(cw, (c0, c1, c2))
    coarse_rows(coarse_ref, (sum_a, sum_b), fc)
    store_moved(trans_ref[...], fc, mv)


def far_first_kernel(
    pos_ref, far_ref, rs_ref, sc_ref, basis_ref, coup_ref, trans_ref, near_ref, cw, mv,
    u_ref, q_ref, cp_ref, part_ref, msg_ref, mx_ref, mo_ref, coefs, acc_uu, acc_ru,
):
    per, rank, leaf = basis_ref.shape
    half = per // 2
    size = rank // 2
    pos = pos_ref[0]
    odd = pos % 2
    acc_uu[...] = jnp.zeros_like(acc_uu)
    acc_ru[...] = jnp.zeros_like(acc_ru)

    def one(l):
        rows = pl.ds(pl.multiple_of(l * rank, rank), rank)
        far = far_sum(l, pos, far_ref, cw, coup_ref, mv[rows], basis_ref)
        right = columns_of(rs_ref, l, leaf)
        scale = columns_of(sc_ref, l, leaf)
        image = RIDGE_TERM * (right * scale) + (near_ref[l] + far)
        u_ref[:, pl.ds(pl.multiple_of(l * leaf, leaf), leaf)] = image
        acc_uu[...] += lane_groups(image * image)
        acc_ru[...] += lane_groups(right * image)
        rounded = (image * scale).astype(BF16)
        q_ref[l] = rounded
        coef = leaf_coefficients(basis_ref[l], rounded)
        coefs[rows] = coef
        cp_ref[pl.ds(pl.multiple_of(l * size, size), size)] = pack_pair(coef)

    leaf_loop(per, FAR_UNROLL, one)
    store_share(share_of(trans_ref[...], coefs[...]), part_ref, cp_ref)
    mx_ref[...] = q_ref[pl.ds(half * (1 - odd), half)]
    mo_ref[...] = q_ref[pl.ds(half * odd, half)]
    msg_ref[...] = as_rows((acc_uu, acc_ru), 0, msg_ref.shape[0])


def near_again_kernel(pos_ref, lists, vo_ref, tile_ref, near_in, near_out):
    half = vo_ref.shape[0]
    n = lists[2, lists.shape[1] - 1]

    def one(at_entry):
        entry, leaf_at, _, m = near_entry(lists, 2, at_entry, half)
        near_out[leaf_at] += dot(vo_ref[m % half], tile_ref[entry], 1, 0)

    list_loop(n, one)


def far_again_kernel(
    pos_ref, far_ref, rs_ref, sc_ref, u_ref, basis_ref, coup_ref, trans_ref,
    coarse_ref, sum_a, sum_b, c0, c1, c2, near_ref, prev_ref, w_ref, msg_ref,
    cw, fc, mv, acc_uw, acc_ww, acc_rw,
):
    per, rank, leaf = basis_ref.shape
    pos = pos_ref[0]
    load_coefficients(cw, (c0, c1, c2))
    coarse_rows(coarse_ref, (sum_a, sum_b), fc)
    store_moved(trans_ref[...], fc, mv)
    for acc in (acc_uw, acc_ww, acc_rw):
        acc[...] = jnp.zeros_like(acc)

    def one(l):
        far = far_sum(l, pos, far_ref, cw, coup_ref, mv[pl.ds(pl.multiple_of(l * rank, rank), rank)], basis_ref)
        image = columns_of(u_ref, l, leaf)
        second = RIDGE_TERM * (image * columns_of(sc_ref, l, leaf)) + (near_ref[l] + far)
        w_ref[:, pl.ds(pl.multiple_of(l * leaf, leaf), leaf)] = second
        acc_uw[...] += lane_groups(image * second)
        acc_ww[...] += lane_groups(second * second)
        acc_rw[...] += lane_groups(columns_of(rs_ref, l, leaf) * second)

    leaf_loop(per, FAR_UNROLL, one)
    msg_ref[...] = prev_ref[...] + as_rows((acc_uw, acc_ww, acc_rw), 2, msg_ref.shape[0])


def call(kernel, name, in_specs, out_shape, scratch, args, aliases=None, flops=0, out_specs=None, limit=VMEM_LIMIT):
    return pl.pallas_call(
        kernel,
        in_specs=in_specs,
        out_specs=out_specs or [WHOLE] * len(out_shape),
        out_shape=out_shape,
        scratch_shapes=scratch,
        input_output_aliases=aliases or {},
        compiler_params=pltpu.CompilerParams(vmem_limit_bytes=limit),
        cost_estimate=pl.CostEstimate(flops=flops, bytes_accessed=0, transcendentals=0),
        name=name,
    )(*args)


def two_clusters():
    return CDEV == 8 and lax.axis_size("leaf") == 2 * CDEV


def other_clusters(plane_sum):
    count = lax.axis_size("leaf")
    if two_clusters():
        return involution(plane_sum, lambda i: i ^ (12 if i % 2 else 8))
    mask = 4
    while mask < CDEV:
        plane_sum = plane_sum + involution(plane_sum, lambda i: i ^ mask)
        mask *= 2
    sums = plane_sum
    while mask < count:
        sums = jnp.concatenate([sums, involution(sums, lambda i: i ^ mask)], axis=0)
        mask *= 2
    return sums[1:]


def pass_kernel(*refs):
    pass


def after(values, *before):
    return call(
        pass_kernel, "after", [WHOLE] * len(values) + [ANYWHERE] * len(before),
        [pltpu.VMEM(value.shape, value.dtype) for value in values], [], (*values, *before),
        aliases={at: at for at in range(len(values))},
    )


def first_messages(cp):
    return sibling(cp), across(cp)


def second_messages(position, cp, got, part, *before):
    rows = cp.shape[0] - 3 * part.shape[0]
    got = (*got, sibling(got[1]))
    quad, plane_sum = call(
        quad_kernel, "quad", [SCALAR] + [WHOLE] * 5 + [ANYWHERE] * len(before),
        [pltpu.VMEM((4, rows, cp.shape[1]), BF16), pltpu.VMEM((1,) + part.shape, F32)],
        [], (position, cp, *got, part, *before),
    )
    return quad, two_chips(quad), other_clusters(plane_sum)


def last_messages(quad, mine):
    other = sibling(mine) if two_clusters() else jnp.zeros_like(mine)
    return (quad, sibling(quad)), (mine, other)


def body(
    right_side, scaling, embeddings, near_leaves, far_leaves, leaf_basis, leaf_coupling,
    transfer, coarse_coupling,
):
    columns, local_points = right_side.shape
    per, rank, leaf = leaf_basis.shape
    features = embeddings.shape[0]
    slots = near_leaves.shape[1] - 1
    far_count = far_leaves.shape[1]
    half = per // 2
    size = rank // 2
    count = lax.axis_size("leaf")
    pos = lax.axis_index("leaf")
    position = pos.reshape(1).astype(jnp.int32)
    near_rows = near_leaves.T
    far_rows = far_leaves.T
    coarse_count = count // CDEV

    scale_row = scaling.reshape(1, local_points)
    leaf_shape = pltpu.VMEM((per, columns, leaf), BF16)
    cp_shape = pltpu.VMEM((per * size + 3 * size, 2 * columns), BF16)
    part_shape = pltpu.VMEM((size, 2 * columns), F32)
    self_shape = pltpu.HBM((8 * per, leaf, leaf), BF16)
    trans_shape = pltpu.VMEM((per, rank, rank), BF16)
    half_shape = pltpu.VMEM((half, columns, leaf), BF16)
    moved_shape = pltpu.VMEM((per * rank, columns), F32)
    tile_shape = pltpu.VMEM((per * slots + 1, leaf, leaf), BF16)
    near_shape = pltpu.VMEM((per + 1, columns, leaf), F32)
    wide_shape = pltpu.VMEM((columns, local_points), F32)
    msg_shape = pltpu.VMEM((8, columns), F32)
    coefs_shape = pltpu.VMEM((per * rank, columns), BF16)
    acc_shape = pltpu.VMEM((columns, 128), F32)
    window = [
        pltpu.VMEM((12 * per, size, 2 * columns), BF16),
        pltpu.VMEM((rank, 3 * columns), BF16),
    ]

    both_shape = pltpu.VMEM((half, columns + 2 * features, leaf), BF16)
    v, cp, part, trans, mx, mo = call(
        prep_kernel, "prep", [SCALAR] + [OUTSIDE] * 5,
        [leaf_shape, cp_shape, part_shape, trans_shape, both_shape, both_shape],
        [pltpu.VMEM(right_side.shape, F32), pltpu.VMEM(scale_row.shape, F32), pltpu.VMEM(leaf_basis.shape, BF16),
         pltpu.VMEM(transfer.shape, BF16), pltpu.VMEM(embeddings.shape, F32),
         pltpu.VMEM((per, 2 * features, leaf), BF16), coefs_shape, pltpu.VMEM((per * rank * rank // 128, 128), F32), pltpu.VMEM((per, rank, 128), F32), pltpu.SemaphoreType.DMA((per // UNROLL + 1, 3))],
        (position, right_side, scale_row, leaf_basis, transfer, embeddings), limit=WIDE_LIMIT,
    )
    got = first_messages(cp)
    coup, coarse, lists = call(
        relayout_kernel, "relayout", [SCALAR] * 2 + [WHOLE] * 2 + [ANYWHERE],
        [pltpu.VMEM((per, 2 * rank, far_count * size), BF16), pltpu.VMEM((coarse_count - 1, rank, rank), BF16),
         jax.ShapeDtypeStruct((4, per * slots + 2 * UNROLL), jnp.int32)],
        [
            pltpu.VMEM((RELAY_UNROLL, far_count * rank * rank // 128, 128), F32),
            pltpu.VMEM((RELAY_UNROLL, 2, far_count // 4, rank, 128), F32),
            pltpu.VMEM((size, 128), F32), pltpu.VMEM((rank, 128), F32),
        ],
        (position, near_rows, leaf_coupling, coarse_coupling, cp), out_specs=[WHOLE, WHOLE, SCALAR],
    )
    across_cp, mo, mx = after((got[1], mo, mx), coup)
    got = (got[0], across_cp)
    vo = beside(mo)
    vx = sibling(mx)
    tself, near = call(
        self_kernel, "self_tiles", [WHOLE] * 2 + [ANYWHERE], [self_shape, near_shape],
        [pltpu.VMEM((per, leaf, leaf), BF16), pltpu.SemaphoreType.DMA((per,))],
        (embeddings, v, mo), out_specs=[OUTSIDE, WHOLE],
    )
    quad, far_quad, mine = second_messages(position, cp, got, part, near)
    tiles, near = call(
        own_kernel, "own_tiles", [SCALAR] * 2 + [WHOLE] * 4 + [ANYWHERE], [tile_shape, near_shape],
        [pltpu.VMEM((per + half, columns, leaf), BF16)],
        (position, lists, embeddings, v, vx, near, quad), aliases={5: 1},
    )
    coefs, sums = last_messages(*after((far_quad, mine), near))
    cw, mv = call(
        setup_kernel, "far_setup", [WHOLE] * 7, [window[0], moved_shape], [window[1]],
        (trans, coarse, *sums, quad, *coefs),
    )
    tiles, near = call(
        foreign_kernel, "foreign_tiles", [SCALAR] * 2 + [WHOLE] * 4 + [ANYWHERE], [tile_shape, near_shape], [],
        (position, lists, embeddings, vo, tiles, near, mv), aliases={4: 0, 5: 1},
    )
    image, q, cp, part, msg, mx, mo = call(
        far_first_kernel, "far_first", [SCALAR] * 2 + [WHOLE] * 8,
        [wide_shape, leaf_shape, cp_shape, part_shape, msg_shape, half_shape, half_shape],
        [coefs_shape, acc_shape, acc_shape],
        (position, far_rows, right_side, scale_row, leaf_basis, coup, trans, near, cw, mv),
    )
    got = first_messages(cp)
    (near,) = call(
        own_again_kernel, "own_again", [SCALAR] * 2 + [WHOLE] * 2, [near_shape], [],
        (position, lists, q, tiles),
    )
    across_cp, mo = after((got[1], mo), near)
    got = (got[0], across_cp)
    vo = beside(mo)
    quad, far_quad, mine = second_messages(position, cp, got, part)
    vx = sibling(mx)
    (near,) = call(
        self_again_kernel, "self_again", [SCALAR] * 2 + [WHOLE] * 3 + [OUTSIDE, WHOLE, ANYWHERE], [near_shape],
        [pltpu.VMEM((per, leaf, leaf), BF16), pltpu.SemaphoreType.DMA((per // UNROLL,))],
        (position, lists, q, vx, tiles, tself, near, quad), aliases={6: 0},
    )
    coefs, sums = last_messages(*after((far_quad, mine), near, vo))
    (near,) = call(
        near_again_kernel, "near_again", [SCALAR] * 2 + [WHOLE] * 3, [near_shape], [],
        (position, lists, vo, tiles, near), aliases={4: 0},
    )
    second, msg = call(
        far_again_kernel, "far_again", [SCALAR] * 2 + [WHOLE] * 14, [wide_shape, msg_shape],
        window + [moved_shape] + [acc_shape] * 3,
        (position, far_rows, right_side, scale_row, image, leaf_basis, coup, trans,
         coarse, *sums, quad, *coefs, near, msg),
    )

    mask = 1
    while mask < count:
        msg = msg + involution(msg, lambda i: i ^ mask)
        mask *= 2
    uu, ru, uw, ww, rw = [msg[k][:, None] for k in range(5)]
    step_one = ru / (uu + EPSILON)
    beta = -(uu - step_one * uw) / (uu + EPSILON)
    lead = 1.0 + beta
    curvature = lead * lead * uu - 2.0 * lead * step_one * uw + step_one * step_one * ww
    aligned = lead * (ru - step_one * uu) - step_one * (rw - step_one * uw)
    step_two = aligned / (curvature + EPSILON)
    first_weight = step_one + step_two * lead
    second_weight = step_two * step_one
    solution = scale_row * (first_weight * right_side - second_weight * image)
    residual = right_side - first_weight * image + second_weight * second
    return (solution, residual)


def solution(mesh):
    return jax.shard_map(
        body,
        mesh=mesh,
        in_specs=(
            P(None, ("groups", "leaf")),
            P(("groups", "leaf")),
            P(None, ("groups", "leaf")),
            P(("groups", "leaf"), None),
            P(("groups", "leaf"), None),
            P(("groups", "leaf"), None, None),
            P(("groups", "leaf"), None, None),
            P(("groups", "leaf"), None),
            P("groups", None, None),
        ),
        out_specs=(P(None, ("groups", "leaf")), P(None, ("groups", "leaf"))),
        check_vma=False,
    )
```
